32 devices in a mesh: gx: 2 (over y), gy: 4 (over z), gz: 4 (over x, core).
Axes of the slice: x: 2, y: 2, z: 4, core: 2. Of those that a mesh axis runs over, the one named last changes fastest.
Arguments:
- history: float32 [56, 32, 32, 256], P(None, 'gz', 'gy', 'gx'), may hold values from -6 to 6
- start: float32 [4, 32, 32, 256], P(None, 'gz', 'gy', 'gx'), may hold values from -51 to 51
- diagonal: float32 [32, 32, 256], P('gz', 'gy', 'gx'), may hold values from 0.25 to 2
Outputs:
- new_basis: float32 [20, 32, 32, 256], P(None, 'gz', 'gy', 'gx')
- r_factor: float32 [20, 20], replicated
The draws below stay inside these ranges and needn't reach their ends.
All inputs are finite; a program needn't handle non-finite values.
Results may differ from the reference program's by a relative error of at most 0.0003.
Values sent between devices are 32-bit elements; how exact they have to be, the bound alone decides.
No kernel may reach another device: no remote copies, remote signals or barrier semaphores. Data moves between devices by JAX's collectives and lax.ppermute only.
A program may use at most 64 MiB of HBM per device.

```python
import math
import jax
import jax.numpy as jnp
from jax import lax

NRHS = 4
STEPS = 4
HIST = 56
COLS = 20
NX = 256
NY = 32
NZ = 32


def shared_fields(key):
    first_key = jax.random.fold_in(key, 11)
    second_key = jax.random.fold_in(key, 12)
    hist_vals = jnp.clip(jax.random.normal(first_key, (HIST, NZ, NY, NX), jnp.float32), -6.0, 6.0)
    noise_vals = jnp.clip(jax.random.normal(second_key, (NRHS, NZ, NY, NX), jnp.float32), -6.0, 6.0)
    rise = 2.0
    ramp = 1.0 + rise * jnp.arange(NY, dtype=jnp.float32) / NY
    start_vals = ramp[None, None, :, None] * (0.8 * hist_vals[HIST - NRHS:] + 0.6 * noise_vals)
    return (hist_vals, start_vals)


def draw_history(key, part):
    return shared_fields(key)[0]


def draw_start(key, part):
    return shared_fields(key)[1]


def steps_of(rng, dims, split, smallest, largest):
    gain, own = 1.0, jax.random.fold_in(rng, 6)
    for position, parts in split:
        draws = jnp.exp(jax.random.uniform(jax.random.fold_in(own, position), (parts,), jnp.float32, smallest / len(split), largest / len(split)))
        gain = gain * jnp.repeat(draws, dims[position] // parts).reshape([-1 if axis == position else 1 for axis in range(len(dims))])
    return gain


def setup_inputs(seed: int = 0) -> dict:
    splits = jax.random.split(jax.random.key(seed), 4)
    return {
        "history": draw_history(jax.random.fold_in(splits[3], 71), 0),
        "start": draw_start(jax.random.fold_in(splits[3], 71), 0),
        "diagonal": jnp.clip(jnp.exp(math.log(2.0) - 2.0794415 * jax.random.uniform(splits[2], (NZ, NY, NX), jnp.float32) ** steps_of(splits[2], (NZ, NY, NX), ((0, 4), (1, 4), (2, 2)), -0.2, 0.2)), 0.25, 2.0),
    }


def apply_scaled(field, diagonal):
    padded = jnp.pad(field, ((0, 0), (1, 1), (1, 1), (1, 1)))
    beside = padded[:, 2:, 1:-1, 1:-1] + padded[:, :-2, 1:-1, 1:-1]
    beside = beside + padded[:, 1:-1, 2:, 1:-1] + padded[:, 1:-1, :-2, 1:-1]
    beside = beside + padded[:, 1:-1, 1:-1, 2:] + padded[:, 1:-1, 1:-1, :-2]
    return ((6.0 + diagonal[None]) * field - beside - 7.0 * field) / 7.0

def reference(history, start, diagonal):
    blocks = [start, apply_scaled(start, diagonal)]
    for level in range(1, STEPS):
        blocks.append(2.0 * apply_scaled(blocks[level], diagonal) - blocks[level - 1])
    basis = jnp.concatenate(blocks, axis=0)
    cell_total = float(NX * NY * NZ)
    flat_basis = basis.reshape(COLS, -1)
    flat_hist = history.reshape(HIST, -1)
    coef = jnp.dot(flat_hist.astype(jnp.float32), flat_basis.T.astype(jnp.float32), precision=lax.Precision.HIGHEST, preferred_element_type=jnp.float32) / cell_total
    projected = flat_basis - jnp.dot(coef.T.astype(jnp.float32), flat_hist.astype(jnp.float32), precision=lax.Precision.HIGHEST, preferred_element_type=jnp.float32)
    gram = jnp.dot(projected.astype(jnp.float32), projected.T.astype(jnp.float32), precision=lax.Precision.HIGHEST, preferred_element_type=jnp.float32) / cell_total
    lower = jnp.linalg.cholesky(gram)
    solved = lax.linalg.triangular_solve(lower, projected, left_side=True, lower=True)
    return (solved.reshape(basis.shape), lower.T)
```

```python
import functools

import jax
import jax.numpy as jnp
from jax import lax
from jax.experimental import pallas as pl
from jax.experimental.pallas import tpu as pltpu
from jax.sharding import PartitionSpec as P

STEPS = 4
F32 = jnp.float32
BF16 = jnp.bfloat16
AXES = ("gx", "gy", "gz")
HIGHEST = lax.Precision.HIGHEST
Z, Y, X = 8, 8, 128
CELLS = Z * Y
SLOTS = 16
BPAD = 32
HPAD = 64


def roll(tile, shift, axis):
    shift %= tile.shape[axis]
    return pltpu.roll(tile, shift, axis) if shift else tile


def iotas():
    return (
        lax.broadcasted_iota(jnp.int32, (Y, X), 0),
        lax.broadcasted_iota(jnp.int32, (Y, X), 1),
    )


def is_even(axis):
    return lax.rem(lax.axis_index(axis), 2) == 0


def facing(axis, count, received):
    index = lax.axis_index(axis)
    even = lax.rem(index, 2) == 0
    low_there, high_there = index > 0, index < count - 1

    def pick(k):
        first = received[0][k]
        if len(received) == 1:
            return jnp.where(even, 0.0, first), jnp.where(even, first, 0.0)
        second = received[1][k]
        low = jnp.where(low_there, jnp.where(even, second, first), 0.0)
        high = jnp.where(high_there, jnp.where(even, first, second), 0.0)
        return low, high

    return pick


def swaps(arrays, axis, count):
    first = [(i, i ^ 1) for i in range(count)]
    second = [(i, (i + 1 if i % 2 else i - 1) % count) for i in range(count)]
    return [lax.ppermute(a, axis, pairs) for a, pairs in zip(arrays, (first, second))]


def pack_x(fields, start, diagonal, *sends):
    _, lane = iotas()
    even = is_even("gx")
    for f in range(fields + 1):
        to_high = jnp.zeros((Y, X), F32)
        to_low = to_high
        for z in range(Z):
            tile = start[f, z] if f < fields else diagonal[z]
            base = 8 * z
            to_high = jnp.where(
                (lane >= base + 1) & (lane < base + 5), roll(tile, base + 5, 1), to_high
            )
            to_low = jnp.where(
                (lane >= base + 3) & (lane < base + 7), roll(tile, base + 3, 1), to_low
            )
        sends[0][f] = jnp.where(even, to_high, to_low)
        if len(sends) > 1:
            sends[1][f] = jnp.where(even, to_low, to_high)


def pack_y(fields, count, ways, start, diagonal, *refs):
    received, (sides, *sends) = refs[:ways], refs[ways:]
    row, lane = iotas()
    column = lane & 7
    pick = facing("gx", count, received)
    even = is_even("gy")
    half = lane < X // 2

    def send(k, one, two):
        one_turned, two_turned = roll(one, 4, 0), roll(two, 4, 0)
        to_high = jnp.where(row < 4, one_turned, two)
        to_low = jnp.where(row < 4, one, two_turned)
        sends[0][k] = jnp.where(even, to_high, to_low)
        if len(sends) > 1:
            sends[1][k] = jnp.where(even, to_low, to_high)

    for f in range(fields + 1):
        tiles = [start[f, z] if f < fields else diagonal[z] for z in range(Z)]
        low, high = pick(f)
        side = jnp.where(half & (column >= 1) & (column <= 4), low, 0.0)
        side = jnp.where(
            jnp.logical_not(half) & (column >= 3) & (column <= 6), roll(high, 64, 1), side
        )
        for z in range(Z):
            base = 8 * z
            side = jnp.where(
                (lane >= base + 5) & (lane < base + 8), roll(tiles[z], base + 5, 1), side
            )
            side = jnp.where(
                (lane >= base + 64) & (lane < base + 67), roll(tiles[z], base + 67, 1), side
            )
        sides[f] = side
        for p in range(4):
            send(4 * f + p, tiles[p], tiles[p + 4])
    for f in range(0, fields + 1, 2):
        send(4 * (fields + 1) + f // 2, sides[f], sides[min(f + 1, fields)])


def pack_z(fields, count, ways, start, diagonal, sides, *refs):
    received, (beyond, beyond_sides, *sends) = refs[:ways], refs[ways:]
    row, lane = iotas()
    pick = facing("gy", count, received)
    even = is_even("gz")
    upper = row < 4

    def unpack(k):
        low, high = pick(k)
        return (
            jnp.where(upper, high, roll(low, 4, 0)),
            jnp.where(upper, roll(high, 4, 0), low),
        )

    for f in range(fields + 1):
        for p in range(4):
            beyond[f, p], beyond[f, p + 4] = unpack(4 * f + p)
    for f in range(0, fields + 1, 2):
        one, two = unpack(4 * (fields + 1) + f // 2)
        beyond_sides[f] = one
        if f < fields:
            beyond_sides[f + 1] = two

    inner = (row == 2) | (row == 3)
    quarter = (lane & 32) == 0
    for which, ref in enumerate(sends):
        up = even if which == 0 else jnp.logical_not(even)
        at = [None] + [jnp.where(up, Z - d, d - 1) for d in range(1, 5)]
        k = 0
        for f in range(fields):
            for d in range(1, 5):
                ref[k] = start[f, at[d]]
                k += 1
            ref[k] = beyond[f, at[1]]
            ref[k + 1] = jnp.where(inner, roll(beyond[f, at[3]], 3, 0), beyond[f, at[2]])
            k += 2
        for d in range(1, 4):
            ref[k] = diagonal[at[d]]
            k += 1
        ref[k] = jnp.where(inner, roll(beyond[fields, at[2]], 3, 0), beyond[fields, at[1]])
        k += 1
        for source in (sides, beyond_sides):
            for f in range(0, fields + 1, 2):
                one, two = source[f], source[min(f + 1, fields)]
                to_high = jnp.where(quarter, roll(one, -32, 1), two)
                to_low = jnp.where(quarter, one, roll(two, 32, 1))
                ref[k] = jnp.where(up, to_high, to_low)
                k += 1


def z_tiles(fields):
    return 6 * fields + 4 + 2 * ((fields + 2) // 2)


def powers(fields, count, ways, start, diagonal, sides, beyond, beyond_sides, *refs):
    received = refs[:ways]
    history_split, history_gram, split, sums = refs[ways : ways + 4]
    halo, center, ends, coef_a, coef_b = refs[ways + 4 :]
    columns = fields * (STEPS + 1)
    row, lane = iotas()
    pick = facing("gz", count, received)

    own = set(range(Z))
    k = 0
    for f in range(fields):
        for z in range(Z):
            center[pl.ds(f * CELLS + z * Y, Y), :] = start[f, z]
            halo[0, f, z, 1] = beyond[f, z]
        for d in range(1, 5):
            halo[0, f, SLOTS - d, 0], halo[0, f, Z - 1 + d, 0] = pick(k)
            k += 1
        halo[0, f, SLOTS - 1, 1], halo[0, f, Z, 1] = pick(k)
        low, high = pick(k + 1)
        halo[0, f, SLOTS - 2, 1], halo[0, f, Z + 1, 1] = low, high
        halo[0, f, SLOTS - 3, 1], halo[0, f, Z + 2, 1] = roll(low, -3, 0), roll(high, -3, 0)
        k += 2

    def coefficients(d):
        inside = d > 0.0
        return jnp.where(inside, (d - 1.0) * (1.0 / 7.0), 0.0), jnp.where(inside, 1.0 / 7.0, 0.0)

    for z in range(Z):
        coef_a[z, 0] = (diagonal[z] - 1.0) * (1.0 / 7.0)
        coef_a[z, 1], coef_b[z, 1] = coefficients(beyond[fields, z])
    for d in range(1, 4):
        low, high = pick(k)
        coef_a[SLOTS - d, 0], coef_b[SLOTS - d, 0] = coefficients(low)
        coef_a[Z - 1 + d, 0], coef_b[Z - 1 + d, 0] = coefficients(high)
        k += 1
    low, high = pick(k)
    k += 1
    coef_a[SLOTS - 1, 1], coef_b[SLOTS - 1, 1] = coefficients(low)
    coef_a[Z, 1], coef_b[Z, 1] = coefficients(high)
    coef_a[SLOTS - 2, 1], coef_b[SLOTS - 2, 1] = coefficients(roll(low, -3, 0))
    coef_a[Z + 1, 1], coef_b[Z + 1, 1] = coefficients(roll(high, -3, 0))

    end_coefs = {}
    for part, source in enumerate((sides, beyond_sides)):
        for f in range(0, fields + 1, 2):
            low, high = pick(k)
            k += 1
            for g in (f, f + 1):
                if g > fields:
                    continue
                shift = 32 * (g - f)
                mine = source[g]
                left = jnp.where(
                    lane < 64,
                    mine,
                    jnp.where(lane < 96, roll(high, 64 - shift, 1), roll(low, 96 - shift, 1)),
                )
                right = jnp.where(
                    lane < 64,
                    roll(mine, 64, 1),
                    jnp.where(lane < 96, roll(high, -shift, 1), roll(low, 32 - shift, 1)),
                )
                if g < fields:
                    ends[0, 0, g, part], ends[0, 1, g, part] = left, right
                else:
                    end_coefs[0, part], end_coefs[1, part] = coefficients(left), coefficients(right)

    def read(level, f, z, part):
        if part == 0 and z in own:
            return center[pl.ds((fields * level + f) * CELLS + z * Y, Y), :]
        return halo[level, f, z, part]

    def beside_y(mine, other):
        above, above_other = roll(mine, -1, 0), roll(other, -1, 0)
        below, below_other = roll(mine, 1, 0), roll(other, 1, 0)
        last, first = row == Y - 1, row == 0
        return (
            jnp.where(last, above_other, above) + jnp.where(first, below_other, below),
            jnp.where(last, above, above_other) + jnp.where(first, below, below_other),
        )

    for level in range(1, STEPS + 1):
        reach = STEPS - level
        for f in range(fields):
            joined = [
                jnp.where((lane & 7) <= 3, ends[level - 1, 1, f, p], ends[level - 1, 0, f, p])
                for p in range(2)
            ]
            for at in range(-reach, Z + reach):
                z, before, after = at % SLOTS, (at - 1) % SLOTS, (at + 1) % SLOTS
                distance = max(-at, at - Z + 1, 0)
                tiles = [read(level - 1, f, z, p) for p in range(2)]
                along_y = beside_y(*tiles)
                for part in range(2 if distance < reach else 1):
                    tile = tiles[part]
                    end = roll(joined[part], 124 - 8 * z, 1)
                    total = jnp.where(lane == 0, end, roll(tile, 1, 1))
                    total = total + jnp.where(lane == X - 1, end, roll(tile, -1, 1))
                    total = total + along_y[part]
                    total = total + read(level - 1, f, before, part)
                    total = total + read(level - 1, f, after, part)
                    if part == 0 and z in own:
                        value = coef_a[z, 0] * tile - (1.0 / 7.0) * total
                    else:
                        value = coef_a[z, part] * tile - coef_b[z, part] * total
                    if level > 1:
                        value = value + value - read(level - 2, f, z, part)
                    if part == 0 and z in own:
                        center[pl.ds((fields * level + f) * CELLS + z * Y, Y), :] = value
                    else:
                        halo[level, f, z, part] = value
            if level < STEPS:
                for side in range(2):
                    tiles = [ends[level - 1, side, f, p] for p in range(2)]
                    along_y = beside_y(*tiles)
                    for part in range(2):
                        tile = tiles[part]
                        total = roll(tile, 1, 1) + roll(tile, -1, 1) + along_y[part]
                        total = total + roll(tile, 8, 1) + roll(tile, -8, 1)
                        a, b = end_coefs[side, part]
                        value = a * tile - b * total
                        if level > 1:
                            value = value + value - ends[level - 2, side, f, part]
                        ends[level, side, f, part] = value

    center[pl.ds(columns * CELLS, (24 - columns) * CELLS), :] = jnp.zeros(
        ((24 - columns) * CELLS, X), F32
    )
    for cell in range(CELLS):
        high, low = split_rows(center[pl.ds(cell, 24, stride=CELLS), :], BPAD)
        split[0:BPAD, cell * X : (cell + 1) * X] = high
        split[BPAD : 2 * BPAD, cell * X : (cell + 1) * X] = low
    basis = product(split[...], split[...])
    cross = product(history_split[...], split[...])
    basis = join(join(basis, BPAD).T, BPAD)
    cross = join(join(cross, HPAD).T, BPAD).T
    sums[:, 0:HPAD] = history_gram[...]
    sums[:, HPAD : HPAD + BPAD] = cross
    sums[0:BPAD, HPAD + BPAD :] = basis
    sums[BPAD:, HPAD + BPAD :] = jnp.zeros((HPAD - BPAD, BPAD), F32)


def split_rows(rows, padded):
    rows = jnp.concatenate([rows, jnp.zeros((padded - rows.shape[0], rows.shape[1]), F32)], axis=0)
    high = rows.astype(BF16)
    return high, (rows - high.astype(F32)).astype(BF16)


def product(left, right):
    return lax.dot_general(left, right, (((1,), (1,)), ((), ())), preferred_element_type=F32)


def join(both, padded):
    return both[:padded] + both[padded:]


def history_kernel(count, history, split, gram):
    for cell in range(CELLS):
        high, low = split_rows(history[pl.ds(cell, count, stride=CELLS), :], HPAD)
        split[0:HPAD, cell * X : (cell + 1) * X] = high
        split[HPAD : 2 * HPAD, cell * X : (cell + 1) * X] = low
    gram[...] = join(join(product(split[...], split[...]), HPAD).T, HPAD)


def split_matrix(matrix):
    high = matrix.astype(BF16)
    return high, (matrix - high.astype(F32)).astype(BF16)


def finish(columns, cells, history_split, split, *refs):
    parts, (out, factor) = refs[:-2], refs[-2:]
    total = (parts[0][...] + parts[1][...]) + (parts[2][...] + parts[3][...])
    total = total * (1.0 / cells)
    history_gram = total[:, 0:HPAD]
    coef = total[:, HPAD : HPAD + BPAD]
    basis_gram = total[0:BPAD, HPAD + BPAD :]
    inner = jnp.dot(history_gram, coef, precision=HIGHEST, preferred_element_type=F32)
    gram = basis_gram + lax.dot_general(
        coef, inner - 2.0 * coef, (((0,), (0,)), ((), ())), precision=HIGHEST, preferred_element_type=F32
    )
    row = lax.broadcasted_iota(jnp.int32, (BPAD, X), 0)
    lane = lax.broadcasted_iota(jnp.int32, (BPAD, X), 1)
    work = jnp.concatenate(
        [gram, jnp.zeros((BPAD, X - BPAD), F32)], axis=1
    )
    work = jnp.where(lane == row + BPAD, 1.0, work)
    for k in range(columns):
        pivot_row = work[k : k + 1, :]
        scale = work[:, k : k + 1] / pivot_row[:, k : k + 1]
        work = work - jnp.where(row > k, scale, 0.0) * pivot_row
    pivots = jnp.sum(jnp.where(lane == row, work, 0.0), axis=1, keepdims=True)
    good = lax.broadcasted_iota(jnp.int32, (BPAD, 1), 0) < columns
    work = work * jnp.where(good, 1.0 / jnp.sqrt(jnp.where(good, pivots, 1.0)), 0.0)
    factor[...] = jnp.where(lane >= row, work, 0.0)[0:columns, 0:columns]
    inverse = work[:, BPAD : 2 * BPAD]
    onto_history = -lax.dot_general(
        inverse, coef, (((1,), (1,)), ((), ())), precision=HIGHEST, preferred_element_type=F32
    )
    history_high, history_low = split_matrix(onto_history)
    basis_high, basis_low = split_matrix(inverse)
    left = jnp.concatenate(
        [
            jnp.concatenate([history_high, history_high, basis_high, basis_high], axis=1),
            jnp.concatenate(
                [history_low, jnp.zeros_like(history_low), basis_low, jnp.zeros_like(basis_low)], axis=1
            ),
        ],
        axis=0,
    )
    width = 4 * X
    for c in range(CELLS * X // width):
        at = slice(c * width, (c + 1) * width)
        right = jnp.concatenate([history_split[:, at], split[:, at]], axis=0)
        result = join(jnp.dot(left, right, preferred_element_type=F32), BPAD)
        for j in range(width // X):
            out[pl.ds(c * (width // X) + j, columns, stride=CELLS), :] = result[
                0:columns, j * X : (j + 1) * X
            ]


def call(kernel, outs, flops, bytes_accessed, scratch=()):
    return pl.pallas_call(
        kernel,
        out_shape=[jax.ShapeDtypeStruct(shape, dtype) for shape, dtype in outs],
        scratch_shapes=list(scratch),
        compiler_params=pltpu.CompilerParams(vmem_limit_bytes=40 * 1024 * 1024),
        cost_estimate=pl.CostEstimate(flops=flops, bytes_accessed=bytes_accessed, transcendentals=0),
    )


def exchange_sums(array, sizes, bits):
    count = sizes[0] * sizes[1] * sizes[2]
    arrays = [array]
    for mask in range(1, 1 << len(bits)):
        flip = sum(bit for i, bit in enumerate(bits) if mask >> i & 1)
        arrays.append(lax.ppermute(array, AXES, [(i, i ^ flip) for i in range(count)]))
    return arrays


def on_device(sizes, history, start, diagonal):
    fields, history_count = start.shape[0], history.shape[0]
    columns = fields * (STEPS + 1)
    all_fields = fields + 1
    count = dict(zip(AXES, sizes))
    ways = {axis: 1 if size == 2 else 2 for axis, size in count.items()}
    cells = Z * Y * X * sizes[0] * sizes[1] * sizes[2]
    tile = Y * X * 4

    with jax.named_scope("history_products"):
        history_split, history_gram = call(
            functools.partial(history_kernel, history_count),
            [((2 * HPAD, CELLS * X), BF16), ((HPAD, HPAD), F32)],
            2 * 128 * 128 * CELLS * X,
            history.size * 4 * 2,
        )(history.reshape(history_count * CELLS, X))

    with jax.named_scope("halo_x"):
        sends = call(
            functools.partial(pack_x, fields),
            [((all_fields, Y, X), F32)] * ways["gx"],
            1000,
            start.size * 4,
        )(start, diagonal)
        received = swaps(sends, "gx", count["gx"])
    with jax.named_scope("halo_y"):
        y_tiles = 4 * all_fields + (all_fields + 1) // 2
        sides, *sends = call(
            functools.partial(pack_y, fields, count["gx"], ways["gx"]),
            [((all_fields, Y, X), F32)] + [((y_tiles, Y, X), F32)] * ways["gy"],
            1000,
            start.size * 4,
        )(start, diagonal, *received)
        received = swaps(sends, "gy", count["gy"])
    with jax.named_scope("halo_z"):
        beyond, beyond_sides, *sends = call(
            functools.partial(pack_z, fields, count["gy"], ways["gy"]),
            [((all_fields, Z, Y, X), F32), ((all_fields, Y, X), F32)]
            + [((z_tiles(fields), Y, X), F32)] * ways["gz"],
            1000,
            start.size * 4,
        )(start, diagonal, sides, *received)
        received = swaps(sends, "gz", count["gz"])
    with jax.named_scope("matrix_powers"):
        split, sums = call(
            functools.partial(powers, fields, count["gz"], ways["gz"]),
            [((2 * BPAD, CELLS * X), BF16), ((HPAD, X), F32)],
            2 * 192 * 64 * CELLS * X,
            start.size * 4,
            [
                pltpu.VMEM((STEPS, fields, SLOTS, 2, Y, X), F32),
                pltpu.VMEM((24 * CELLS, X), F32),
                pltpu.VMEM((STEPS, 2, fields, 2, Y, X), F32),
                pltpu.VMEM((SLOTS, 2, Y, X), F32),
                pltpu.VMEM((SLOTS, 2, Y, X), F32),
            ],
        )(start, diagonal, sides, beyond, beyond_sides, *received, history_split, history_gram)
    with jax.named_scope("sum_over_devices"):
        devices = sizes[0] * sizes[1] * sizes[2]
        bits = []
        for axis, stride in (("gz", 1), ("gx", sizes[1] * sizes[2]), ("gy", sizes[2])):
            bits += [stride << b for b in range(count[axis].bit_length() - 1)]
        first, rest = bits[: 1 + (len(bits) - 1) % 2], bits[1 + (len(bits) - 1) % 2 :]
        for bit in first:
            pair = exchange_sums(sums, sizes, [bit])
            sums = pair[0] + pair[1]
        while rest:
            parts = exchange_sums(sums, sizes, rest[:2])
            rest = rest[2:]
            if rest:
                sums = (parts[0] + parts[1]) + (parts[2] + parts[3])
    with jax.named_scope("orthonormalize"):
        out, factor = call(
            functools.partial(finish, columns, cells),
            [((columns * CELLS, X), F32), ((columns, columns), F32)],
            2 * 192 * 64 * CELLS * X,
            columns * CELLS * X * 4,
        )(history_split, split, *parts)
    return out.reshape(columns, Z, Y, X), factor


def solution(mesh):
    sizes = tuple(mesh.shape[axis] for axis in AXES)
    return jax.shard_map(
        functools.partial(on_device, sizes),
        mesh=mesh,
        in_specs=(P(None, "gz", "gy", "gx"), P(None, "gz", "gy", "gx"), P("gz", "gy", "gx")),
        out_specs=(P(None, "gz", "gy", "gx"), P()),
        check_vma=False,
    )
```

```python
import functools

import jax
import jax.numpy as jnp
from jax import lax
from jax.experimental import pallas as pl
from jax.experimental.pallas import tpu as pltpu
from jax.sharding import PartitionSpec as P

STEPS = 4
F32 = jnp.float32
BF16 = jnp.bfloat16
AXES = ("gx", "gy", "gz")
HIGHEST = lax.Precision.HIGHEST
Z, Y, X = 8, 8, 128
CELLS = Z * Y
HALF = CELLS // 2
SLOTS = 16
BPAD = 32
BROWS = 24
HPAD = 64
ROWS = 56


def roll(tile, shift, axis):
    shift %= tile.shape[axis]
    return pltpu.roll(tile, shift, axis) if shift else tile


def iotas():
    return (
        lax.broadcasted_iota(jnp.int32, (Y, X), 0),
        lax.broadcasted_iota(jnp.int32, (Y, X), 1),
    )


def is_even(axis):
    return lax.rem(lax.axis_index(axis), 2) == 0


def facing(axis, count, received):
    index = lax.axis_index(axis)
    even = lax.rem(index, 2) == 0
    low_there, high_there = index > 0, index < count - 1

    def pick(k):
        first = received[0][k]
        if len(received) == 1:
            return jnp.where(even, 0.0, first), jnp.where(even, first, 0.0)
        second = received[1][k]
        low = jnp.where(low_there, jnp.where(even, second, first), 0.0)
        high = jnp.where(high_there, jnp.where(even, first, second), 0.0)
        return low, high

    return pick


def swaps(arrays, axis, count, around=True):
    first = [(i, i ^ 1) for i in range(count)]
    second = [(i, (i + 1 if i % 2 else i - 1) % count) for i in range(count)]
    if not around:
        second = second[1:-1]
    return [lax.ppermute(a, axis, pairs) for a, pairs in zip(arrays, (first, second))]


def pack_x(fields, start_there, diagonal_there, start, diagonal, *refs):
    sends, done = refs[:-1], refs[-1]
    copies = [
        pltpu.make_async_copy(start_there, start, done.at[0]),
        pltpu.make_async_copy(diagonal_there, diagonal, done.at[1]),
    ]
    for copy in copies:
        copy.start()
    for copy in copies:
        copy.wait()
    _, lane = iotas()
    even = is_even("gx")
    for f in range(fields + 1):
        to_high = jnp.zeros((Y, X), F32)
        to_low = to_high
        for z in range(Z):
            tile = start[f, z] if f < fields else diagonal[z]
            base = 8 * z
            to_high = jnp.where(
                (lane >= base + 1) & (lane < base + 5), roll(tile, base + 5, 1), to_high
            )
            to_low = jnp.where(
                (lane >= base + 3) & (lane < base + 7), roll(tile, base + 3, 1), to_low
            )
        sends[0][f] = jnp.where(even, to_high, to_low)
        if len(sends) > 1:
            sends[1][f] = jnp.where(even, to_low, to_high)


def pack_y(fields, count, ways, start, diagonal, _, *refs):
    received, (sides, *sends) = refs[:ways], refs[ways:]
    row, lane = iotas()
    column = lane & 7
    pick = facing("gx", count, received)
    even = is_even("gy")
    half = lane < X // 2

    def send(k, one, two):
        one_turned, two_turned = roll(one, 4, 0), roll(two, 4, 0)
        to_high = jnp.where(row < 4, one_turned, two)
        to_low = jnp.where(row < 4, one, two_turned)
        sends[0][k] = jnp.where(even, to_high, to_low)
        if len(sends) > 1:
            sends[1][k] = jnp.where(even, to_low, to_high)

    for f in range(fields + 1):
        tiles = [start[f, z] if f < fields else diagonal[z] for z in range(Z)]
        low, high = pick(f)
        side = jnp.where(half & (column >= 1) & (column <= 4), low, 0.0)
        side = jnp.where(
            jnp.logical_not(half) & (column >= 3) & (column <= 6), roll(high, 64, 1), side
        )
        for z in range(Z):
            base = 8 * z
            side = jnp.where(
                (lane >= base + 5) & (lane < base + 8), roll(tiles[z], base + 5, 1), side
            )
            side = jnp.where(
                (lane >= base + 64) & (lane < base + 67), roll(tiles[z], base + 67, 1), side
            )
        sides[f] = side
        for p in range(4):
            send(4 * f + p, tiles[p], tiles[p + 4])
    for f in range(0, fields + 1, 2):
        send(4 * (fields + 1) + f // 2, sides[f], sides[min(f + 1, fields)])


def pack_z(fields, count, ways, start, diagonal, _, sides, *refs):
    received, (beyond, beyond_sides, *sends) = refs[:ways], refs[ways:]
    row, lane = iotas()
    pick = facing("gy", count, received)
    even = is_even("gz")
    upper = row < 4

    def unpack(k):
        low, high = pick(k)
        return (
            jnp.where(upper, high, roll(low, 4, 0)),
            jnp.where(upper, roll(high, 4, 0), low),
        )

    for f in range(fields + 1):
        for p in range(4):
            beyond[f, p], beyond[f, p + 4] = unpack(4 * f + p)
    for f in range(0, fields + 1, 2):
        one, two = unpack(4 * (fields + 1) + f // 2)
        beyond_sides[f] = one
        if f < fields:
            beyond_sides[f + 1] = two

    inner = (row == 2) | (row == 3)
    quarter = (lane & 32) == 0
    for which, ref in enumerate(sends):
        up = even if which == 0 else jnp.logical_not(even)
        at = [None] + [jnp.where(up, Z - d, d - 1) for d in range(1, 5)]
        k = 0
        for f in range(fields):
            for d in range(1, 5):
                ref[k] = start[f, at[d]]
                k += 1
            ref[k] = beyond[f, at[1]]
            ref[k + 1] = jnp.where(inner, roll(beyond[f, at[3]], 3, 0), beyond[f, at[2]])
            k += 2
        for d in range(1, 4):
            ref[k] = diagonal[at[d]]
            k += 1
        ref[k] = jnp.where(inner, roll(beyond[fields, at[2]], 3, 0), beyond[fields, at[1]])
        k += 1
        for source in (sides, beyond_sides):
            for f in range(0, fields + 1, 2):
                one, two = source[f], source[min(f + 1, fields)]
                to_high = jnp.where(quarter, roll(one, -32, 1), two)
                to_low = jnp.where(quarter, one, roll(two, 32, 1))
                ref[k] = jnp.where(up, to_high, to_low)
                k += 1


def z_tiles(fields):
    return 6 * fields + 4 + 2 * ((fields + 2) // 2)


def powers(fields, count, ways, start, diagonal, sides, beyond, beyond_sides, *refs):
    received = refs[:ways]
    history_splits, history_grams, (split, sums) = (
        refs[ways : ways + 2],
        refs[ways + 2 : ways + 4],
        refs[ways + 4 : ways + 6],
    )
    halo, center, ends, coef_a, coef_b = refs[ways + 6 :]
    columns = fields * (STEPS + 1)
    row, lane = iotas()
    pick = facing("gz", count, received)

    own = set(range(Z))
    k = 0
    for f in range(fields):
        for z in range(Z):
            center[pl.ds(f * CELLS + z * Y, Y), :] = start[f, z]
            halo[0, f, z, 1] = beyond[f, z]
        for d in range(1, 5):
            halo[0, f, SLOTS - d, 0], halo[0, f, Z - 1 + d, 0] = pick(k)
            k += 1
        halo[0, f, SLOTS - 1, 1], halo[0, f, Z, 1] = pick(k)
        low, high = pick(k + 1)
        halo[0, f, SLOTS - 2, 1], halo[0, f, Z + 1, 1] = low, high
        halo[0, f, SLOTS - 3, 1], halo[0, f, Z + 2, 1] = roll(low, -3, 0), roll(high, -3, 0)
        k += 2

    def coefficients(d):
        inside = d > 0.0
        return jnp.where(inside, (d - 1.0) * (1.0 / 7.0), 0.0), jnp.where(inside, 1.0 / 7.0, 0.0)

    for z in range(Z):
        coef_a[z, 0] = (diagonal[z] - 1.0) * (1.0 / 7.0)
        coef_a[z, 1], coef_b[z, 1] = coefficients(beyond[fields, z])
    for d in range(1, 4):
        low, high = pick(k)
        coef_a[SLOTS - d, 0], coef_b[SLOTS - d, 0] = coefficients(low)
        coef_a[Z - 1 + d, 0], coef_b[Z - 1 + d, 0] = coefficients(high)
        k += 1
    low, high = pick(k)
    k += 1
    coef_a[SLOTS - 1, 1], coef_b[SLOTS - 1, 1] = coefficients(low)
    coef_a[Z, 1], coef_b[Z, 1] = coefficients(high)
    coef_a[SLOTS - 2, 1], coef_b[SLOTS - 2, 1] = coefficients(roll(low, -3, 0))
    coef_a[Z + 1, 1], coef_b[Z + 1, 1] = coefficients(roll(high, -3, 0))

    end_coefs = {}
    for part, source in enumerate((sides, beyond_sides)):
        for f in range(0, fields + 1, 2):
            low, high = pick(k)
            k += 1
            for g in (f, f + 1):
                if g > fields:
                    continue
                shift = 32 * (g - f)
                mine = source[g]
                left = jnp.where(
                    lane < 64,
                    mine,
                    jnp.where(lane < 96, roll(high, 64 - shift, 1), roll(low, 96 - shift, 1)),
                )
                right = jnp.where(
                    lane < 64,
                    roll(mine, 64, 1),
                    jnp.where(lane < 96, roll(high, -shift, 1), roll(low, 32 - shift, 1)),
                )
                if g < fields:
                    ends[0, 0, g, part], ends[0, 1, g, part] = left, right
                else:
                    end_coefs[0, part], end_coefs[1, part] = coefficients(left), coefficients(right)

    def read(level, f, z, part):
        if part == 0 and z in own:
            return center[pl.ds((fields * level + f) * CELLS + z * Y, Y), :]
        return halo[level, f, z, part]

    def beside_y(mine, other):
        above, above_other = roll(mine, -1, 0), roll(other, -1, 0)
        below, below_other = roll(mine, 1, 0), roll(other, 1, 0)
        last, first = row == Y - 1, row == 0
        return (
            jnp.where(last, above_other, above) + jnp.where(first, below_other, below),
            jnp.where(last, above, above_other) + jnp.where(first, below, below_other),
        )

    for level in range(1, STEPS + 1):
        reach = STEPS - level
        for f in range(fields):
            joined = [
                jnp.where((lane & 7) <= 3, ends[level - 1, 1, f, p], ends[level - 1, 0, f, p])
                for p in range(2)
            ]
            for at in range(-reach, Z + reach):
                z, before, after = at % SLOTS, (at - 1) % SLOTS, (at + 1) % SLOTS
                distance = max(-at, at - Z + 1, 0)
                tiles = [read(level - 1, f, z, p) for p in range(2)]
                along_y = beside_y(*tiles)
                for part in range(2 if distance < reach else 1):
                    tile = tiles[part]
                    end = roll(joined[part], 124 - 8 * z, 1)
                    total = jnp.where(lane == 0, end, roll(tile, 1, 1))
                    total = total + jnp.where(lane == X - 1, end, roll(tile, -1, 1))
                    total = total + along_y[part]
                    total = total + read(level - 1, f, before, part)
                    total = total + read(level - 1, f, after, part)
                    if part == 0 and z in own:
                        value = coef_a[z, 0] * tile - (1.0 / 7.0) * total
                    else:
                        value = coef_a[z, part] * tile - coef_b[z, part] * total
                    if level > 1:
                        value = value + value - read(level - 2, f, z, part)
                    if part == 0 and z in own:
                        center[pl.ds((fields * level + f) * CELLS + z * Y, Y), :] = value
                    else:
                        halo[level, f, z, part] = value
            if level < STEPS:
                for side in range(2):
                    tiles = [ends[level - 1, side, f, p] for p in range(2)]
                    along_y = beside_y(*tiles)
                    for part in range(2):
                        tile = tiles[part]
                        total = roll(tile, 1, 1) + roll(tile, -1, 1) + along_y[part]
                        total = total + roll(tile, 8, 1) + roll(tile, -8, 1)
                        a, b = end_coefs[side, part]
                        value = a * tile - b * total
                        if level > 1:
                            value = value + value - ends[level - 2, side, f, part]
                        ends[level, side, f, part] = value

    center[pl.ds(columns * CELLS, (BROWS - columns) * CELLS), :] = jnp.zeros(
        ((BROWS - columns) * CELLS, X), F32
    )
    for cell in range(CELLS):
        high, low = split_rows(center[pl.ds(cell, BROWS, stride=CELLS), :], BPAD)
        split[0:BPAD, cell * X : (cell + 1) * X] = high
        split[BPAD : 2 * BPAD, cell * X : (cell + 1) * X] = low
    basis = join_lanes(join(product(split[...], split[...]), BPAD), BPAD)
    cross = product(split[:, : HALF * X], history_splits[0][...])
    cross = cross + product(split[:, HALF * X :], history_splits[1][...])
    cross = join_lanes(join(cross, BPAD), HPAD)
    sums[:, 0:HPAD] = (history_grams[0][...] + history_grams[1][...])[:ROWS]
    sums[0:BROWS, HPAD:] = cross[:BROWS]
    sums[BROWS : 2 * BROWS, HPAD : HPAD + BPAD] = basis[:BROWS]
    sums[BROWS : 2 * BROWS, HPAD + BPAD :] = jnp.zeros((BROWS, X - HPAD - BPAD), F32)
    sums[2 * BROWS :, HPAD:] = jnp.zeros((ROWS - 2 * BROWS, X - HPAD), F32)


def split_rows(rows, padded):
    rows = jnp.concatenate([rows, jnp.zeros((padded - rows.shape[0], rows.shape[1]), F32)], axis=0)
    high = rows.astype(BF16)
    return high, (rows - high.astype(F32)).astype(BF16)


def product(left, right):
    return lax.dot_general(left, right, (((1,), (1,)), ((), ())), preferred_element_type=F32)


def join(both, padded):
    return both[:padded] + both[padded:]


def join_lanes(both, padded):
    return both[:, :padded] + both[:, padded:]


def history_kernel(count, first, history, split, gram):
    for cell in range(HALF):
        high, low = split_rows(history[pl.ds(first + cell, count, stride=CELLS), :], HPAD)
        split[0:HPAD, cell * X : (cell + 1) * X] = high
        split[HPAD : 2 * HPAD, cell * X : (cell + 1) * X] = low
    gram[...] = join_lanes(join(product(split[...], split[...]), HPAD), HPAD)


def split_matrix(matrix):
    high = matrix.astype(BF16)
    return high, (matrix - high.astype(F32)).astype(BF16)


def reciprocal(value):
    guess = pl.reciprocal(value, approx=True)
    guess = guess * (2.0 - value * guess)
    return guess * (2.0 - value * guess)


def finish(columns, cells, first_half, second_half, split, *refs):
    parts, (out, factor) = refs[:-2], refs[-2:]
    total = (parts[0][...] + parts[1][...]) + (parts[2][...] + parts[3][...])
    total = total * (1.0 / cells)
    history_gram = jnp.concatenate([total[:, 0:HPAD], jnp.zeros((HPAD - ROWS, HPAD), F32)], axis=0)
    coef = total[0:BROWS, HPAD:]
    basis_gram = total[BROWS : 2 * BROWS, HPAD : HPAD + BPAD]
    inner = jnp.dot(coef, history_gram, precision=HIGHEST, preferred_element_type=F32) - 2.0 * coef
    inner = jnp.concatenate([inner, jnp.zeros((BPAD - BROWS, HPAD), F32)], axis=0)
    gram = basis_gram + lax.dot_general(
        coef, inner, (((1,), (1,)), ((), ())), precision=HIGHEST, preferred_element_type=F32
    )
    row = lax.broadcasted_iota(jnp.int32, (BROWS, X), 0)
    lane = lax.broadcasted_iota(jnp.int32, (BROWS, X), 1)
    work = jnp.concatenate([gram, jnp.zeros((BROWS, X - BPAD - HPAD), F32), coef], axis=1)
    work = jnp.where(lane == row + BPAD, 1.0, work)
    panel = columns
    for start in range(0, columns, panel):
        spread = [
            jnp.broadcast_to(work[:, k : k + 1], (BROWS, X)) for k in range(start, start + panel)
        ]
        for j in range(panel):
            k = start + j
            scale = spread[j] * reciprocal(spread[j][k : k + 1, :])
            scale = jnp.where(row > k, scale, 0.0)
            for later in range(j + 1, panel):
                spread[later] = spread[later] - scale * spread[later][k : k + 1, :]
            work = work - scale * work[k : k + 1, :]
    pivots = jnp.sum(jnp.where(lane == row, work, 0.0), axis=1, keepdims=True)
    good = lax.broadcasted_iota(jnp.int32, (BROWS, 1), 0) < columns
    work = work * jnp.where(good, 1.0 / jnp.sqrt(jnp.where(good, pivots, 1.0)), 0.0)
    factor[...] = jnp.where(lane >= row, work, 0.0)[0:columns, 0:columns]
    work = jnp.concatenate([work, jnp.zeros((BPAD - BROWS, X), F32)], axis=0)
    history_high, history_low = split_matrix(-work[:, X - HPAD :])
    basis_high, basis_low = split_matrix(work[:, BPAD : 2 * BPAD])
    left = jnp.concatenate(
        [
            jnp.concatenate([history_high, history_high, basis_high, basis_high], axis=1),
            jnp.concatenate(
                [history_low, jnp.zeros_like(history_low), basis_low, jnp.zeros_like(basis_low)], axis=1
            ),
        ],
        axis=0,
    )
    width = 4 * X
    for c in range(CELLS * X // width):
        half, base = (first_half, 0) if c * width < HALF * X else (second_half, HALF * X)
        right = jnp.concatenate(
            [
                half[:, c * width - base : (c + 1) * width - base],
                split[:, c * width : (c + 1) * width],
            ],
            axis=0,
        )
        result = join(jnp.dot(left, right, preferred_element_type=F32), BPAD)
        for j in range(width // X):
            out[pl.ds(c * (width // X) + j, columns, stride=CELLS), :] = result[
                0:columns, j * X : (j + 1) * X
            ]


def call(kernel, outs, flops, bytes_accessed, scratch=(), **specs):
    return pl.pallas_call(
        kernel,
        **specs,
        out_shape=[jax.ShapeDtypeStruct(shape, dtype) for shape, dtype in outs],
        scratch_shapes=list(scratch),
        compiler_params=pltpu.CompilerParams(vmem_limit_bytes=40 * 1024 * 1024),
        cost_estimate=pl.CostEstimate(flops=flops, bytes_accessed=bytes_accessed, transcendentals=0),
    )


def exchange_sums(array, sizes, bits):
    count = sizes[0] * sizes[1] * sizes[2]
    arrays = [array]
    for mask in range(1, 1 << len(bits)):
        flip = sum(bit for i, bit in enumerate(bits) if mask >> i & 1)
        arrays.append(lax.ppermute(array, AXES, [(i, i ^ flip) for i in range(count)]))
    return arrays


def on_device(sizes, history, start, diagonal):
    fields, history_count = start.shape[0], history.shape[0]
    columns = fields * (STEPS + 1)
    all_fields = fields + 1
    count = dict(zip(AXES, sizes))
    ways = {axis: 1 if size == 2 else 2 for axis, size in count.items()}
    cells = Z * Y * X * sizes[0] * sizes[1] * sizes[2]
    tile = Y * X * 4

    def history_products(half):
        with jax.named_scope("history_products"):
            return call(
                functools.partial(history_kernel, history_count, half * HALF),
                [((2 * HPAD, HALF * X), BF16), ((HPAD, HPAD), F32)],
                128 * 128 * CELLS * X,
                history.size * 2,
            )(history.reshape(history_count * CELLS, X))

    with jax.named_scope("halo_x"):
        there = pl.BlockSpec(memory_space=pltpu.HBM)
        start, diagonal, *sends = call(
            functools.partial(pack_x, fields),
            [(start.shape, F32), (diagonal.shape, F32)] + [((all_fields, Y, X), F32)] * ways["gx"],
            1000,
            start.size * 4,
            [pltpu.SemaphoreType.DMA((2,))],
            in_specs=[there, there],
        )(start, diagonal)
        received = swaps(sends, "gx", count["gx"])
    first_split, first_gram = history_products(0)
    with jax.named_scope("halo_y"):
        y_tiles = 4 * all_fields + (all_fields + 1) // 2
        sides, *sends = call(
            functools.partial(pack_y, fields, count["gx"], ways["gx"]),
            [((all_fields, Y, X), F32)] + [((y_tiles, Y, X), F32)] * ways["gy"],
            1000,
            start.size * 4,
        )(start, diagonal, first_gram, *received)
        received = swaps(sends, "gy", count["gy"], False)
    second_split, second_gram = history_products(1)
    with jax.named_scope("halo_z"):
        beyond, beyond_sides, *sends = call(
            functools.partial(pack_z, fields, count["gy"], ways["gy"]),
            [((all_fields, Z, Y, X), F32), ((all_fields, Y, X), F32)]
            + [((z_tiles(fields), Y, X), F32)] * ways["gz"],
            1000,
            start.size * 4,
        )(start, diagonal, second_gram, sides, *received)
        received = swaps(sends, "gz", count["gz"])
    with jax.named_scope("matrix_powers"):
        split, sums = call(
            functools.partial(powers, fields, count["gz"], ways["gz"]),
            [((2 * BPAD, CELLS * X), BF16), ((ROWS, X), F32)],
            2 * 192 * 64 * CELLS * X,
            start.size * 4,
            [
                pltpu.VMEM((STEPS, fields, SLOTS, 2, Y, X), F32),
                pltpu.VMEM((BROWS * CELLS, X), F32),
                pltpu.VMEM((STEPS, 2, fields, 2, Y, X), F32),
                pltpu.VMEM((SLOTS, 2, Y, X), F32),
                pltpu.VMEM((SLOTS, 2, Y, X), F32),
            ],
        )(
            start,
            diagonal,
            sides,
            beyond,
            beyond_sides,
            *received,
            first_split,
            second_split,
            first_gram,
            second_gram,
        )
    with jax.named_scope("sum_over_devices"):
        devices = sizes[0] * sizes[1] * sizes[2]
        bits = []
        for axis, stride in (("gz", 1), ("gx", sizes[1] * sizes[2]), ("gy", sizes[2])):
            bits += [stride << b for b in range(count[axis].bit_length() - 1)]
        first, rest = bits[: 1 + (len(bits) - 1) % 2], bits[1 + (len(bits) - 1) % 2 :]
        for bit in first:
            pair = exchange_sums(sums, sizes, [bit])
            sums = pair[0] + pair[1]
        while rest:
            parts = exchange_sums(sums, sizes, rest[:2])
            rest = rest[2:]
            if rest:
                sums = (parts[0] + parts[1]) + (parts[2] + parts[3])
    with jax.named_scope("orthonormalize"):
        out, factor = call(
            functools.partial(finish, columns, cells),
            [((columns * CELLS, X), F32), ((columns, columns), F32)],
            2 * 192 * 64 * CELLS * X,
            columns * CELLS * X * 4,
        )(first_split, second_split, split, *parts)
    return out.reshape(columns, Z, Y, X), factor


def solution(mesh):
    sizes = tuple(mesh.shape[axis] for axis in AXES)
    return jax.shard_map(
        functools.partial(on_device, sizes),
        mesh=mesh,
        in_specs=(P(None, "gz", "gy", "gx"), P(None, "gz", "gy", "gx"), P("gz", "gy", "gx")),
        out_specs=(P(None, "gz", "gy", "gx"), P()),
        check_vma=False,
    )
```

```python
import functools
import itertools

import jax
import jax.numpy as jnp
from jax import lax
from jax.experimental import pallas as pl
from jax.experimental.pallas import tpu as pltpu
from jax.sharding import PartitionSpec as P

STEPS = 4
F32 = jnp.float32
BF16 = jnp.bfloat16
AXES = ("gx", "gy", "gz")
HIGHEST = lax.Precision.HIGHEST
Z, Y, X = 8, 8, 128
CELLS = Z * Y
HALF = CELLS // 2
PIECE = 16
SLOTS = 16
BPAD = 32
BROWS = 24
HPAD = 64
ROWS = 56


def roll(tile, shift, axis):
    shift %= tile.shape[axis]
    return pltpu.roll(tile, shift, axis) if shift else tile


def iotas():
    return (
        lax.broadcasted_iota(jnp.int32, (Y, X), 0),
        lax.broadcasted_iota(jnp.int32, (Y, X), 1),
    )


def is_even(axis):
    return lax.rem(lax.axis_index(axis), 2) == 0


def facing(axis, count, received):
    index = lax.axis_index(axis)
    even = lax.rem(index, 2) == 0
    low_there, high_there = index > 0, index < count - 1

    def pick(k):
        first = received[0][k]
        if len(received) == 1:
            return jnp.where(even, 0.0, first), jnp.where(even, first, 0.0)
        second = received[1][k]
        low = jnp.where(low_there, jnp.where(even, second, first), 0.0)
        high = jnp.where(high_there, jnp.where(even, first, second), 0.0)
        return low, high

    return pick


def swaps(arrays, sizes, axis):
    first, second = [], []
    dimension = AXES.index(axis)
    aside = 0 if dimension == 2 else 2
    for place in itertools.product(*map(range, sizes)):
        at = place[dimension]

        def pair(dimension, to):
            other = place[:dimension] + (to,) + place[dimension + 1 :]
            return tuple(
                (p[0] * sizes[1] + p[1]) * sizes[2] + p[2] for p in (place, other)
            )

        first.append(pair(dimension, at ^ 1))
        beyond = at + 1 if at % 2 else at - 1
        if 0 <= beyond < sizes[dimension]:
            second.append(pair(dimension, beyond))
        else:
            second.append(pair(aside, place[aside] ^ 1))
    return [lax.ppermute(a, AXES, pairs) for a, pairs in zip(arrays, (first, second))]


def pack_x(fields, start_there, diagonal_there, start, diagonal, *refs):
    sends, done = refs[:-1], refs[-1]
    copies = [
        pltpu.make_async_copy(start_there, start, done.at[0]),
        pltpu.make_async_copy(diagonal_there, diagonal, done.at[1]),
    ]
    for copy in copies:
        copy.start()
    for copy in copies:
        copy.wait()
    _, lane = iotas()
    even = is_even("gx")
    for f in range(fields + 1):
        to_high = jnp.zeros((Y, X), F32)
        to_low = to_high
        for z in range(Z):
            tile = start[f, z] if f < fields else diagonal[z]
            base = 8 * z
            to_high = jnp.where(
                (lane >= base + 1) & (lane < base + 5), roll(tile, base + 5, 1), to_high
            )
            to_low = jnp.where(
                (lane >= base + 3) & (lane < base + 7), roll(tile, base + 3, 1), to_low
            )
        sends[0][f] = jnp.where(even, to_high, to_low)
        if len(sends) > 1:
            sends[1][f] = jnp.where(even, to_low, to_high)


def pack_y(fields, count, ways, start, diagonal, _, *refs):
    received, (sides, *sends) = refs[:ways], refs[ways:]
    row, lane = iotas()
    column = lane & 7
    pick = facing("gx", count, received)
    even = is_even("gy")
    half = lane < X // 2

    def send(k, one, two):
        one_turned, two_turned = roll(one, 4, 0), roll(two, 4, 0)
        to_high = jnp.where(row < 4, one_turned, two)
        to_low = jnp.where(row < 4, one, two_turned)
        sends[0][k] = jnp.where(even, to_high, to_low)
        if len(sends) > 1:
            sends[1][k] = jnp.where(even, to_low, to_high)

    for f in range(fields + 1):
        tiles = [start[f, z] if f < fields else diagonal[z] for z in range(Z)]
        low, high = pick(f)
        side = jnp.where(half & (column >= 1) & (column <= 4), low, 0.0)
        side = jnp.where(
            jnp.logical_not(half) & (column >= 3) & (column <= 6), roll(high, 64, 1), side
        )
        for z in range(Z):
            base = 8 * z
            side = jnp.where(
                (lane >= base + 5) & (lane < base + 8), roll(tiles[z], base + 5, 1), side
            )
            side = jnp.where(
                (lane >= base + 64) & (lane < base + 67), roll(tiles[z], base + 67, 1), side
            )
        sides[f] = side
        for p in range(4):
            send(4 * f + p, tiles[p], tiles[p + 4])
    for f in range(0, fields + 1, 2):
        send(4 * (fields + 1) + f // 2, sides[f], sides[min(f + 1, fields)])


def pack_z(fields, count, ways, start, diagonal, _, __, sides, *refs):
    received, (beyond, beyond_sides, *sends) = refs[:ways], refs[ways:]
    row, lane = iotas()
    pick = facing("gy", count, received)
    even = is_even("gz")
    upper = row < 4

    def unpack(k):
        low, high = pick(k)
        return (
            jnp.where(upper, high, roll(low, 4, 0)),
            jnp.where(upper, roll(high, 4, 0), low),
        )

    for f in range(fields + 1):
        for p in range(4):
            beyond[f, p], beyond[f, p + 4] = unpack(4 * f + p)
    for f in range(0, fields + 1, 2):
        one, two = unpack(4 * (fields + 1) + f // 2)
        beyond_sides[f] = one
        if f < fields:
            beyond_sides[f + 1] = two

    inner = (row == 2) | (row == 3)
    quarter = (lane & 32) == 0
    for which, ref in enumerate(sends):
        up = even if which == 0 else jnp.logical_not(even)
        at = [None] + [jnp.where(up, Z - d, d - 1) for d in range(1, 5)]
        k = 0
        for f in range(fields):
            for d in range(1, 5):
                ref[k] = start[f, at[d]]
                k += 1
            ref[k] = beyond[f, at[1]]
            ref[k + 1] = jnp.where(inner, roll(beyond[f, at[3]], 3, 0), beyond[f, at[2]])
            k += 2
        for d in range(1, 4):
            ref[k] = diagonal[at[d]]
            k += 1
        ref[k] = jnp.where(inner, roll(beyond[fields, at[2]], 3, 0), beyond[fields, at[1]])
        k += 1
        for source in (sides, beyond_sides):
            for f in range(0, fields + 1, 2):
                one, two = source[f], source[min(f + 1, fields)]
                to_high = jnp.where(quarter, roll(one, -32, 1), two)
                to_low = jnp.where(quarter, one, roll(two, 32, 1))
                ref[k] = jnp.where(up, to_high, to_low)
                k += 1


def z_tiles(fields):
    return 6 * fields + 4 + 2 * ((fields + 2) // 2)


def powers(fields, count, ways, start, diagonal, sides, beyond, beyond_sides, *refs):
    received = refs[:ways]
    history_splits, history_grams, (split, sums) = (
        refs[ways : ways + 2],
        refs[ways + 2 : ways + 4],
        refs[ways + 4 : ways + 6],
    )
    halo, center, ends, coef_a, coef_b = refs[ways + 6 :]
    columns = fields * (STEPS + 1)
    row, lane = iotas()
    pick = facing("gz", count, received)

    own = set(range(Z))
    k = 0
    for f in range(fields):
        for z in range(Z):
            center[pl.ds(f * CELLS + z * Y, Y), :] = start[f, z]
            halo[0, f, z, 1] = beyond[f, z]
        for d in range(1, 5):
            halo[0, f, SLOTS - d, 0], halo[0, f, Z - 1 + d, 0] = pick(k)
            k += 1
        halo[0, f, SLOTS - 1, 1], halo[0, f, Z, 1] = pick(k)
        low, high = pick(k + 1)
        halo[0, f, SLOTS - 2, 1], halo[0, f, Z + 1, 1] = low, high
        halo[0, f, SLOTS - 3, 1], halo[0, f, Z + 2, 1] = roll(low, -3, 0), roll(high, -3, 0)
        k += 2

    def coefficients(d):
        inside = d > 0.0
        return jnp.where(inside, (d - 1.0) * (1.0 / 7.0), 0.0), jnp.where(inside, 1.0 / 7.0, 0.0)

    for z in range(Z):
        coef_a[z, 0] = (diagonal[z] - 1.0) * (1.0 / 7.0)
        coef_a[z, 1], coef_b[z, 1] = coefficients(beyond[fields, z])
    for d in range(1, 4):
        low, high = pick(k)
        coef_a[SLOTS - d, 0], coef_b[SLOTS - d, 0] = coefficients(low)
        coef_a[Z - 1 + d, 0], coef_b[Z - 1 + d, 0] = coefficients(high)
        k += 1
    low, high = pick(k)
    k += 1
    coef_a[SLOTS - 1, 1], coef_b[SLOTS - 1, 1] = coefficients(low)
    coef_a[Z, 1], coef_b[Z, 1] = coefficients(high)
    coef_a[SLOTS - 2, 1], coef_b[SLOTS - 2, 1] = coefficients(roll(low, -3, 0))
    coef_a[Z + 1, 1], coef_b[Z + 1, 1] = coefficients(roll(high, -3, 0))

    end_coefs = {}
    for part, source in enumerate((sides, beyond_sides)):
        for f in range(0, fields + 1, 2):
            low, high = pick(k)
            k += 1
            for g in (f, f + 1):
                if g > fields:
                    continue
                shift = 32 * (g - f)
                mine = source[g]
                left = jnp.where(
                    lane < 64,
                    mine,
                    jnp.where(lane < 96, roll(high, 64 - shift, 1), roll(low, 96 - shift, 1)),
                )
                right = jnp.where(
                    lane < 64,
                    roll(mine, 64, 1),
                    jnp.where(lane < 96, roll(high, -shift, 1), roll(low, 32 - shift, 1)),
                )
                if g < fields:
                    ends[0, 0, g, part], ends[0, 1, g, part] = left, right
                else:
                    end_coefs[0, part], end_coefs[1, part] = coefficients(left), coefficients(right)

    def read(level, f, z, part):
        if part == 0 and z in own:
            return center[pl.ds((fields * level + f) * CELLS + z * Y, Y), :]
        return halo[level, f, z, part]

    def beside_y(mine, other):
        above, above_other = roll(mine, -1, 0), roll(other, -1, 0)
        below, below_other = roll(mine, 1, 0), roll(other, 1, 0)
        last, first = row == Y - 1, row == 0
        return (
            jnp.where(last, above_other, above) + jnp.where(first, below_other, below),
            jnp.where(last, above, above_other) + jnp.where(first, below, below_other),
        )

    for level in range(1, STEPS + 1):
        reach = STEPS - level
        for f in range(fields):
            joined = [
                jnp.where((lane & 7) <= 3, ends[level - 1, 1, f, p], ends[level - 1, 0, f, p])
                for p in range(2)
            ]
            for at in range(-reach, Z + reach):
                z, before, after = at % SLOTS, (at - 1) % SLOTS, (at + 1) % SLOTS
                distance = max(-at, at - Z + 1, 0)
                tiles = [read(level - 1, f, z, p) for p in range(2)]
                along_y = beside_y(*tiles)
                for part in range(2 if distance < reach else 1):
                    tile = tiles[part]
                    end = roll(joined[part], 124 - 8 * z, 1)
                    total = jnp.where(lane == 0, end, roll(tile, 1, 1))
                    total = total + jnp.where(lane == X - 1, end, roll(tile, -1, 1))
                    total = total + along_y[part]
                    total = total + read(level - 1, f, before, part)
                    total = total + read(level - 1, f, after, part)
                    if part == 0 and z in own:
                        value = coef_a[z, 0] * tile - (1.0 / 7.0) * total
                    else:
                        value = coef_a[z, part] * tile - coef_b[z, part] * total
                    if level > 1:
                        value = value + value - read(level - 2, f, z, part)
                    if part == 0 and z in own:
                        center[pl.ds((fields * level + f) * CELLS + z * Y, Y), :] = value
                    else:
                        halo[level, f, z, part] = value
            if level < STEPS:
                for side in range(2):
                    tiles = [ends[level - 1, side, f, p] for p in range(2)]
                    along_y = beside_y(*tiles)
                    for part in range(2):
                        tile = tiles[part]
                        total = roll(tile, 1, 1) + roll(tile, -1, 1) + along_y[part]
                        total = total + roll(tile, 8, 1) + roll(tile, -8, 1)
                        a, b = end_coefs[side, part]
                        value = a * tile - b * total
                        if level > 1:
                            value = value + value - ends[level - 2, side, f, part]
                        ends[level, side, f, part] = value

    center[pl.ds(columns * CELLS, (BROWS - columns) * CELLS), :] = jnp.zeros(
        ((BROWS - columns) * CELLS, X), F32
    )
    for cell in range(CELLS):
        high, low = split_rows(center[pl.ds(cell, BROWS, stride=CELLS), :], BPAD)
        split[0:BPAD, cell * X : (cell + 1) * X] = high
        split[BPAD : 2 * BPAD, cell * X : (cell + 1) * X] = low
    basis = join_lanes(join(product(split[...], split[...]), BPAD), BPAD)
    cross = product(split[:, : HALF * X], history_splits[0][...])
    cross = cross + product(split[:, HALF * X :], history_splits[1][...])
    cross = join_lanes(join(cross, BPAD), HPAD)
    sums[:, 0:HPAD] = (history_grams[0][...] + history_grams[1][...])[:ROWS]
    sums[0:BROWS, HPAD:] = cross[:BROWS]
    sums[BROWS : 2 * BROWS, HPAD : HPAD + BPAD] = basis[:BROWS]
    sums[BROWS : 2 * BROWS, HPAD + BPAD :] = jnp.zeros((BROWS, X - HPAD - BPAD), F32)
    sums[2 * BROWS :, HPAD:] = jnp.zeros((ROWS - 2 * BROWS, X - HPAD), F32)


def split_rows(rows, padded):
    rows = jnp.concatenate([rows, jnp.zeros((padded - rows.shape[0], rows.shape[1]), F32)], axis=0)
    high = rows.astype(BF16)
    return high, (rows - high.astype(F32)).astype(BF16)


def product(left, right):
    return lax.dot_general(left, right, (((1,), (1,)), ((), ())), preferred_element_type=F32)


def join(both, padded):
    return both[:padded] + both[padded:]


def join_lanes(both, padded):
    return both[:, :padded] + both[:, padded:]


def load_history(first, history, here, done):
    copy = pltpu.make_async_copy(history.at[:, pl.ds(first, Z // 2)], here, done)
    copy.start()
    copy.wait()


def history_kernel(count, history, split, gram):
    for cell in range(HALF):
        high, low = split_rows(history[pl.ds(cell, count, stride=HALF), :], HPAD)
        split[0:HPAD, cell * X : (cell + 1) * X] = high
        split[HPAD : 2 * HPAD, cell * X : (cell + 1) * X] = low
    gram[...] = join_lanes(join(product(split[...], split[...]), HPAD), HPAD)


def split_matrix(matrix):
    high = matrix.astype(BF16)
    return high, (matrix - high.astype(F32)).astype(BF16)


def reciprocal(value):
    guess = pl.reciprocal(value, approx=True)
    guess = guess * (2.0 - value * guess)
    return guess * (2.0 - value * guess)


def finish(columns, cells, first_half, second_half, split, *refs):
    parts, (out, factor, staged, factor_staged, done) = refs[:-5], refs[-5:]
    total = (parts[0][...] + parts[1][...]) + (parts[2][...] + parts[3][...])
    total = total * (1.0 / cells)
    history_gram = jnp.concatenate([total[:, 0:HPAD], jnp.zeros((HPAD - ROWS, HPAD), F32)], axis=0)
    coef = total[0:BROWS, HPAD:]
    basis_gram = total[BROWS : 2 * BROWS, HPAD : HPAD + BPAD]
    inner = jnp.dot(coef, history_gram, precision=HIGHEST, preferred_element_type=F32) - 2.0 * coef
    inner = jnp.concatenate([inner, jnp.zeros((BPAD - BROWS, HPAD), F32)], axis=0)
    gram = basis_gram + lax.dot_general(
        coef, inner, (((1,), (1,)), ((), ())), precision=HIGHEST, preferred_element_type=F32
    )
    row = lax.broadcasted_iota(jnp.int32, (BROWS, X), 0)
    lane = lax.broadcasted_iota(jnp.int32, (BROWS, X), 1)
    work = jnp.concatenate([gram, jnp.zeros((BROWS, X - BPAD - HPAD), F32), coef], axis=1)
    work = jnp.where(lane == row + BPAD, 1.0, work)
    panel = columns
    for start in range(0, columns, panel):
        spread = [
            jnp.broadcast_to(work[:, k : k + 1], (BROWS, X)) for k in range(start, start + panel)
        ]
        for j in range(panel):
            k = start + j
            scale = spread[j] * reciprocal(spread[j][k : k + 1, :])
            scale = jnp.where(row > k, scale, 0.0)
            for later in range(j + 1, panel):
                spread[later] = spread[later] - scale * spread[later][k : k + 1, :]
            work = work - scale * work[k : k + 1, :]
    pivots = jnp.sum(jnp.where(lane == row, work, 0.0), axis=1, keepdims=True)
    good = lax.broadcasted_iota(jnp.int32, (BROWS, 1), 0) < columns
    work = work * jnp.where(good, 1.0 / jnp.sqrt(jnp.where(good, pivots, 1.0)), 0.0)
    factor_staged[...] = jnp.where(lane >= row, work, 0.0)[0:columns, 0:columns]
    copies = [pltpu.make_async_copy(factor_staged, factor, done.at[0])]
    copies[0].start()
    work = jnp.concatenate([work, jnp.zeros((BPAD - BROWS, X), F32)], axis=0)
    history_high, history_low = split_matrix(-work[:, X - HPAD :])
    basis_high, basis_low = split_matrix(work[:, BPAD : 2 * BPAD])
    left = jnp.concatenate(
        [
            jnp.concatenate([history_high, history_high, basis_high, basis_high], axis=1),
            jnp.concatenate(
                [history_low, jnp.zeros_like(history_low), basis_low, jnp.zeros_like(basis_low)], axis=1
            ),
        ],
        axis=0,
    )
    width = 4 * X
    inside = width // X
    blocks = staged.reshape(columns, CELLS, X)
    for c in range(CELLS // inside):
        half, base = (first_half, 0) if c * inside < HALF else (second_half, HALF * X)
        right = jnp.concatenate(
            [
                half[:, c * width - base : (c + 1) * width - base],
                split[:, c * width : (c + 1) * width],
            ],
            axis=0,
        )
        result = join(jnp.dot(left, right, preferred_element_type=F32), BPAD)
        for j in range(inside):
            staged[pl.ds(c * inside + j, columns, stride=CELLS), :] = result[
                0:columns, j * X : (j + 1) * X
            ]
        cells_done = (c + 1) * inside
        if cells_done % PIECE == 0:
            piece = pl.ds(cells_done - PIECE, PIECE)
            copies.append(
                pltpu.make_async_copy(
                    blocks.at[:, piece, :], out.at[:, piece, :], done.at[len(copies)]
                )
            )
            copies[-1].start()
    for copy in copies:
        copy.wait()


def call(
    kernel,
    outs,
    flops,
    bytes_accessed,
    scratch=(),
    limit=40 * 1024 * 1024,
    place=jax.ShapeDtypeStruct,
    **specs,
):
    return pl.pallas_call(
        kernel,
        **specs,
        out_shape=[place(shape, dtype) for shape, dtype in outs],
        scratch_shapes=list(scratch),
        compiler_params=pltpu.CompilerParams(vmem_limit_bytes=limit),
        cost_estimate=pl.CostEstimate(flops=flops, bytes_accessed=bytes_accessed, transcendentals=0),
    )


def exchange_sums(array, sizes, flips):
    devices = range(sizes[0] * sizes[1] * sizes[2])
    return [array] + [lax.ppermute(array, AXES, [(i, i ^ flip) for i in devices]) for flip in flips]


def on_device(sizes, history, start, diagonal):
    fields, history_count = start.shape[0], history.shape[0]
    columns = fields * (STEPS + 1)
    all_fields = fields + 1
    count = dict(zip(AXES, sizes))
    ways = {axis: 1 if size == 2 else 2 for axis, size in count.items()}
    cells = Z * Y * X * sizes[0] * sizes[1] * sizes[2]
    tile = Y * X * 4

    there = pl.BlockSpec(memory_space=pltpu.HBM)
    anywhere = pl.BlockSpec(memory_space=pl.ANY)
    here = pl.BlockSpec(memory_space=pltpu.VMEM)

    def history_half(half):
        with jax.named_scope("load_history"):
            return call(
                functools.partial(load_history, half * (Z // 2)),
                [((history_count, Z // 2, Y, X), F32)],
                1000,
                history.size * 4,
                [pltpu.SemaphoreType.DMA],
                None,
                pltpu.VMEM,
                in_specs=[there],
            )(history)[0].reshape(history_count * HALF, X)

    def history_products(rows):
        with jax.named_scope("history_products"):
            return call(
                functools.partial(history_kernel, history_count),
                [((2 * HPAD, HALF * X), BF16), ((HPAD, HPAD), F32)],
                128 * 128 * CELLS * X,
                history.size * 2,
            )(rows)

    with jax.named_scope("halo_x"):
        start, diagonal, *sends = call(
            functools.partial(pack_x, fields),
            [(start.shape, F32), (diagonal.shape, F32)] + [((all_fields, Y, X), F32)] * ways["gx"],
            1000,
            start.size * 4,
            [pltpu.SemaphoreType.DMA((2,))],
            None,
            pltpu.VMEM,
            in_specs=[there, there],
        )(start, diagonal)
        received = swaps(sends, sizes, "gx")
    first_rows = history_half(0)
    with jax.named_scope("halo_y"):
        y_tiles = 4 * all_fields + (all_fields + 1) // 2
        sides, *sends = call(
            functools.partial(pack_y, fields, count["gx"], ways["gx"]),
            [((all_fields, Y, X), F32)] + [((y_tiles, Y, X), F32)] * ways["gy"],
            1000,
            start.size * 4,
            in_specs=[here, here, anywhere] + [here] * ways["gx"],
        )(start, diagonal, first_rows, *received)
        received = swaps(sends, sizes, "gy")
    second_rows = history_half(1)
    first_split, first_gram = history_products(first_rows)
    with jax.named_scope("halo_z"):
        beyond, beyond_sides, *sends = call(
            functools.partial(pack_z, fields, count["gy"], ways["gy"]),
            [((all_fields, Z, Y, X), F32), ((all_fields, Y, X), F32)]
            + [((z_tiles(fields), Y, X), F32)] * ways["gz"],
            1000,
            start.size * 4,
            in_specs=[here, here, here, anywhere, here] + [here] * ways["gy"],
        )(start, diagonal, first_gram, second_rows, sides, *received)
        received = swaps(sends, sizes, "gz")
    second_split, second_gram = history_products(second_rows)
    with jax.named_scope("matrix_powers"):
        split, sums = call(
            functools.partial(powers, fields, count["gz"], ways["gz"]),
            [((2 * BPAD, CELLS * X), BF16), ((ROWS, X), F32)],
            2 * 192 * 64 * CELLS * X,
            start.size * 4,
            [
                pltpu.VMEM((STEPS, fields, SLOTS, 2, Y, X), F32),
                pltpu.VMEM((BROWS * CELLS, X), F32),
                pltpu.VMEM((STEPS, 2, fields, 2, Y, X), F32),
                pltpu.VMEM((SLOTS, 2, Y, X), F32),
                pltpu.VMEM((SLOTS, 2, Y, X), F32),
            ],
        )(
            start,
            diagonal,
            sides,
            beyond,
            beyond_sides,
            *received,
            first_split,
            second_split,
            first_gram,
            second_gram,
        )
    with jax.named_scope("sum_over_devices"):
        bits = []
        for axis, stride in (("gz", 1), ("gx", sizes[1] * sizes[2]), ("gy", sizes[2])):
            bits += [stride << b for b in range(count[axis].bit_length() - 1)]
        alone = 1 + (len(bits) - 1) % 2
        for bit in bits[:alone]:
            pair = exchange_sums(sums, sizes, [bit])
            sums = pair[0] + pair[1]
        for k in range(alone, len(bits), 2):
            if k > alone:
                sums = (parts[0] + parts[1]) + (parts[2] + parts[3])
            one, two = bits[k : k + 2]
            flips = [one, two ^ 1, one ^ two ^ 1] if k + 2 == len(bits) else [one ^ 1, two ^ 1, one ^ two]
            parts = exchange_sums(sums, sizes, flips)
    with jax.named_scope("orthonormalize"):
        out, factor = call(
            functools.partial(finish, columns, cells),
            [((columns, CELLS, X), F32), ((columns, columns), F32)],
            2 * 192 * 64 * CELLS * X,
            columns * CELLS * X * 4,
            [
                pltpu.VMEM((columns * CELLS, X), F32),
                pltpu.VMEM((columns, columns), F32),
                pltpu.SemaphoreType.DMA((CELLS // PIECE + 1,)),
            ],
            out_specs=[pl.BlockSpec(memory_space=pltpu.HBM)] * 2,
        )(first_split, second_split, split, *parts)
    return out.reshape(columns, Z, Y, X), factor


def solution(mesh):
    sizes = tuple(mesh.shape[axis] for axis in AXES)
    return jax.shard_map(
        functools.partial(on_device, sizes),
        mesh=mesh,
        in_specs=(P(None, "gz", "gy", "gx"), P(None, "gz", "gy", "gx"), P("gz", "gy", "gx")),
        out_specs=(P(None, "gz", "gy", "gx"), P()),
        check_vma=False,
    )
```

```python
import functools
import itertools

import jax
import jax.numpy as jnp
from jax import lax
from jax.experimental import pallas as pl
from jax.experimental.pallas import tpu as pltpu
from jax.sharding import PartitionSpec as P

STEPS = 4
F32 = jnp.float32
BF16 = jnp.bfloat16
AXES = ("gx", "gy", "gz")
HIGHEST = lax.Precision.HIGHEST
Z, Y, X = 8, 8, 128
CELLS = Z * Y
PIECE = 16
SLOTS = 16
BPAD = 32
BROWS = 24
HPAD = 64
ROWS = 56


def roll(tile, shift, axis):
    shift %= tile.shape[axis]
    return pltpu.roll(tile, shift, axis) if shift else tile


def iotas():
    return (
        lax.broadcasted_iota(jnp.int32, (Y, X), 0),
        lax.broadcasted_iota(jnp.int32, (Y, X), 1),
    )


def is_even(axis):
    return lax.rem(lax.axis_index(axis), 2) == 0


def facing(axis, count, received):
    index = lax.axis_index(axis)
    even = lax.rem(index, 2) == 0
    low_there, high_there = index > 0, index < count - 1

    def pick(k):
        first = received[0][k]
        if len(received) == 1:
            return jnp.where(even, 0.0, first), jnp.where(even, first, 0.0)
        second = received[1][k]
        low = jnp.where(low_there, jnp.where(even, second, first), 0.0)
        high = jnp.where(high_there, jnp.where(even, first, second), 0.0)
        return low, high

    return pick


def swaps(arrays, sizes, axis):
    first, second = [], []
    dimension = AXES.index(axis)
    aside = 0 if dimension == 2 else 2
    for place in itertools.product(*map(range, sizes)):
        at = place[dimension]

        def pair(dimension, to):
            other = place[:dimension] + (to,) + place[dimension + 1 :]
            return tuple(
                (p[0] * sizes[1] + p[1]) * sizes[2] + p[2] for p in (place, other)
            )

        first.append(pair(dimension, at ^ 1))
        beyond = at + 1 if at % 2 else at - 1
        if 0 <= beyond < sizes[dimension]:
            second.append(pair(dimension, beyond))
        else:
            second.append(pair(aside, place[aside] ^ 1))
    return [lax.ppermute(a, AXES, pairs) for a, pairs in zip(arrays, (first, second))]


def choose(right, there, here):
    return (there if right else here) if isinstance(right, bool) else jnp.where(right, there, here)


def turn(tile, right, there, here):
    if isinstance(right, bool):
        return roll(tile, there if right else here, 1)
    return pltpu.roll(tile, jnp.where(right, there % X, here % X), 1)


def ends_of(count):
    return [is_even("gx")] if count == 2 else [False, True]


def pack_y(fields, start_there, diagonal_there, start, diagonal, *refs):
    sends, done = refs[:-1], refs[-1]
    copies = [
        pltpu.make_async_copy(start_there, start, done.at[0]),
        pltpu.make_async_copy(diagonal_there, diagonal, done.at[1]),
    ]
    for copy in copies:
        copy.start()
    for copy in copies:
        copy.wait()
    row, _ = iotas()
    even = is_even("gy")
    for f in range(fields + 1):
        for p in range(4):
            one, two = (start[f, z] if f < fields else diagonal[z] for z in (p, p + 4))
            to_high = jnp.where(row < 4, roll(one, 4, 0), two)
            to_low = jnp.where(row < 4, one, roll(two, 4, 0))
            sends[0][4 * f + p] = jnp.where(even, to_high, to_low)
            if len(sends) > 1:
                sends[1][4 * f + p] = jnp.where(even, to_low, to_high)


def pack_z(fields, count, ways, start, diagonal, _, *refs):
    received, (beyond, *sends) = refs[:ways], refs[ways:]
    row, _ = iotas()
    pick = facing("gy", count, received)
    even = is_even("gz")
    for f in range(fields + 1):
        for p in range(4):
            low, high = pick(4 * f + p)
            beyond[f, p] = jnp.where(row < 4, high, roll(low, 4, 0))
            beyond[f, p + 4] = jnp.where(row < 4, roll(high, 4, 0), low)
    inner = (row == 2) | (row == 3)
    for which, ref in enumerate(sends):
        up = even if which == 0 else jnp.logical_not(even)
        at = [None] + [jnp.where(up, Z - d, d - 1) for d in range(1, 5)]
        k = 0
        for f in range(fields):
            for d in range(1, 5):
                ref[k] = start[f, at[d]]
                k += 1
            ref[k] = beyond[f, at[1]]
            ref[k + 1] = jnp.where(inner, roll(beyond[f, at[3]], 3, 0), beyond[f, at[2]])
            k += 2
        for d in range(1, 4):
            ref[k] = diagonal[at[d]]
            k += 1
        ref[k] = jnp.where(inner, roll(beyond[fields, at[2]], 3, 0), beyond[fields, at[1]])


def z_tiles(fields):
    return 6 * fields + 4


def known(fields, f):
    depth = 4 if f < fields else 3
    for at in range(-depth, Z + depth):
        distance = max(-at, at - Z + 1, 0)
        for part in range(2 if distance < depth else 1):
            yield at % SLOTS, part


def pack_x(fields, count, ways, start, diagonal, _, beyond, *refs):
    received, (wide, *sends) = refs[:ways], refs[ways:]
    _, lane = iotas()
    pick = facing("gz", count, received)
    even = is_even("gx")
    k = 0
    for f in range(fields + 1):
        depth = 4 if f < fields else 3
        for z in range(Z):
            wide[f, z, 0] = start[f, z] if f < fields else diagonal[z]
            wide[f, z, 1] = beyond[f, z]
        for d in range(1, depth + 1):
            wide[f, SLOTS - d, 0], wide[f, Z - 1 + d, 0] = pick(k)
            k += 1
        if f < fields:
            wide[f, SLOTS - 1, 1], wide[f, Z, 1] = pick(k)
            k += 1
        low, high = pick(k)
        k += 1
        wide[f, SLOTS - depth + 2, 1], wide[f, Z + depth - 3, 1] = low, high
        wide[f, SLOTS - depth + 1, 1], wide[f, Z + depth - 2, 1] = roll(low, -3, 0), roll(high, -3, 0)
    for which, ref in enumerate(sends):
        up = even if which == 0 else jnp.logical_not(even)
        for k in range(x_tiles(fields)):
            ref[k] = jnp.zeros((Y, X), F32)
        for f in range(fields + 1):
            for z, part in known(fields, f):
                index, column = divmod(2 * f + part, 4)
                base = 16 * (z % 8) + 4 * column
                moved = turn(wide[f, z, part], up, base + 4, base)
                k = 2 * index + z // 8
                ref[k] = jnp.where((lane >= base) & (lane < base + 4), moved, ref[k])


def x_tiles(fields):
    return 2 * ((2 * (fields + 1) + 3) // 4)


def coefficients(d):
    inside = d > 0.0
    return jnp.where(inside, (d - 1.0) * (1.0 / 7.0), 0.0), jnp.where(inside, 1.0 / 7.0, 0.0)


def beside_y(mine, other):
    row, _ = iotas()
    above, above_other = roll(mine, -1, 0), roll(other, -1, 0)
    below, below_other = roll(mine, 1, 0), roll(other, 1, 0)
    last, first = row == Y - 1, row == 0
    return (
        jnp.where(last, above_other, above) + jnp.where(first, below_other, below),
        jnp.where(last, above, above_other) + jnp.where(first, below, below_other),
    )


def powers(fields, count, wide, history_split, history_gram, center, own, sums, *refs):
    halo, coef_a, coef_b, split = refs
    columns = fields * (STEPS + 1)
    _, lane = iotas()
    inside = set(range(Z))
    ends = ends_of(count)

    for z, part in known(fields, fields):
        if part == 0 and z in inside:
            coef_a[z, 0] = (wide[fields, z, 0] - 1.0) * (1.0 / 7.0)
        else:
            coef_a[z, part], coef_b[z, part] = coefficients(wide[fields, z, part])

    def read(level, f, z, part):
        if level == 0:
            return wide[f, z, part]
        if part == 0 and z in inside:
            return center[pl.ds((fields * level + f) * CELLS + z * Y, Y), :]
        return halo[level - 1, f, z, part]

    for f in range(fields):
        for z in range(Z):
            center[pl.ds(f * CELLS + z * Y, Y), :] = wide[f, z, 0]
    for level in range(1, STEPS + 1):
        reach = STEPS - level
        for f in range(fields):
            for at in range(-reach, Z + reach):
                z, before, after = at % SLOTS, (at - 1) % SLOTS, (at + 1) % SLOTS
                distance = max(-at, at - Z + 1, 0)
                tiles = [read(level - 1, f, z, p) for p in range(2)]
                along_y = beside_y(*tiles)
                for part in range(2 if distance < reach else 1):
                    tile = tiles[part]
                    total = jnp.where(lane == 0, 0.0, roll(tile, 1, 1))
                    total = total + jnp.where(lane == X - 1, 0.0, roll(tile, -1, 1))
                    total = total + along_y[part]
                    total = total + read(level - 1, f, before, part)
                    total = total + read(level - 1, f, after, part)
                    own_cells = part == 0 and z in inside
                    b = 1.0 / 7.0 if own_cells else coef_b[z, part]
                    value = coef_a[z, part] * tile - b * total
                    if level > 1:
                        value = value + value - read(level - 2, f, z, part)
                    if own_cells:
                        center[pl.ds((fields * level + f) * CELLS + z * Y, Y), :] = value
                    else:
                        halo[level - 1, f, z, part] = value
    center[pl.ds(columns * CELLS, (BROWS - columns) * CELLS), :] = jnp.zeros(
        ((BROWS - columns) * CELLS, X), F32
    )

    lanes = lax.broadcasted_iota(jnp.int32, (BROWS, X), 1)
    taken = [(lanes >= first) & (lanes < first + 4) for first in (choose(r, X - 4, 0) for r in ends)]
    for cell in range(CELLS):
        rows = center[pl.ds(cell, BROWS, stride=CELLS), :]
        for mask in taken:
            rows = jnp.where(mask, 0.0, rows)
        high, low = split_rows(rows, BPAD)
        split[0:BPAD, cell * X : (cell + 1) * X] = high
        split[BPAD : 2 * BPAD, cell * X : (cell + 1) * X] = low
    write_sums(sums, split[...], history_split[...])
    sums[:, 0:HPAD] = history_gram[0:ROWS]

    for e, right in enumerate(ends):
        for f in range(fields + 1):
            tiles = [[jnp.zeros((Y, X), F32)] * 2 for _ in range(2)]
            for z, part in known(fields, f):
                base = 16 * (z % 8)
                first = choose(right, base, base + 4)
                moved = turn(wide[f, z, part], right, base + 8, base + 4)
                tiles[part][z // 8] = jnp.where(
                    (lane >= first) & (lane < first + 8), moved, tiles[part][z // 8]
                )
            for part in range(2):
                for t in range(2):
                    own[e, f, part, t] = tiles[part][t]


def write_sums(sums, split, history_split):
    basis = join_lanes(join(product(split, split), BPAD), BPAD)
    cross = join_lanes(join(product(split, history_split), BPAD), HPAD)
    sums[0:BROWS, HPAD:] = cross[:BROWS]
    sums[BROWS : 2 * BROWS, HPAD : HPAD + BPAD] = basis[:BROWS]
    sums[BROWS : 2 * BROWS, HPAD + BPAD :] = jnp.zeros((BROWS, X - HPAD - BPAD), F32)
    sums[2 * BROWS :, HPAD:] = jnp.zeros((ROWS - 2 * BROWS, X - HPAD), F32)


def powers_at_ends(fields, count, ways, own, history_ends, before, *refs):
    received, (sums, patch, work, split) = refs[:ways], refs[ways:]
    columns = fields * (STEPS + 1)
    _, lane = iotas()
    column = lane & 15
    pick = facing("gx", count, received) if count > 2 else None
    ends = ends_of(count)
    taken = (column >= 4) & (column < 8)

    for e, right in enumerate(ends):

        def halo_of(k):
            return received[0][k] if count == 2 else pick(k)[e]

        first = choose(right, 8, 0)
        from_halo = (column >= first) & (column < first + 4)
        coefs = {}
        for f in range(fields + 1):
            for part in range(2):
                index, c = divmod(2 * f + part, 4)
                for t in range(2):
                    moved = turn(halo_of(2 * index + t), right, 8 - 4 * c, -4 * c)
                    tile = jnp.where(from_halo, moved, own[e, f, part, t])
                    if f < fields:
                        work[0, f, part, t] = tile
                    else:
                        coefs[part, t] = coefficients(tile)
        for level in range(1, STEPS + 1):
            for f in range(fields):
                tiles = [[work[level - 1, f, p, t] for t in range(2)] for p in range(2)]
                along_y = [beside_y(tiles[0][t], tiles[1][t]) for t in range(2)]
                for part, t in ((0, 0), (0, 1), (1, 0), (1, 1)):
                    if (level == STEPS and (part or t)) or (level == STEPS - 1 and part and t):
                        continue
                    tile = tiles[part][t]
                    nexts = [roll(tiles[part][i], -16, 1) for i in (t, 1 - t)]
                    lasts = [roll(tiles[part][i], 16, 1) for i in (t, 1 - t)]
                    total = roll(tile, 1, 1) + roll(tile, -1, 1) + along_y[t][part]
                    total = total + jnp.where(lane >= X - 16, nexts[1], nexts[0])
                    total = total + jnp.where(lane < 16, lasts[1], lasts[0])
                    a, b = coefs[part, t]
                    value = a * tile - b * total
                    if level > 1:
                        value = value + value - work[level - 2, f, part, t]
                    work[level, f, part, t] = value
        for level in range(STEPS + 1):
            for f in range(fields):
                k = fields * level + f
                patch[e, k * Y : (k + 1) * Y, :] = jnp.where(taken, work[level, f, 0, 0], 0.0)
        patch[e, columns * Y :, :] = jnp.zeros(((BROWS - columns) * Y, X), F32)
        for y in range(Y):
            high, low = split_rows(patch[e, pl.ds(y, BROWS, stride=Y), :], BPAD)
            at = (e * Y + y) * X
            split[0:BPAD, at : at + X] = high
            split[BPAD : 2 * BPAD, at : at + X] = low
    write_sums(sums, split[...], history_ends[...])
    sums[:, 0:HPAD] = before[:, 0:HPAD]
    sums[:, HPAD:] = sums[:, HPAD:] + before[:, HPAD:]


def patch_and_split(fields, count, center, patch, split, whole):
    _, lane = iotas()
    for k in range(BROWS):
        for z in range(Z):
            tile = center[pl.ds(k * CELLS + z * Y, Y), :]
            if fields <= k < fields * (STEPS + 1):
                for e, right in enumerate(ends_of(count)):
                    base = 16 * z + 4
                    moved = turn(patch[e, k * Y : (k + 1) * Y, :], right, X - 4 - base, -base)
                    first = choose(right, X - 4, 0)
                    tile = jnp.where((lane >= first) & (lane < first + 4), moved, tile)
            whole[pl.ds(k * CELLS + z * Y, Y), :] = tile
    for cell in range(CELLS):
        high, low = split_rows(whole[pl.ds(cell, BROWS, stride=CELLS), :], BPAD)
        split[0:BPAD, cell * X : (cell + 1) * X] = high
        split[BPAD : 2 * BPAD, cell * X : (cell + 1) * X] = low


def split_rows(rows, padded):
    rows = jnp.concatenate([rows, jnp.zeros((padded - rows.shape[0], rows.shape[1]), F32)], axis=0)
    high = rows.astype(BF16)
    return high, (rows - high.astype(F32)).astype(BF16)


def product(left, right):
    return lax.dot_general(left, right, (((1,), (1,)), ((), ())), preferred_element_type=F32)


def join(both, padded):
    return both[:padded] + both[padded:]


def join_lanes(both, padded):
    return both[:, :padded] + both[:, padded:]


def load_history(history, here, done):
    copy = pltpu.make_async_copy(history, here, done)
    copy.start()
    copy.wait()


def pack_history(count, ends_count, history, split, packed):
    _, lane = iotas()
    for e, right in enumerate(ends_of(ends_count)):
        for h in range(count):
            tile = jnp.zeros((Y, X), F32)
            for z in range(Z):
                base = 16 * z + 4
                moved = turn(history[pl.ds(h * CELLS + z * Y, Y), :], right, base + 4, base)
                tile = jnp.where((lane >= base) & (lane < base + 4), moved, tile)
            packed[pl.ds(h * Y, Y), :] = tile
        for y in range(Y):
            high, low = split_rows(packed[pl.ds(y, count, stride=Y), :], HPAD)
            at = (e * Y + y) * X
            split[0:HPAD, at : at + X] = high
            split[HPAD : 2 * HPAD, at : at + X] = low


def history_kernel(count, history, split, gram):
    for cell in range(CELLS):
        high, low = split_rows(history[pl.ds(cell, count, stride=CELLS), :], HPAD)
        split[0:HPAD, cell * X : (cell + 1) * X] = high
        split[HPAD : 2 * HPAD, cell * X : (cell + 1) * X] = low
    gram[...] = join_lanes(join(product(split[...], split[...]), HPAD), HPAD)


def split_matrix(matrix):
    high = matrix.astype(BF16)
    return high, (matrix - high.astype(F32)).astype(BF16)


def reciprocal(value):
    guess = pl.reciprocal(value, approx=True)
    guess = guess * (2.0 - value * guess)
    return guess * (2.0 - value * guess)


def finish(columns, cells, history_split, split, *refs):
    parts, (out, factor, staged, factor_staged, done) = refs[:-5], refs[-5:]
    total = (parts[0][...] + parts[1][...]) + (parts[2][...] + parts[3][...])
    total = total * (1.0 / cells)
    history_gram = jnp.concatenate([total[:, 0:HPAD], jnp.zeros((HPAD - ROWS, HPAD), F32)], axis=0)
    coef = total[0:BROWS, HPAD:]
    basis_gram = total[BROWS : 2 * BROWS, HPAD : HPAD + BPAD]
    inner = jnp.dot(coef, history_gram, precision=HIGHEST, preferred_element_type=F32) - 2.0 * coef
    inner = jnp.concatenate([inner, jnp.zeros((BPAD - BROWS, HPAD), F32)], axis=0)
    gram = basis_gram + lax.dot_general(
        coef, inner, (((1,), (1,)), ((), ())), precision=HIGHEST, preferred_element_type=F32
    )
    row = lax.broadcasted_iota(jnp.int32, (BROWS, X), 0)
    lane = lax.broadcasted_iota(jnp.int32, (BROWS, X), 1)
    work = jnp.concatenate([gram, jnp.zeros((BROWS, X - BPAD - HPAD), F32), coef], axis=1)
    work = jnp.where(lane == row + BPAD, 1.0, work)
    panel = columns
    for start in range(0, columns, panel):
        spread = [
            jnp.broadcast_to(work[:, k : k + 1], (BROWS, X)) for k in range(start, start + panel)
        ]
        for j in range(panel):
            k = start + j
            scale = spread[j] * reciprocal(spread[j][k : k + 1, :])
            scale = jnp.where(row > k, scale, 0.0)
            for later in range(j + 1, panel):
                spread[later] = spread[later] - scale * spread[later][k : k + 1, :]
            work = work - scale * work[k : k + 1, :]
    pivots = jnp.sum(jnp.where(lane == row, work, 0.0), axis=1, keepdims=True)
    good = lax.broadcasted_iota(jnp.int32, (BROWS, 1), 0) < columns
    work = work * jnp.where(good, 1.0 / jnp.sqrt(jnp.where(good, pivots, 1.0)), 0.0)
    factor_staged[...] = jnp.where(lane >= row, work, 0.0)[0:columns, 0:columns]
    copies = [pltpu.make_async_copy(factor_staged, factor, done.at[0])]
    copies[0].start()
    work = jnp.concatenate([work, jnp.zeros((BPAD - BROWS, X), F32)], axis=0)
    history_high, history_low = split_matrix(-work[:, X - HPAD :])
    basis_high, basis_low = split_matrix(work[:, BPAD : 2 * BPAD])
    left = jnp.concatenate(
        [
            jnp.concatenate([history_high, history_high, basis_high, basis_high], axis=1),
            jnp.concatenate(
                [history_low, jnp.zeros_like(history_low), basis_low, jnp.zeros_like(basis_low)], axis=1
            ),
        ],
        axis=0,
    )
    width = 4 * X
    inside = width // X
    blocks = staged.reshape(columns, CELLS, X)
    for c in range(CELLS // inside):
        right = jnp.concatenate(
            [
                history_split[:, c * width : (c + 1) * width],
                split[:, c * width : (c + 1) * width],
            ],
            axis=0,
        )
        result = join(jnp.dot(left, right, preferred_element_type=F32), BPAD)
        for j in range(inside):
            staged[pl.ds(c * inside + j, columns, stride=CELLS), :] = result[
                0:columns, j * X : (j + 1) * X
            ]
        cells_done = (c + 1) * inside
        if cells_done % PIECE == 0:
            piece = pl.ds(cells_done - PIECE, PIECE)
            copies.append(
                pltpu.make_async_copy(
                    blocks.at[:, piece, :], out.at[:, piece, :], done.at[len(copies)]
                )
            )
            copies[-1].start()
    for copy in copies:
        copy.wait()


def call(
    kernel,
    outs,
    flops,
    bytes_accessed,
    scratch=(),
    limit=40 * 1024 * 1024,
    place=jax.ShapeDtypeStruct,
    **specs,
):
    return pl.pallas_call(
        kernel,
        **specs,
        out_shape=[place(shape, dtype) for shape, dtype in outs],
        scratch_shapes=list(scratch),
        compiler_params=pltpu.CompilerParams(vmem_limit_bytes=limit),
        cost_estimate=pl.CostEstimate(flops=flops, bytes_accessed=bytes_accessed, transcendentals=0),
    )


def exchange_sums(array, sizes, flips):
    devices = range(sizes[0] * sizes[1] * sizes[2])
    return [array] + [lax.ppermute(array, AXES, [(i, i ^ flip) for i in devices]) for flip in flips]


def on_device(sizes, history, start, diagonal):
    fields, history_count = start.shape[0], history.shape[0]
    columns = fields * (STEPS + 1)
    all_fields = fields + 1
    count = dict(zip(AXES, sizes))
    ways = {axis: 1 if size == 2 else 2 for axis, size in count.items()}
    cells = Z * Y * X * sizes[0] * sizes[1] * sizes[2]
    tile = Y * X * 4

    ends = 1 if count["gx"] == 2 else 2
    there = pl.BlockSpec(memory_space=pltpu.HBM)
    anywhere = pl.BlockSpec(memory_space=pl.ANY)
    here = pl.BlockSpec(memory_space=pltpu.VMEM)

    with jax.named_scope("halo_y"):
        start, diagonal, *sends = call(
            functools.partial(pack_y, fields),
            [(start.shape, F32), (diagonal.shape, F32)]
            + [((4 * all_fields, Y, X), F32)] * ways["gy"],
            1000,
            start.size * 4,
            [pltpu.SemaphoreType.DMA((2,))],
            None,
            pltpu.VMEM,
            in_specs=[there, there],
        )(start, diagonal)
        received = swaps(sends, sizes, "gy")
    with jax.named_scope("load_history"):
        rows = call(
            load_history,
            [(history.shape, F32)],
            1000,
            history.size * 4,
            [pltpu.SemaphoreType.DMA],
            None,
            pltpu.VMEM,
            in_specs=[there],
        )(history)[0].reshape(history_count * CELLS, X)
    with jax.named_scope("history_at_ends"):
        history_ends = call(
            functools.partial(pack_history, history_count, count["gx"]),
            [((2 * HPAD, ends * Y * X), BF16)],
            1000,
            history.size * 2,
            [pltpu.VMEM((history_count * Y, X), F32)],
        )(rows)[0]
    with jax.named_scope("halo_z"):
        beyond, *sends = call(
            functools.partial(pack_z, fields, count["gy"], ways["gy"]),
            [((all_fields, Z, Y, X), F32)] + [((z_tiles(fields), Y, X), F32)] * ways["gz"],
            1000,
            start.size * 4,
            in_specs=[here, here, anywhere] + [here] * ways["gy"],
        )(start, diagonal, history_ends, *received)
        received = swaps(sends, sizes, "gz")
    with jax.named_scope("history_products"):
        history_split, history_gram = call(
            functools.partial(history_kernel, history_count),
            [((2 * HPAD, CELLS * X), BF16), ((HPAD, HPAD), F32)],
            2 * 128 * 128 * CELLS * X,
            history.size * 4,
        )(rows)
    with jax.named_scope("halo_x"):
        wide, *sends = call(
            functools.partial(pack_x, fields, count["gz"], ways["gz"]),
            [((all_fields, SLOTS, 2, Y, X), F32)]
            + [((x_tiles(fields), Y, X), F32)] * ways["gx"],
            1000,
            start.size * 4,
            in_specs=[here, here, anywhere, here] + [here] * ways["gz"],
        )(start, diagonal, history_gram, beyond, *received)
        received = swaps(sends, sizes, "gx")
    with jax.named_scope("matrix_powers"):
        center, own, sums = call(
            functools.partial(powers, fields, count["gx"]),
            [
                ((BROWS * CELLS, X), F32),
                ((ends, all_fields, 2, 2, Y, X), F32),
                ((ROWS, X), F32),
            ],
            2 * 192 * 64 * CELLS * X,
            start.size * 4,
            [
                pltpu.VMEM((STEPS - 1, fields, SLOTS, 2, Y, X), F32),
                pltpu.VMEM((SLOTS, 2, Y, X), F32),
                pltpu.VMEM((SLOTS, 2, Y, X), F32),
                pltpu.VMEM((2 * BPAD, CELLS * X), BF16),
            ],
        )(wide, history_split, history_gram)
    with jax.named_scope("powers_at_ends"):
        sums, patch = call(
            functools.partial(powers_at_ends, fields, count["gx"], ways["gx"]),
            [((ROWS, X), F32), ((ends, BROWS * Y, X), F32)],
            1000000,
            start.size * 4,
            [
                pltpu.VMEM((STEPS + 1, fields, 2, 2, Y, X), F32),
                pltpu.VMEM((2 * BPAD, ends * Y * X), BF16),
            ],
        )(own, history_ends, sums, *received)
    with jax.named_scope("whole_basis"):
        split = call(
            functools.partial(patch_and_split, fields, count["gx"]),
            [((2 * BPAD, CELLS * X), BF16)],
            1000,
            columns * CELLS * X * 4,
            [pltpu.VMEM((BROWS * CELLS, X), F32)],
        )(center, patch)[0]
    with jax.named_scope("sum_over_devices"):
        bits = []
        for axis, stride in (("gz", 1), ("gx", sizes[1] * sizes[2]), ("gy", sizes[2])):
            bits += [stride << b for b in range(count[axis].bit_length() - 1)]
        alone = 1 + (len(bits) - 1) % 2
        for bit in bits[:alone]:
            pair = exchange_sums(sums, sizes, [bit])
            sums = pair[0] + pair[1]
        for k in range(alone, len(bits), 2):
            if k > alone:
                sums = (parts[0] + parts[1]) + (parts[2] + parts[3])
            one, two = bits[k : k + 2]
            flips = [one, two ^ 1, one ^ two ^ 1] if k + 2 == len(bits) else [one ^ 1, two ^ 1, one ^ two]
            parts = exchange_sums(sums, sizes, flips)
    with jax.named_scope("orthonormalize"):
        out, factor = call(
            functools.partial(finish, columns, cells),
            [((columns, CELLS, X), F32), ((columns, columns), F32)],
            2 * 192 * 64 * CELLS * X,
            columns * CELLS * X * 4,
            [
                pltpu.VMEM((columns * CELLS, X), F32),
                pltpu.VMEM((columns, columns), F32),
                pltpu.SemaphoreType.DMA((CELLS // PIECE + 1,)),
            ],
            out_specs=[pl.BlockSpec(memory_space=pltpu.HBM)] * 2,
        )(history_split, split, *parts)
    return out.reshape(columns, Z, Y, X), factor


def solution(mesh):
    sizes = tuple(mesh.shape[axis] for axis in AXES)
    return jax.shard_map(
        functools.partial(on_device, sizes),
        mesh=mesh,
        in_specs=(P(None, "gz", "gy", "gx"), P(None, "gz", "gy", "gx"), P("gz", "gy", "gx")),
        out_specs=(P(None, "gz", "gy", "gx"), P()),
        check_vma=False,
    )
```

```python
import functools
import itertools

import jax
import jax.numpy as jnp
from jax import lax
from jax.experimental import pallas as pl
from jax.experimental.pallas import tpu as pltpu
from jax.sharding import PartitionSpec as P

STEPS = 4
F32 = jnp.float32
BF16 = jnp.bfloat16
AXES = ("gx", "gy", "gz")
HIGHEST = lax.Precision.HIGHEST
Z, Y, X = 8, 8, 128
CELLS = Z * Y
PIECE = 16
WIDTH = 8
SLOTS = 16
BPAD = 32
BROWS = 24
HPAD = 64
ROWS = 56


def roll(tile, shift, axis):
    shift %= tile.shape[axis]
    return pltpu.roll(tile, shift, axis) if shift else tile


def iotas():
    return (
        lax.broadcasted_iota(jnp.int32, (Y, X), 0),
        lax.broadcasted_iota(jnp.int32, (Y, X), 1),
    )


def is_even(axis):
    return lax.rem(lax.axis_index(axis), 2) == 0


def facing(axis, count, received):
    index = lax.axis_index(axis)
    even = lax.rem(index, 2) == 0
    low_there, high_there = index > 0, index < count - 1

    def pick(k):
        first = received[0][k]
        if len(received) == 1:
            return jnp.where(even, 0.0, first), jnp.where(even, first, 0.0)
        second = received[1][k]
        low = jnp.where(low_there, jnp.where(even, second, first), 0.0)
        high = jnp.where(high_there, jnp.where(even, first, second), 0.0)
        return low, high

    return pick


def swaps(arrays, sizes, axis):
    first, second = [], []
    dimension = AXES.index(axis)
    aside = 0 if dimension == 2 else 2
    for place in itertools.product(*map(range, sizes)):
        at = place[dimension]

        def pair(dimension, to):
            other = place[:dimension] + (to,) + place[dimension + 1 :]
            return tuple(
                (p[0] * sizes[1] + p[1]) * sizes[2] + p[2] for p in (place, other)
            )

        first.append(pair(dimension, at ^ 1))
        beyond = at + 1 if at % 2 else at - 1
        if 0 <= beyond < sizes[dimension]:
            second.append(pair(dimension, beyond))
        else:
            second.append(pair(aside, place[aside] ^ 1))
    return [lax.ppermute(a, AXES, pairs) for a, pairs in zip(arrays, (first, second))]


def choose(right, there, here):
    return (there if right else here) if isinstance(right, bool) else jnp.where(right, there, here)


def turn(tile, right, there, here):
    if isinstance(right, bool):
        return roll(tile, there if right else here, 1)
    return pltpu.roll(tile, jnp.where(right, there % X, here % X), 1)


def ends_of(count):
    return [is_even("gx")] if count == 2 else [False, True]


def pack_y(fields, start_there, diagonal_there, start, diagonal, *refs):
    sends, done = refs[:-1], refs[-1]
    copies = [
        pltpu.make_async_copy(start_there, start, done.at[0]),
        pltpu.make_async_copy(diagonal_there, diagonal, done.at[1]),
    ]
    for copy in copies:
        copy.start()
    for copy in copies:
        copy.wait()
    row, _ = iotas()
    even = is_even("gy")
    for f in range(fields + 1):
        for p in range(4):
            one, two = (start[f, z] if f < fields else diagonal[z] for z in (p, p + 4))
            to_high = jnp.where(row < 4, roll(one, 4, 0), two)
            to_low = jnp.where(row < 4, one, roll(two, 4, 0))
            sends[0][4 * f + p] = jnp.where(even, to_high, to_low)
            if len(sends) > 1:
                sends[1][4 * f + p] = jnp.where(even, to_low, to_high)


def pack_z(fields, count, ways, start, diagonal, _, *refs):
    received, (beyond, *sends) = refs[:ways], refs[ways:]
    row, _ = iotas()
    pick = facing("gy", count, received)
    even = is_even("gz")
    for f in range(fields + 1):
        for p in range(4):
            low, high = pick(4 * f + p)
            beyond[f, p] = jnp.where(row < 4, high, roll(low, 4, 0))
            beyond[f, p + 4] = jnp.where(row < 4, roll(high, 4, 0), low)
    inner = (row == 2) | (row == 3)
    for which, ref in enumerate(sends):
        up = even if which == 0 else jnp.logical_not(even)
        at = [None] + [jnp.where(up, Z - d, d - 1) for d in range(1, 5)]
        k = 0
        for f in range(fields):
            for d in range(1, 5):
                ref[k] = start[f, at[d]]
                k += 1
            ref[k] = beyond[f, at[1]]
            ref[k + 1] = jnp.where(inner, roll(beyond[f, at[3]], 3, 0), beyond[f, at[2]])
            k += 2
        for d in range(1, 4):
            ref[k] = diagonal[at[d]]
            k += 1
        ref[k] = jnp.where(inner, roll(beyond[fields, at[2]], 3, 0), beyond[fields, at[1]])


def z_tiles(fields):
    return 6 * fields + 4


def known(fields, f):
    depth = 4 if f < fields else 3
    for at in range(-depth, Z + depth):
        distance = max(-at, at - Z + 1, 0)
        for part in range(2 if distance < depth else 1):
            yield at % SLOTS, part


def pack_x(fields, count, ways, start, diagonal, _, beyond, *refs):
    received, (wide, *sends) = refs[:ways], refs[ways:]
    _, lane = iotas()
    pick = facing("gz", count, received)
    even = is_even("gx")
    k = 0
    for f in range(fields + 1):
        depth = 4 if f < fields else 3
        for z in range(Z):
            wide[f, z, 0] = start[f, z] if f < fields else diagonal[z]
            wide[f, z, 1] = beyond[f, z]
        for d in range(1, depth + 1):
            wide[f, SLOTS - d, 0], wide[f, Z - 1 + d, 0] = pick(k)
            k += 1
        if f < fields:
            wide[f, SLOTS - 1, 1], wide[f, Z, 1] = pick(k)
            k += 1
        low, high = pick(k)
        k += 1
        wide[f, SLOTS - depth + 2, 1], wide[f, Z + depth - 3, 1] = low, high
        wide[f, SLOTS - depth + 1, 1], wide[f, Z + depth - 2, 1] = roll(low, -3, 0), roll(high, -3, 0)
    for which, ref in enumerate(sends):
        up = even if which == 0 else jnp.logical_not(even)
        for k in range(x_tiles(fields)):
            ref[k] = jnp.zeros((Y, X), F32)
        for f in range(fields + 1):
            for z, part in known(fields, f):
                index, column = divmod(2 * f + part, 4)
                base = 16 * (z % 8) + 4 * column
                moved = turn(wide[f, z, part], up, base + 4, base)
                k = 2 * index + z // 8
                ref[k] = jnp.where((lane >= base) & (lane < base + 4), moved, ref[k])


def x_tiles(fields):
    return 2 * ((2 * (fields + 1) + 3) // 4)


def coefficients(d):
    inside = d > 0.0
    return jnp.where(inside, (d - 1.0) * (1.0 / 7.0), 0.0), jnp.where(inside, 1.0 / 7.0, 0.0)


def beside_y(mine, other):
    row, _ = iotas()
    above, above_other = roll(mine, -1, 0), roll(other, -1, 0)
    below, below_other = roll(mine, 1, 0), roll(other, 1, 0)
    last, first = row == Y - 1, row == 0
    return (
        jnp.where(last, above_other, above) + jnp.where(first, below_other, below),
        jnp.where(last, above, above_other) + jnp.where(first, below, below_other),
    )


def powers(fields, count, wide, history_split, center, own, sums, *refs):
    halo, coef_a, coef_b, split = refs
    columns = fields * (STEPS + 1)
    _, lane = iotas()
    inside = set(range(Z))
    ends = ends_of(count)

    for z, part in known(fields, fields):
        if part == 0 and z in inside:
            coef_a[z, 0] = (wide[fields, z, 0] - 1.0) * (1.0 / 7.0)
        else:
            coef_a[z, part], coef_b[z, part] = coefficients(wide[fields, z, part])

    def read(level, f, z, part):
        if level == 0:
            return wide[f, z, part]
        if part == 0 and z in inside:
            return center[pl.ds((fields * level + f) * CELLS + z * Y, Y), :]
        return halo[level - 1, f, z, part]

    for f in range(fields):
        for z in range(Z):
            center[pl.ds(f * CELLS + z * Y, Y), :] = wide[f, z, 0]
    for level in range(1, STEPS + 1):
        reach = STEPS - level
        for f in range(fields):
            for at in range(-reach, Z + reach):
                z, before, after = at % SLOTS, (at - 1) % SLOTS, (at + 1) % SLOTS
                distance = max(-at, at - Z + 1, 0)
                tiles = [read(level - 1, f, z, p) for p in range(2)]
                along_y = beside_y(*tiles)
                for part in range(2 if distance < reach else 1):
                    tile = tiles[part]
                    total = jnp.where(lane == 0, 0.0, roll(tile, 1, 1))
                    total = total + jnp.where(lane == X - 1, 0.0, roll(tile, -1, 1))
                    total = total + along_y[part]
                    total = total + read(level - 1, f, before, part)
                    total = total + read(level - 1, f, after, part)
                    own_cells = part == 0 and z in inside
                    b = 1.0 / 7.0 if own_cells else coef_b[z, part]
                    value = coef_a[z, part] * tile - b * total
                    if level > 1:
                        value = value + value - read(level - 2, f, z, part)
                    if own_cells:
                        center[pl.ds((fields * level + f) * CELLS + z * Y, Y), :] = value
                    else:
                        halo[level - 1, f, z, part] = value
    center[pl.ds(columns * CELLS, (BROWS - columns) * CELLS), :] = jnp.zeros(
        ((BROWS - columns) * CELLS, X), F32
    )

    lanes = lax.broadcasted_iota(jnp.int32, (BROWS, X), 1)
    taken = [(lanes >= first) & (lanes < first + 4) for first in (choose(r, X - 4, 0) for r in ends)]
    for cell in range(CELLS):
        rows = center[pl.ds(cell, BROWS, stride=CELLS), :]
        for mask in taken:
            rows = jnp.where(mask, 0.0, rows)
        high, low = split_rows(rows, BPAD)
        split[0:BPAD, cell * X : (cell + 1) * X] = high
        split[BPAD : 2 * BPAD, cell * X : (cell + 1) * X] = low
    sums[...] = inner_products(split[...], history_split[...])

    for e, right in enumerate(ends):
        for f in range(fields + 1):
            tiles = [[jnp.zeros((Y, X), F32)] * 2 for _ in range(2)]
            for z, part in known(fields, f):
                base = 16 * (z % 8)
                first = choose(right, base, base + 4)
                moved = turn(wide[f, z, part], right, base + 8, base + 4)
                tiles[part][z // 8] = jnp.where(
                    (lane >= first) & (lane < first + 8), moved, tiles[part][z // 8]
                )
            for part in range(2):
                for t in range(2):
                    own[e, f, part, t] = tiles[part][t]


def inner_products(split, history_split):
    basis = join_lanes(join(product(split, split), BPAD), BPAD)
    cross = join_lanes(join(product(split, history_split), BPAD), HPAD)
    both = jnp.concatenate([cross, basis, jnp.zeros((BPAD, X - HPAD - BPAD), F32)], axis=1)
    return both[:BROWS]


def powers_at_ends(fields, count, ways, own, history_ends, before, history_gram, *refs):
    received, (sums, patch, work, split) = refs[:ways], refs[ways:]
    columns = fields * (STEPS + 1)
    _, lane = iotas()
    column = lane & 15
    pick = facing("gx", count, received) if count > 2 else None
    ends = ends_of(count)
    taken = (column >= 4) & (column < 8)

    for e, right in enumerate(ends):

        def halo_of(k):
            return received[0][k] if count == 2 else pick(k)[e]

        first = choose(right, 8, 0)
        from_halo = (column >= first) & (column < first + 4)
        coefs = {}
        for f in range(fields + 1):
            for part in range(2):
                index, c = divmod(2 * f + part, 4)
                for t in range(2):
                    moved = turn(halo_of(2 * index + t), right, 8 - 4 * c, -4 * c)
                    tile = jnp.where(from_halo, moved, own[e, f, part, t])
                    if f < fields:
                        work[0, f, part, t] = tile
                    else:
                        coefs[part, t] = coefficients(tile)
        for level in range(1, STEPS + 1):
            for f in range(fields):
                tiles = [[work[level - 1, f, p, t] for t in range(2)] for p in range(2)]
                along_y = [beside_y(tiles[0][t], tiles[1][t]) for t in range(2)]
                for part, t in ((0, 0), (0, 1), (1, 0), (1, 1)):
                    if (level == STEPS and (part or t)) or (level == STEPS - 1 and part and t):
                        continue
                    tile = tiles[part][t]
                    nexts = [roll(tiles[part][i], -16, 1) for i in (t, 1 - t)]
                    lasts = [roll(tiles[part][i], 16, 1) for i in (t, 1 - t)]
                    total = roll(tile, 1, 1) + roll(tile, -1, 1) + along_y[t][part]
                    total = total + jnp.where(lane >= X - 16, nexts[1], nexts[0])
                    total = total + jnp.where(lane < 16, lasts[1], lasts[0])
                    a, b = coefs[part, t]
                    value = a * tile - b * total
                    if level > 1:
                        value = value + value - work[level - 2, f, part, t]
                    work[level, f, part, t] = value
        for level in range(STEPS + 1):
            for f in range(fields):
                k = fields * level + f
                patch[e, k * Y : (k + 1) * Y, :] = jnp.where(taken, work[level, f, 0, 0], 0.0)
        patch[e, columns * Y :, :] = jnp.zeros(((BROWS - columns) * Y, X), F32)
        for y in range(Y):
            high, low = split_rows(patch[e, pl.ds(y, BROWS, stride=Y), :], BPAD)
            at = (e * Y + y) * X
            split[0:BPAD, at : at + X] = high
            split[BPAD : 2 * BPAD, at : at + X] = low
    both = before[...] + inner_products(split[...], history_ends[...])
    first, second, third = (both[k : k + Y] for k in range(0, BROWS, Y))
    sums[0:8] = history_gram[0:8]
    sums[8:16] = jnp.where(lane < 96, history_gram[8:16], roll(first, 32, 1))
    sums[16:24] = jnp.where(lane < ROWS, first, roll(second, ROWS, 1))
    sums[24:32] = jnp.where(
        lane < ROWS, third, jnp.where(lane < 80, roll(second, -8, 1), roll(third, 16, 1))
    )


PACKED = ((0, 0), (0, 56), (1, 0), (1, 40), (0, 104), (1, 72), (1, 88))


def pack_gram(gram):
    _, lane = iotas()
    gram = jnp.concatenate([gram, jnp.zeros((HPAD, X - HPAD), F32)], axis=1)
    tiles = [jnp.zeros((Y, X), F32)] * 2
    for i, (t, first) in enumerate(PACKED):
        inside = (lane >= first) & (lane < first + ROWS - 8 * i)
        tiles[t] = jnp.where(inside, roll(gram[8 * i : 8 * i + 8], first - 8 * i, 1), tiles[t])
    return jnp.concatenate(tiles, axis=0)


def unpack_sums(total):
    _, lane = iotas()
    tiles = [total[8 * k : 8 * k + 8] for k in range(4)]
    rows = []
    for i, (t, first) in enumerate(PACKED):
        row = jnp.where((lane >= 8 * i) & (lane < ROWS), roll(tiles[t], 8 * i - first, 1), 0.0)
        rows.append(jnp.where(lane < 8 * i + 8, 0.5 * row, row))
    rows.append(jnp.zeros((Y, X), F32))
    upper = jnp.concatenate(rows, axis=0)[:, :HPAD]
    coef = [tiles[2], roll(tiles[2], -ROWS, 1), tiles[3]]
    coef = jnp.concatenate([jnp.where(lane < ROWS, c, 0.0) for c in coef], axis=0)[:, :HPAD]
    basis = [roll(tiles[1], -96, 1), roll(tiles[3], -ROWS, 1), roll(tiles[3], -80, 1)]
    basis = jnp.concatenate([jnp.where(lane < BROWS, b, 0.0) for b in basis], axis=0)[:, :BPAD]
    return upper, coef, basis


def patch_and_split(fields, count, center, patch, split, whole):
    _, lane = iotas()
    for k in range(BROWS):
        for z in range(Z):
            tile = center[pl.ds(k * CELLS + z * Y, Y), :]
            if fields <= k < fields * (STEPS + 1):
                for e, right in enumerate(ends_of(count)):
                    base = 16 * z + 4
                    moved = turn(patch[e, k * Y : (k + 1) * Y, :], right, X - 4 - base, -base)
                    first = choose(right, X - 4, 0)
                    tile = jnp.where((lane >= first) & (lane < first + 4), moved, tile)
            whole[pl.ds(k * CELLS + z * Y, Y), :] = tile
    for cell in range(CELLS):
        high, low = split_rows(whole[pl.ds(cell, BROWS, stride=CELLS), :], BPAD)
        split[0:BPAD, cell * X : (cell + 1) * X] = high
        split[BPAD : 2 * BPAD, cell * X : (cell + 1) * X] = low


def split_rows(rows, padded):
    rows = jnp.concatenate([rows, jnp.zeros((padded - rows.shape[0], rows.shape[1]), F32)], axis=0)
    high = rows.astype(BF16)
    return high, (rows - high.astype(F32)).astype(BF16)


def product(left, right):
    return lax.dot_general(left, right, (((1,), (1,)), ((), ())), preferred_element_type=F32)


def join(both, padded):
    return both[:padded] + both[padded:]


def join_lanes(both, padded):
    return both[:, :padded] + both[:, padded:]


def load_history(history, here, done):
    copy = pltpu.make_async_copy(history, here, done)
    copy.start()
    copy.wait()


def pack_history(count, ends_count, history, split, packed):
    _, lane = iotas()
    for e, right in enumerate(ends_of(ends_count)):
        for h in range(count):
            tile = jnp.zeros((Y, X), F32)
            for z in range(Z):
                base = 16 * z + 4
                moved = turn(history[pl.ds(h * CELLS + z * Y, Y), :], right, base + 4, base)
                tile = jnp.where((lane >= base) & (lane < base + 4), moved, tile)
            packed[pl.ds(h * Y, Y), :] = tile
        for y in range(Y):
            high, low = split_rows(packed[pl.ds(y, count, stride=Y), :], HPAD)
            at = (e * Y + y) * X
            split[0:HPAD, at : at + X] = high
            split[HPAD : 2 * HPAD, at : at + X] = low


def history_kernel(count, history, split, gram):
    for cell in range(CELLS):
        high, low = split_rows(history[pl.ds(cell, count, stride=CELLS), :], HPAD)
        split[0:HPAD, cell * X : (cell + 1) * X] = high
        split[HPAD : 2 * HPAD, cell * X : (cell + 1) * X] = low
    gram[...] = pack_gram(join_lanes(join(product(split[...], split[...]), HPAD), HPAD))


def split_matrix(matrix):
    high = matrix.astype(BF16)
    return high, (matrix - high.astype(F32)).astype(BF16)


def reciprocal(value):
    guess = pl.reciprocal(value, approx=True)
    guess = guess * (2.0 - value * guess)
    return guess * (2.0 - value * guess)


def finish(columns, cells, history_split, split, *refs):
    parts, (out, factor, staged, factor_staged, done, projected) = refs[:-6], refs[-6:]
    total = (parts[0][...] + parts[1][...]) * (1.0 / cells)
    upper, coef, basis_gram = unpack_sums(total)
    inner = jnp.dot(coef, upper, precision=HIGHEST, preferred_element_type=F32)
    inner = inner + lax.dot_general(
        coef, upper, (((1,), (1,)), ((), ())), precision=HIGHEST, preferred_element_type=F32
    )
    inner = inner - 2.0 * coef
    inner = jnp.concatenate([inner, jnp.zeros((BPAD - BROWS, HPAD), F32)], axis=0)
    gram = basis_gram + lax.dot_general(
        coef, inner, (((1,), (1,)), ((), ())), precision=HIGHEST, preferred_element_type=F32
    )
    coef_high, coef_low = split_matrix(-jnp.concatenate([coef, jnp.zeros((BPAD - BROWS, HPAD), F32)], axis=0))
    one = jnp.where(
        lax.broadcasted_iota(jnp.int32, (BPAD, BPAD), 0) == lax.broadcasted_iota(jnp.int32, (BPAD, BPAD), 1), 1.0, 0.0
    ).astype(BF16)
    basis_minus = jnp.concatenate(
        [
            jnp.concatenate([coef_high, coef_high, one, one], axis=1),
            jnp.concatenate([coef_low, jnp.zeros((BPAD, HPAD + 2 * BPAD), BF16)], axis=1),
        ],
        axis=0,
    )
    width = WIDTH * X
    for c in range(CELLS * X // width):
        at = slice(c * width, (c + 1) * width)
        right = jnp.concatenate([history_split[:, at], split[:, at]], axis=0)
        high, low = split_matrix(join(jnp.dot(basis_minus, right, preferred_element_type=F32), BPAD))
        projected[0:BPAD, at] = high
        projected[BPAD:, at] = low
    row = lax.broadcasted_iota(jnp.int32, (BROWS, X), 0)
    lane = lax.broadcasted_iota(jnp.int32, (BROWS, X), 1)
    work = jnp.concatenate([gram, jnp.zeros((BROWS, X - BPAD), F32)], axis=1)
    work = jnp.where(lane == row + BPAD, 1.0, work)
    panel = columns
    for start in range(0, columns, panel):
        spread = [
            jnp.broadcast_to(work[:, k : k + 1], (BROWS, X)) for k in range(start, start + panel)
        ]
        for j in range(panel):
            k = start + j
            scale = spread[j] * reciprocal(spread[j][k : k + 1, :])
            scale = jnp.where(row > k, scale, 0.0)
            for later in range(j + 1, panel):
                spread[later] = spread[later] - scale * spread[later][k : k + 1, :]
            work = work - scale * work[k : k + 1, :]
    pivots = jnp.sum(jnp.where(lane == row, work, 0.0), axis=1, keepdims=True)
    good = lax.broadcasted_iota(jnp.int32, (BROWS, 1), 0) < columns
    work = work * jnp.where(good, 1.0 / jnp.sqrt(jnp.where(good, pivots, 1.0)), 0.0)
    factor_staged[...] = jnp.where(lane >= row, work, 0.0)[0:columns, 0:columns]
    copies = [pltpu.make_async_copy(factor_staged, factor, done.at[0])]
    copies[0].start()
    work = jnp.concatenate([work, jnp.zeros((BPAD - BROWS, X), F32)], axis=0)
    basis_high, basis_low = split_matrix(work[:, BPAD : 2 * BPAD])
    left = jnp.concatenate(
        [
            jnp.concatenate([basis_high, basis_high], axis=1),
            jnp.concatenate([basis_low, jnp.zeros_like(basis_low)], axis=1),
        ],
        axis=0,
    )
    width = WIDTH * X
    inside = width // X
    blocks = staged.reshape(columns, CELLS, X)
    for c in range(CELLS // inside):
        result = join(jnp.dot(left, projected[:, c * width : (c + 1) * width], preferred_element_type=F32), BPAD)
        for j in range(inside):
            staged[pl.ds(c * inside + j, columns, stride=CELLS), :] = result[
                0:columns, j * X : (j + 1) * X
            ]
        cells_done = (c + 1) * inside
        if cells_done % PIECE == 0:
            piece = pl.ds(cells_done - PIECE, PIECE)
            copies.append(
                pltpu.make_async_copy(
                    blocks.at[:, piece, :], out.at[:, piece, :], done.at[len(copies)]
                )
            )
            copies[-1].start()
    for copy in copies:
        copy.wait()


def call(
    kernel,
    outs,
    flops,
    bytes_accessed,
    scratch=(),
    limit=40 * 1024 * 1024,
    place=jax.ShapeDtypeStruct,
    **specs,
):
    return pl.pallas_call(
        kernel,
        **specs,
        out_shape=[place(shape, dtype) for shape, dtype in outs],
        scratch_shapes=list(scratch),
        compiler_params=pltpu.CompilerParams(vmem_limit_bytes=limit),
        cost_estimate=pl.CostEstimate(flops=flops, bytes_accessed=bytes_accessed, transcendentals=0),
    )


def sum_over_devices(array, sizes):
    devices = range(sizes[0] * sizes[1] * sizes[2])
    bits = []
    for axis, stride in ((2, 1), (0, sizes[1] * sizes[2]), (1, sizes[2])):
        bits += [stride << b for b in range(sizes[axis].bit_length() - 1)]
    others = None
    for bit in bits:
        array = array if others is None else array + others
        others = lax.ppermute(array, AXES, [(i, i ^ (bit | 1)) for i in devices])
    return [array, others]


def on_device(sizes, history, start, diagonal):
    fields, history_count = start.shape[0], history.shape[0]
    columns = fields * (STEPS + 1)
    all_fields = fields + 1
    count = dict(zip(AXES, sizes))
    ways = {axis: 1 if size == 2 else 2 for axis, size in count.items()}
    cells = Z * Y * X * sizes[0] * sizes[1] * sizes[2]
    tile = Y * X * 4

    ends = 1 if count["gx"] == 2 else 2
    there = pl.BlockSpec(memory_space=pltpu.HBM)
    anywhere = pl.BlockSpec(memory_space=pl.ANY)
    here = pl.BlockSpec(memory_space=pltpu.VMEM)

    with jax.named_scope("halo_y"):
        start, diagonal, *sends = call(
            functools.partial(pack_y, fields),
            [(start.shape, F32), (diagonal.shape, F32)]
            + [((4 * all_fields, Y, X), F32)] * ways["gy"],
            1000,
            start.size * 4,
            [pltpu.SemaphoreType.DMA((2,))],
            None,
            pltpu.VMEM,
            in_specs=[there, there],
        )(start, diagonal)
        received = swaps(sends, sizes, "gy")
    with jax.named_scope("load_history"):
        rows = call(
            load_history,
            [(history.shape, F32)],
            1000,
            history.size * 4,
            [pltpu.SemaphoreType.DMA],
            None,
            pltpu.VMEM,
            in_specs=[there],
        )(history)[0].reshape(history_count * CELLS, X)
    with jax.named_scope("history_at_ends"):
        history_ends = call(
            functools.partial(pack_history, history_count, count["gx"]),
            [((2 * HPAD, ends * Y * X), BF16)],
            1000,
            history.size * 2,
            [pltpu.VMEM((history_count * Y, X), F32)],
        )(rows)[0]
    with jax.named_scope("halo_z"):
        beyond, *sends = call(
            functools.partial(pack_z, fields, count["gy"], ways["gy"]),
            [((all_fields, Z, Y, X), F32)] + [((z_tiles(fields), Y, X), F32)] * ways["gz"],
            1000,
            start.size * 4,
            in_specs=[here, here, anywhere] + [here] * ways["gy"],
        )(start, diagonal, history_ends, *received)
        received = swaps(sends, sizes, "gz")
    with jax.named_scope("history_products"):
        history_split, history_gram = call(
            functools.partial(history_kernel, history_count),
            [((2 * HPAD, CELLS * X), BF16), ((2 * Y, X), F32)],
            2 * 128 * 128 * CELLS * X,
            history.size * 4,
        )(rows)
    with jax.named_scope("halo_x"):
        wide, *sends = call(
            functools.partial(pack_x, fields, count["gz"], ways["gz"]),
            [((all_fields, SLOTS, 2, Y, X), F32)]
            + [((x_tiles(fields), Y, X), F32)] * ways["gx"],
            1000,
            start.size * 4,
            in_specs=[here, here, anywhere, here] + [here] * ways["gz"],
        )(start, diagonal, history_gram, beyond, *received)
        received = swaps(sends, sizes, "gx")
    with jax.named_scope("matrix_powers"):
        center, own, sums = call(
            functools.partial(powers, fields, count["gx"]),
            [
                ((BROWS * CELLS, X), F32),
                ((ends, all_fields, 2, 2, Y, X), F32),
                ((BROWS, X), F32),
            ],
            2 * 192 * 64 * CELLS * X,
            start.size * 4,
            [
                pltpu.VMEM((STEPS - 1, fields, SLOTS, 2, Y, X), F32),
                pltpu.VMEM((SLOTS, 2, Y, X), F32),
                pltpu.VMEM((SLOTS, 2, Y, X), F32),
                pltpu.VMEM((2 * BPAD, CELLS * X), BF16),
            ],
        )(wide, history_split)
    with jax.named_scope("powers_at_ends"):
        sums, patch = call(
            functools.partial(powers_at_ends, fields, count["gx"], ways["gx"]),
            [((4 * Y, X), F32), ((ends, BROWS * Y, X), F32)],
            1000000,
            start.size * 4,
            [
                pltpu.VMEM((STEPS + 1, fields, 2, 2, Y, X), F32),
                pltpu.VMEM((2 * BPAD, ends * Y * X), BF16),
            ],
        )(own, history_ends, sums, history_gram, *received)
    with jax.named_scope("whole_basis"):
        split = call(
            functools.partial(patch_and_split, fields, count["gx"]),
            [((2 * BPAD, CELLS * X), BF16)],
            1000,
            columns * CELLS * X * 4,
            [pltpu.VMEM((BROWS * CELLS, X), F32)],
        )(center, patch)[0]
    with jax.named_scope("sum_over_devices"):
        parts = sum_over_devices(sums, sizes)
    with jax.named_scope("orthonormalize"):
        out, factor = call(
            functools.partial(finish, columns, cells),
            [((columns, CELLS, X), F32), ((columns, columns), F32)],
            2 * 192 * 64 * CELLS * X,
            columns * CELLS * X * 4,
            [
                pltpu.VMEM((columns * CELLS, X), F32),
                pltpu.VMEM((columns, columns), F32),
                pltpu.SemaphoreType.DMA((CELLS // PIECE + 1,)),
                pltpu.VMEM((2 * BPAD, CELLS * X), BF16),
            ],
            out_specs=[pl.BlockSpec(memory_space=pltpu.HBM)] * 2,
        )(history_split, split, *parts)
    return out.reshape(columns, Z, Y, X), factor


def solution(mesh):
    sizes = tuple(mesh.shape[axis] for axis in AXES)
    return jax.shard_map(
        functools.partial(on_device, sizes),
        mesh=mesh,
        in_specs=(P(None, "gz", "gy", "gx"), P(None, "gz", "gy", "gx"), P("gz", "gy", "gx")),
        out_specs=(P(None, "gz", "gy", "gx"), P()),
        check_vma=False,
    )
```

```python
import functools
import itertools

import jax
import jax.numpy as jnp
from jax import lax
from jax.experimental import pallas as pl
from jax.experimental.pallas import tpu as pltpu
from jax.sharding import PartitionSpec as P

STEPS = 4
F32 = jnp.float32
BF16 = jnp.bfloat16
AXES = ("gx", "gy", "gz")
HIGHEST = lax.Precision.HIGHEST
Z, Y, X = 8, 8, 128
CELLS = Z * Y
PIECE = 16
WIDTH = 8
SLOTS = 16
BPAD = 32
BROWS = 24
HPAD = 64
ROWS = 56


def roll(tile, shift, axis):
    shift %= tile.shape[axis]
    return pltpu.roll(tile, shift, axis) if shift else tile


def iotas():
    return (
        lax.broadcasted_iota(jnp.int32, (Y, X), 0),
        lax.broadcasted_iota(jnp.int32, (Y, X), 1),
    )


def is_even(axis):
    return lax.rem(lax.axis_index(axis), 2) == 0


def facing(axis, count, received):
    index = lax.axis_index(axis)
    even = lax.rem(index, 2) == 0
    low_there, high_there = index > 0, index < count - 1

    def pick(k):
        first = received[0][k]
        if len(received) == 1:
            return jnp.where(even, 0.0, first), jnp.where(even, first, 0.0)
        second = received[1][k]
        low = jnp.where(low_there, jnp.where(even, second, first), 0.0)
        high = jnp.where(high_there, jnp.where(even, first, second), 0.0)
        return low, high

    return pick


def swaps(arrays, sizes, axis):
    first, second = [], []
    dimension = AXES.index(axis)
    aside = 0 if dimension == 2 else 2
    for place in itertools.product(*map(range, sizes)):
        at = place[dimension]

        def pair(dimension, to):
            other = place[:dimension] + (to,) + place[dimension + 1 :]
            return tuple(
                (p[0] * sizes[1] + p[1]) * sizes[2] + p[2] for p in (place, other)
            )

        first.append(pair(dimension, at ^ 1))
        beyond = at + 1 if at % 2 else at - 1
        if 0 <= beyond < sizes[dimension]:
            second.append(pair(dimension, beyond))
        else:
            second.append(pair(aside, place[aside] ^ 1))
    return [lax.ppermute(a, AXES, pairs) for a, pairs in zip(arrays, (first, second))]


def choose(right, there, here):
    return (there if right else here) if isinstance(right, bool) else jnp.where(right, there, here)


def turn(tile, right, there, here):
    if isinstance(right, bool):
        return roll(tile, there if right else here, 1)
    return pltpu.roll(tile, jnp.where(right, there % X, here % X), 1)


def ends_of(count):
    return [is_even("gx")] if count == 2 else [False, True]


def pack_y(fields, start_there, diagonal_there, start, diagonal, *refs):
    sends, done = refs[:-1], refs[-1]
    copies = [
        pltpu.make_async_copy(start_there.at[f], start.at[f], done.at[f]) for f in range(fields)
    ]
    copies.append(pltpu.make_async_copy(diagonal_there, diagonal, done.at[fields]))
    for copy in copies:
        copy.start()
    row, _ = iotas()
    even = is_even("gy")
    for f in range(fields + 1):
        copies[f].wait()
        for p in range(4):
            one, two = (start[f, z] if f < fields else diagonal[z] for z in (p, p + 4))
            to_high = jnp.where(row < 4, roll(one, 4, 0), two)
            to_low = jnp.where(row < 4, one, roll(two, 4, 0))
            sends[0][4 * f + p] = jnp.where(even, to_high, to_low)
            if len(sends) > 1:
                sends[1][4 * f + p] = jnp.where(even, to_low, to_high)


def pack_z(fields, count, ways, start, diagonal, _, *refs):
    received, (beyond, *sends) = refs[:ways], refs[ways:]
    row, _ = iotas()
    pick = facing("gy", count, received)
    even = is_even("gz")
    for f in range(fields + 1):
        for p in range(4):
            low, high = pick(4 * f + p)
            beyond[f, p] = jnp.where(row < 4, high, roll(low, 4, 0))
            beyond[f, p + 4] = jnp.where(row < 4, roll(high, 4, 0), low)
    inner = (row == 2) | (row == 3)
    for which, ref in enumerate(sends):
        up = even if which == 0 else jnp.logical_not(even)
        at = [None] + [jnp.where(up, Z - d, d - 1) for d in range(1, 5)]
        k = 0
        for f in range(fields):
            for d in range(1, 5):
                ref[k] = start[f, at[d]]
                k += 1
            ref[k] = beyond[f, at[1]]
            ref[k + 1] = jnp.where(inner, roll(beyond[f, at[3]], 3, 0), beyond[f, at[2]])
            k += 2
        for d in range(1, 4):
            ref[k] = diagonal[at[d]]
            k += 1
        ref[k] = jnp.where(inner, roll(beyond[fields, at[2]], 3, 0), beyond[fields, at[1]])


def z_tiles(fields):
    return 6 * fields + 4


def known(fields, f):
    depth = 4 if f < fields else 3
    for at in range(-depth, Z + depth):
        distance = max(-at, at - Z + 1, 0)
        for part in range(2 if distance < depth else 1):
            yield at % SLOTS, part


def end_columns(fields, up, tile_of, halo):
    _, lane = iotas()
    tiles = [jnp.zeros((Y, X), F32)] * x_tiles(fields)
    for f in range(fields + 1):
        for z, part in known(fields, f):
            if (z >= Z) != halo:
                continue
            index, column = divmod(2 * f + part, 4)
            base = 16 * (z % 8) + 4 * column
            moved = turn(tile_of(f, z, part), up, base + 4, base)
            k = 2 * index + z // 8
            tiles[k] = jnp.where((lane >= base) & (lane < base + 4), moved, tiles[k])
    return tiles


def pack_x_own(fields, start, diagonal, beyond, *sends):
    def tile_of(f, z, part):
        if part:
            return beyond[f, z]
        return start[f, z] if f < fields else diagonal[z]

    even = is_even("gx")
    for which, ref in enumerate(sends):
        tiles = end_columns(fields, even if which == 0 else jnp.logical_not(even), tile_of, False)
        for k, tile in enumerate(tiles):
            ref[k] = tile


def pack_x(fields, count, ways, x_ways, *refs):
    owns, refs = refs[:x_ways], refs[x_ways + 1 :]
    received, (wide, *sends) = refs[:ways], refs[ways:]
    pick = facing("gz", count, received)
    even = is_even("gx")
    found = {}
    k = 0
    for f in range(fields + 1):
        depth = 4 if f < fields else 3
        for d in range(1, depth + 1):
            found[f, SLOTS - d, 0], found[f, Z - 1 + d, 0] = pick(k)
            k += 1
        if f < fields:
            found[f, SLOTS - 1, 1], found[f, Z, 1] = pick(k)
            k += 1
        low, high = pick(k)
        k += 1
        found[f, SLOTS - depth + 2, 1], found[f, Z + depth - 3, 1] = low, high
        found[f, SLOTS - depth + 1, 1] = roll(low, -3, 0)
        found[f, Z + depth - 2, 1] = roll(high, -3, 0)
    for (f, z, part), tile in found.items():
        wide[f, z - Z, part] = tile
    for which, ref in enumerate(sends):
        up = even if which == 0 else jnp.logical_not(even)
        tiles = end_columns(fields, up, lambda f, z, part: found[f, z, part], True)
        for k, tile in enumerate(tiles):
            ref[k] = tile + owns[which][k]


def x_tiles(fields):
    return 2 * ((2 * (fields + 1) + 3) // 4)


def coefficients(d):
    inside = d > 0.0
    return jnp.where(inside, (d - 1.0) * (1.0 / 7.0), 0.0), jnp.where(inside, 1.0 / 7.0, 0.0)


def beside_y(mine, other):
    row, _ = iotas()
    above, above_other = roll(mine, -1, 0), roll(other, -1, 0)
    below, below_other = roll(mine, 1, 0), roll(other, 1, 0)
    last, first = row == Y - 1, row == 0
    return (
        jnp.where(last, above_other, above) + jnp.where(first, below_other, below),
        jnp.where(last, above, above_other) + jnp.where(first, below, below_other),
    )


def powers(fields, count, start, diagonal, beyond, wide, history_split, center, own, sums, *refs):
    halo, coef_a, coef_b, split = refs
    columns = fields * (STEPS + 1)
    _, lane = iotas()
    inside = set(range(Z))
    ends = ends_of(count)

    def given(f, z, part):
        if z >= Z:
            return wide[f, z - Z, part]
        if part:
            return beyond[f, z]
        return start[f, z] if f < fields else diagonal[z]

    for z, part in known(fields, fields):
        if part == 0 and z in inside:
            coef_a[z, 0] = (diagonal[z] - 1.0) * (1.0 / 7.0)
        else:
            coef_a[z, part], coef_b[z, part] = coefficients(given(fields, z, part))

    def read(level, f, z, part):
        if level == 0:
            return given(f, z, part)
        if part == 0 and z in inside:
            return center[pl.ds((fields * level + f) * CELLS + z * Y, Y), :]
        return halo[level - 1, f, z, part]

    for f in range(fields):
        for z in range(Z):
            center[pl.ds(f * CELLS + z * Y, Y), :] = start[f, z]
    for level in range(1, STEPS + 1):
        reach = STEPS - level
        for f in range(fields):
            for at in range(-reach, Z + reach):
                z, before, after = at % SLOTS, (at - 1) % SLOTS, (at + 1) % SLOTS
                distance = max(-at, at - Z + 1, 0)
                tiles = [read(level - 1, f, z, p) for p in range(2)]
                along_y = beside_y(*tiles)
                for part in range(2 if distance < reach else 1):
                    tile = tiles[part]
                    total = jnp.where(lane == 0, 0.0, roll(tile, 1, 1))
                    total = total + jnp.where(lane == X - 1, 0.0, roll(tile, -1, 1))
                    total = total + along_y[part]
                    total = total + read(level - 1, f, before, part)
                    total = total + read(level - 1, f, after, part)
                    own_cells = part == 0 and z in inside
                    b = 1.0 / 7.0 if own_cells else coef_b[z, part]
                    value = coef_a[z, part] * tile - b * total
                    if level > 1:
                        value = value + value - read(level - 2, f, z, part)
                    if own_cells:
                        center[pl.ds((fields * level + f) * CELLS + z * Y, Y), :] = value
                    else:
                        halo[level - 1, f, z, part] = value
    center[pl.ds(columns * CELLS, (BROWS - columns) * CELLS), :] = jnp.zeros(
        ((BROWS - columns) * CELLS, X), F32
    )

    lanes = lax.broadcasted_iota(jnp.int32, (BROWS, X), 1)
    taken = [(lanes >= first) & (lanes < first + 4) for first in (choose(r, X - 4, 0) for r in ends)]
    for cell in range(CELLS):
        rows = center[pl.ds(cell, BROWS, stride=CELLS), :]
        for mask in taken:
            rows = jnp.where(mask, 0.0, rows)
        high, low = split_rows(rows, BPAD)
        split[0:BPAD, cell * X : (cell + 1) * X] = high
        split[BPAD : 2 * BPAD, cell * X : (cell + 1) * X] = low
    sums[...] = inner_products(split[...], history_split[...])

    for e, right in enumerate(ends):
        for f in range(fields + 1):
            tiles = [[jnp.zeros((Y, X), F32)] * 2 for _ in range(2)]
            for z, part in known(fields, f):
                base = 16 * (z % 8)
                first = choose(right, base, base + 4)
                moved = turn(given(f, z, part), right, base + 8, base + 4)
                tiles[part][z // 8] = jnp.where(
                    (lane >= first) & (lane < first + 8), moved, tiles[part][z // 8]
                )
            for part in range(2):
                for t in range(2):
                    own[e, f, part, t] = tiles[part][t]


def inner_products(split, history_split):
    basis = join_lanes(join(product(split, split), BPAD), BPAD)
    cross = join_lanes(join(product(split, history_split), BPAD), HPAD)
    both = jnp.concatenate([cross, basis, jnp.zeros((BPAD, X - HPAD - BPAD), F32)], axis=1)
    return both[:BROWS]


def powers_at_ends(fields, count, ways, own, history_ends, before, history_gram, *refs):
    received, (sums, patch, work, split) = refs[:ways], refs[ways:]
    columns = fields * (STEPS + 1)
    _, lane = iotas()
    column = lane & 15
    pick = facing("gx", count, received) if count > 2 else None
    ends = ends_of(count)
    taken = (column >= 4) & (column < 8)

    for e, right in enumerate(ends):

        def halo_of(k):
            return received[0][k] if count == 2 else pick(k)[e]

        first = choose(right, 8, 0)
        from_halo = (column >= first) & (column < first + 4)
        coefs = {}
        for f in range(fields + 1):
            for part in range(2):
                index, c = divmod(2 * f + part, 4)
                for t in range(2):
                    moved = turn(halo_of(2 * index + t), right, 8 - 4 * c, -4 * c)
                    tile = jnp.where(from_halo, moved, own[e, f, part, t])
                    if f < fields:
                        work[0, f, part, t] = tile
                    else:
                        coefs[part, t] = coefficients(tile)
        for level in range(1, STEPS + 1):
            for f in range(fields):
                tiles = [[work[level - 1, f, p, t] for t in range(2)] for p in range(2)]
                along_y = [beside_y(tiles[0][t], tiles[1][t]) for t in range(2)]
                for part, t in ((0, 0), (0, 1), (1, 0), (1, 1)):
                    if (level == STEPS and (part or t)) or (level == STEPS - 1 and part and t):
                        continue
                    tile = tiles[part][t]
                    nexts = [roll(tiles[part][i], -16, 1) for i in (t, 1 - t)]
                    lasts = [roll(tiles[part][i], 16, 1) for i in (t, 1 - t)]
                    total = roll(tile, 1, 1) + roll(tile, -1, 1) + along_y[t][part]
                    total = total + jnp.where(lane >= X - 16, nexts[1], nexts[0])
                    total = total + jnp.where(lane < 16, lasts[1], lasts[0])
                    a, b = coefs[part, t]
                    value = a * tile - b * total
                    if level > 1:
                        value = value + value - work[level - 2, f, part, t]
                    work[level, f, part, t] = value
        for level in range(STEPS + 1):
            for f in range(fields):
                k = fields * level + f
                patch[e, k * Y : (k + 1) * Y, :] = jnp.where(taken, work[level, f, 0, 0], 0.0)
        patch[e, columns * Y :, :] = jnp.zeros(((BROWS - columns) * Y, X), F32)
        for y in range(Y):
            high, low = split_rows(patch[e, pl.ds(y, BROWS, stride=Y), :], BPAD)
            at = (e * Y + y) * X
            split[0:BPAD, at : at + X] = high
            split[BPAD : 2 * BPAD, at : at + X] = low
    both = before[...] + inner_products(split[...], history_ends[...])
    first, second, third = (both[k : k + Y] for k in range(0, BROWS, Y))
    sums[0:8] = history_gram[0:8]
    sums[8:16] = jnp.where(lane < 96, history_gram[8:16], roll(first, 32, 1))
    sums[16:24] = jnp.where(lane < ROWS, first, roll(second, ROWS, 1))
    sums[24:32] = jnp.where(
        lane < ROWS, third, jnp.where(lane < 80, roll(second, -8, 1), roll(third, 16, 1))
    )


PACKED = ((0, 0), (0, 56), (1, 0), (1, 40), (0, 104), (1, 72), (1, 88))


def pack_gram(gram):
    _, lane = iotas()
    gram = jnp.concatenate([gram, jnp.zeros((HPAD, X - HPAD), F32)], axis=1)
    tiles = [jnp.zeros((Y, X), F32)] * 2
    for i, (t, first) in enumerate(PACKED):
        inside = (lane >= first) & (lane < first + ROWS - 8 * i)
        tiles[t] = jnp.where(inside, roll(gram[8 * i : 8 * i + 8], first - 8 * i, 1), tiles[t])
    return jnp.concatenate(tiles, axis=0)


def unpack_sums(total):
    _, lane = iotas()
    tiles = [total[8 * k : 8 * k + 8] for k in range(4)]
    rows = []
    for i, (t, first) in enumerate(PACKED):
        row = jnp.where((lane >= 8 * i) & (lane < ROWS), roll(tiles[t], 8 * i - first, 1), 0.0)
        rows.append(jnp.where(lane < 8 * i + 8, 0.5 * row, row))
    rows.append(jnp.zeros((Y, X), F32))
    upper = jnp.concatenate(rows, axis=0)[:, :HPAD]
    coef = [tiles[2], roll(tiles[2], -ROWS, 1), tiles[3]]
    coef = jnp.concatenate([jnp.where(lane < ROWS, c, 0.0) for c in coef], axis=0)[:, :HPAD]
    basis = [roll(tiles[1], -96, 1), roll(tiles[3], -ROWS, 1), roll(tiles[3], -80, 1)]
    basis = jnp.concatenate([jnp.where(lane < BROWS, b, 0.0) for b in basis], axis=0)[:, :BPAD]
    return upper, coef, basis


def patch_and_split(fields, count, center, patch, split, whole):
    _, lane = iotas()
    for k in range(BROWS):
        for z in range(Z):
            tile = center[pl.ds(k * CELLS + z * Y, Y), :]
            if fields <= k < fields * (STEPS + 1):
                for e, right in enumerate(ends_of(count)):
                    base = 16 * z + 4
                    moved = turn(patch[e, k * Y : (k + 1) * Y, :], right, X - 4 - base, -base)
                    first = choose(right, X - 4, 0)
                    tile = jnp.where((lane >= first) & (lane < first + 4), moved, tile)
            whole[pl.ds(k * CELLS + z * Y, Y), :] = tile
    for cell in range(CELLS):
        high, low = split_rows(whole[pl.ds(cell, BROWS, stride=CELLS), :], BPAD)
        split[0:BPAD, cell * X : (cell + 1) * X] = high
        split[BPAD : 2 * BPAD, cell * X : (cell + 1) * X] = low


def split_rows(rows, padded):
    rows = jnp.concatenate([rows, jnp.zeros((padded - rows.shape[0], rows.shape[1]), F32)], axis=0)
    high = rows.astype(BF16)
    return high, (rows - high.astype(F32)).astype(BF16)


def product(left, right):
    return lax.dot_general(left, right, (((1,), (1,)), ((), ())), preferred_element_type=F32)


def join(both, padded):
    return both[:padded] + both[padded:]


def join_lanes(both, padded):
    return both[:, :padded] + both[:, padded:]


def load_history(history, here, done):
    copy = pltpu.make_async_copy(history, here, done)
    copy.start()
    copy.wait()


def pack_history(count, ends_count, history, split, packed):
    _, lane = iotas()
    for e, right in enumerate(ends_of(ends_count)):
        for h in range(count):
            tile = jnp.zeros((Y, X), F32)
            for z in range(Z):
                base = 16 * z + 4
                moved = turn(history[pl.ds(h * CELLS + z * Y, Y), :], right, base + 4, base)
                tile = jnp.where((lane >= base) & (lane < base + 4), moved, tile)
            packed[pl.ds(h * Y, Y), :] = tile
        for y in range(Y):
            high, low = split_rows(packed[pl.ds(y, count, stride=Y), :], HPAD)
            at = (e * Y + y) * X
            split[0:HPAD, at : at + X] = high
            split[HPAD : 2 * HPAD, at : at + X] = low


def history_kernel(count, history, split, gram):
    for cell in range(CELLS):
        high, low = split_rows(history[pl.ds(cell, count, stride=CELLS), :], HPAD)
        split[0:HPAD, cell * X : (cell + 1) * X] = high
        split[HPAD : 2 * HPAD, cell * X : (cell + 1) * X] = low
    gram[...] = pack_gram(join_lanes(join(product(split[...], split[...]), HPAD), HPAD))


def split_matrix(matrix):
    high = matrix.astype(BF16)
    return high, (matrix - high.astype(F32)).astype(BF16)


def reciprocal(value):
    guess = pl.reciprocal(value, approx=True)
    guess = guess * (2.0 - value * guess)
    return guess * (2.0 - value * guess)


def finish(columns, cells, history_split, split, *refs):
    parts, (out, factor, staged, factor_staged, done, projected) = refs[:-6], refs[-6:]
    total = (parts[0][...] + parts[1][...]) * (1.0 / cells)
    upper, coef, basis_gram = unpack_sums(total)
    inner = jnp.dot(coef, upper, precision=HIGHEST, preferred_element_type=F32)
    inner = inner + lax.dot_general(
        coef, upper, (((1,), (1,)), ((), ())), precision=HIGHEST, preferred_element_type=F32
    )
    inner = inner - 2.0 * coef
    inner = jnp.concatenate([inner, jnp.zeros((BPAD - BROWS, HPAD), F32)], axis=0)
    gram = basis_gram + lax.dot_general(
        coef, inner, (((1,), (1,)), ((), ())), precision=HIGHEST, preferred_element_type=F32
    )
    coef_high, coef_low = split_matrix(-jnp.concatenate([coef, jnp.zeros((BPAD - BROWS, HPAD), F32)], axis=0))
    one = jnp.where(
        lax.broadcasted_iota(jnp.int32, (BPAD, BPAD), 0) == lax.broadcasted_iota(jnp.int32, (BPAD, BPAD), 1), 1.0, 0.0
    ).astype(BF16)
    basis_minus = jnp.concatenate(
        [
            jnp.concatenate([coef_high, coef_high, one, one], axis=1),
            jnp.concatenate([coef_low, jnp.zeros((BPAD, HPAD + 2 * BPAD), BF16)], axis=1),
        ],
        axis=0,
    )
    width = WIDTH * X
    for c in range(CELLS * X // width):
        at = slice(c * width, (c + 1) * width)
        right = jnp.concatenate([history_split[:, at], split[:, at]], axis=0)
        high, low = split_matrix(join(jnp.dot(basis_minus, right, preferred_element_type=F32), BPAD))
        projected[0:BPAD, at] = high
        projected[BPAD:, at] = low
    row = lax.broadcasted_iota(jnp.int32, (BROWS, X), 0)
    lane = lax.broadcasted_iota(jnp.int32, (BROWS, X), 1)
    work = jnp.concatenate([gram, jnp.zeros((BROWS, X - BPAD), F32)], axis=1)
    work = jnp.where(lane == row + BPAD, 1.0, work)
    panel = columns
    for start in range(0, columns, panel):
        spread = [
            jnp.broadcast_to(work[:, k : k + 1], (BROWS, X)) for k in range(start, start + panel)
        ]
        for j in range(panel):
            k = start + j
            scale = spread[j] * reciprocal(spread[j][k : k + 1, :])
            scale = jnp.where(row > k, scale, 0.0)
            for later in range(j + 1, panel):
                spread[later] = spread[later] - scale * spread[later][k : k + 1, :]
            work = work - scale * work[k : k + 1, :]
    pivots = jnp.sum(jnp.where(lane == row, work, 0.0), axis=1, keepdims=True)
    good = lax.broadcasted_iota(jnp.int32, (BROWS, 1), 0) < columns
    work = work * jnp.where(good, 1.0 / jnp.sqrt(jnp.where(good, pivots, 1.0)), 0.0)
    factor_staged[...] = jnp.where(lane >= row, work, 0.0)[0:columns, 0:columns]
    copies = [pltpu.make_async_copy(factor_staged, factor, done.at[0])]
    copies[0].start()
    work = jnp.concatenate([work, jnp.zeros((BPAD - BROWS, X), F32)], axis=0)
    basis_high, basis_low = split_matrix(work[:, BPAD : 2 * BPAD])
    left = jnp.concatenate([basis_high, basis_high, basis_low], axis=1)
    width = WIDTH * X
    inside = width // X
    blocks = staged.reshape(BROWS, CELLS, X)
    for c in range(CELLS // inside):
        right = projected[:, c * width : (c + 1) * width]
        right = jnp.concatenate([right, right[:BPAD]], axis=0)
        result = jnp.dot(left, right, preferred_element_type=F32)
        for j in range(inside):
            staged[pl.ds(c * inside + j, columns, stride=CELLS), :] = result[
                0:columns, j * X : (j + 1) * X
            ]
        cells_done = (c + 1) * inside
        if cells_done % PIECE == 0:
            piece = pl.ds(cells_done - PIECE, PIECE)
            copies.append(
                pltpu.make_async_copy(
                    blocks.at[pl.ds(0, columns), piece, :], out.at[:, piece, :], done.at[len(copies)]
                )
            )
            copies[-1].start()
    for copy in copies:
        copy.wait()


def call(
    kernel,
    outs,
    flops,
    bytes_accessed,
    scratch=(),
    limit=40 * 1024 * 1024,
    place=jax.ShapeDtypeStruct,
    **specs,
):
    return pl.pallas_call(
        kernel,
        **specs,
        out_shape=[place(shape, dtype) for shape, dtype in outs],
        scratch_shapes=list(scratch),
        compiler_params=pltpu.CompilerParams(vmem_limit_bytes=limit),
        cost_estimate=pl.CostEstimate(flops=flops, bytes_accessed=bytes_accessed, transcendentals=0),
    )


def sum_over_devices(array, sizes):
    devices = range(sizes[0] * sizes[1] * sizes[2])
    bits = []
    for axis, stride in ((2, 1), (0, sizes[1] * sizes[2]), (1, sizes[2])):
        bits += [stride << b for b in range(sizes[axis].bit_length() - 1)]
    others = None
    for bit in bits:
        array = array if others is None else array + others
        others = lax.ppermute(array, AXES, [(i, i ^ (bit | 1)) for i in devices])
    return [array, others]


def on_device(sizes, history, start, diagonal):
    fields, history_count = start.shape[0], history.shape[0]
    columns = fields * (STEPS + 1)
    all_fields = fields + 1
    count = dict(zip(AXES, sizes))
    ways = {axis: 1 if size == 2 else 2 for axis, size in count.items()}
    cells = Z * Y * X * sizes[0] * sizes[1] * sizes[2]
    tile = Y * X * 4

    ends = 1 if count["gx"] == 2 else 2
    there = pl.BlockSpec(memory_space=pltpu.HBM)
    anywhere = pl.BlockSpec(memory_space=pl.ANY)
    here = pl.BlockSpec(memory_space=pltpu.VMEM)

    with jax.named_scope("halo_y"):
        start, diagonal, *sends = call(
            functools.partial(pack_y, fields),
            [(start.shape, F32), (diagonal.shape, F32)]
            + [((4 * all_fields, Y, X), F32)] * ways["gy"],
            1000,
            start.size * 4,
            [pltpu.SemaphoreType.DMA((all_fields,))],
            None,
            pltpu.VMEM,
            in_specs=[there, there],
        )(start, diagonal)
        received = swaps(sends, sizes, "gy")
    with jax.named_scope("load_history"):
        rows = call(
            load_history,
            [(history.shape, F32)],
            1000,
            history.size * 4,
            [pltpu.SemaphoreType.DMA],
            None,
            pltpu.VMEM,
            in_specs=[there],
        )(history)[0].reshape(history_count * CELLS, X)
    with jax.named_scope("history_at_ends"):
        history_ends = call(
            functools.partial(pack_history, history_count, count["gx"]),
            [((2 * HPAD, ends * Y * X), BF16)],
            1000,
            history.size * 2,
            [pltpu.VMEM((history_count * Y, X), F32)],
        )(rows)[0]
    with jax.named_scope("halo_z"):
        beyond, *sends = call(
            functools.partial(pack_z, fields, count["gy"], ways["gy"]),
            [((all_fields, Z, Y, X), F32)] + [((z_tiles(fields), Y, X), F32)] * ways["gz"],
            1000,
            start.size * 4,
            in_specs=[here, here, anywhere] + [here] * ways["gy"],
        )(start, diagonal, history_ends, *received)
        received = swaps(sends, sizes, "gz")
    with jax.named_scope("history_products"):
        history_split, history_gram = call(
            functools.partial(history_kernel, history_count),
            [((2 * HPAD, CELLS * X), BF16), ((2 * Y, X), F32)],
            2 * 128 * 128 * CELLS * X,
            history.size * 4,
        )(rows)
    with jax.named_scope("halo_x"):
        x_shapes = [((x_tiles(fields), Y, X), F32)] * ways["gx"]
        owns = call(functools.partial(pack_x_own, fields), x_shapes, 1000, start.size * 4)(
            start, diagonal, beyond
        )
        wide, *sends = call(
            functools.partial(pack_x, fields, count["gz"], ways["gz"], ways["gx"]),
            [((all_fields, SLOTS - Z, 2, Y, X), F32)] + x_shapes,
            1000,
            start.size * 4,
            in_specs=[here] * ways["gx"] + [anywhere] + [here] * ways["gz"],
        )(*owns, history_gram, *received)
        received = swaps(sends, sizes, "gx")
    with jax.named_scope("matrix_powers"):
        center, own, sums = call(
            functools.partial(powers, fields, count["gx"]),
            [
                ((BROWS * CELLS, X), F32),
                ((ends, all_fields, 2, 2, Y, X), F32),
                ((BROWS, X), F32),
            ],
            2 * 192 * 64 * CELLS * X,
            start.size * 4,
            [
                pltpu.VMEM((STEPS - 1, fields, SLOTS, 2, Y, X), F32),
                pltpu.VMEM((SLOTS, 2, Y, X), F32),
                pltpu.VMEM((SLOTS, 2, Y, X), F32),
                pltpu.VMEM((2 * BPAD, CELLS * X), BF16),
            ],
        )(start, diagonal, beyond, wide, history_split)
    with jax.named_scope("powers_at_ends"):
        sums, patch = call(
            functools.partial(powers_at_ends, fields, count["gx"], ways["gx"]),
            [((4 * Y, X), F32), ((ends, BROWS * Y, X), F32)],
            1000000,
            start.size * 4,
            [
                pltpu.VMEM((STEPS + 1, fields, 2, 2, Y, X), F32),
                pltpu.VMEM((2 * BPAD, ends * Y * X), BF16),
            ],
        )(own, history_ends, sums, history_gram, *received)
    with jax.named_scope("whole_basis"):
        split = call(
            functools.partial(patch_and_split, fields, count["gx"]),
            [((2 * BPAD, CELLS * X), BF16)],
            1000,
            columns * CELLS * X * 4,
            [pltpu.VMEM((BROWS * CELLS, X), F32)],
        )(center, patch)[0]
    with jax.named_scope("sum_over_devices"):
        parts = sum_over_devices(sums, sizes)
    with jax.named_scope("orthonormalize"):
        out, factor = call(
            functools.partial(finish, columns, cells),
            [((columns, CELLS, X), F32), ((columns, columns), F32)],
            2 * 192 * 64 * CELLS * X,
            columns * CELLS * X * 4,
            [
                pltpu.VMEM((BROWS * CELLS, X), F32),
                pltpu.VMEM((columns, columns), F32),
                pltpu.SemaphoreType.DMA((CELLS // PIECE + 1,)),
                pltpu.VMEM((2 * BPAD, CELLS * X), BF16),
            ],
            out_specs=[pl.BlockSpec(memory_space=pltpu.HBM)] * 2,
        )(history_split, split, *parts)
    return out.reshape(columns, Z, Y, X), factor


def solution(mesh):
    sizes = tuple(mesh.shape[axis] for axis in AXES)
    return jax.shard_map(
        functools.partial(on_device, sizes),
        mesh=mesh,
        in_specs=(P(None, "gz", "gy", "gx"), P(None, "gz", "gy", "gx"), P("gz", "gy", "gx")),
        out_specs=(P(None, "gz", "gy", "gx"), P()),
        check_vma=False,
    )
```

```python
import functools
import itertools

import jax
import jax.numpy as jnp
from jax import lax
from jax.experimental import pallas as pl
from jax.experimental.pallas import tpu as pltpu
from jax.sharding import PartitionSpec as P

STEPS = 4
F32 = jnp.float32
BF16 = jnp.bfloat16
AXES = ("gx", "gy", "gz")
HIGHEST = lax.Precision.HIGHEST
Z, Y, X = 8, 8, 128
CELLS = Z * Y
PIECE = 16
WIDTH = 8
SLOTS = 16
BPAD = 32
BROWS = 24
HPAD = 64
ROWS = 56


def roll(tile, shift, axis):
    shift %= tile.shape[axis]
    return pltpu.roll(tile, shift, axis) if shift else tile


def iotas():
    return (
        lax.broadcasted_iota(jnp.int32, (Y, X), 0),
        lax.broadcasted_iota(jnp.int32, (Y, X), 1),
    )


def is_even(axis):
    return lax.rem(lax.axis_index(axis), 2) == 0


def facing(axis, count, received):
    index = lax.axis_index(axis)
    even = lax.rem(index, 2) == 0
    low_there, high_there = index > 0, index < count - 1

    def pick(k):
        first = received[0][k]
        if len(received) == 1:
            return jnp.where(even, 0.0, first), jnp.where(even, first, 0.0)
        second = received[1][k]
        low = jnp.where(low_there, jnp.where(even, second, first), 0.0)
        high = jnp.where(high_there, jnp.where(even, first, second), 0.0)
        return low, high

    return pick


def swaps(arrays, sizes, axis):
    first, second = [], []
    dimension = AXES.index(axis)
    aside = 0 if dimension == 2 else 2
    for place in itertools.product(*map(range, sizes)):
        at = place[dimension]

        def pair(dimension, to):
            other = place[:dimension] + (to,) + place[dimension + 1 :]
            return tuple(
                (p[0] * sizes[1] + p[1]) * sizes[2] + p[2] for p in (place, other)
            )

        first.append(pair(dimension, at ^ 1))
        beyond = at + 1 if at % 2 else at - 1
        if 0 <= beyond < sizes[dimension]:
            second.append(pair(dimension, beyond))
        else:
            second.append(pair(aside, place[aside] ^ 1))
    return [lax.ppermute(a, AXES, pairs) for a, pairs in zip(arrays, (first, second))]


def choose(right, there, here):
    return (there if right else here) if isinstance(right, bool) else jnp.where(right, there, here)


def turn(tile, right, there, here):
    if isinstance(right, bool):
        return roll(tile, there if right else here, 1)
    return pltpu.roll(tile, jnp.where(right, there % X, here % X), 1)


def ends_of(count):
    return [is_even("gx")] if count == 2 else [False, True]


def pack_y(fields, start_there, diagonal_there, start, diagonal, *refs):
    sends, done = refs[:-1], refs[-1]
    copies = [
        pltpu.make_async_copy(start_there.at[f], start.at[f], done.at[f]) for f in range(fields)
    ]
    copies.append(pltpu.make_async_copy(diagonal_there, diagonal, done.at[fields]))
    for copy in copies:
        copy.start()
    row, _ = iotas()
    even = is_even("gy")
    for f in range(fields + 1):
        copies[f].wait()
        for p in range(4):
            one, two = (start[f, z] if f < fields else diagonal[z] for z in (p, p + 4))
            to_high = jnp.where(row < 4, roll(one, 4, 0), two)
            to_low = jnp.where(row < 4, one, roll(two, 4, 0))
            sends[0][4 * f + p] = jnp.where(even, to_high, to_low)
            if len(sends) > 1:
                sends[1][4 * f + p] = jnp.where(even, to_low, to_high)


def pack_z(fields, count, ways, start, diagonal, _, *refs):
    received, (beyond, *sends) = refs[:ways], refs[ways:]
    row, _ = iotas()
    pick = facing("gy", count, received)
    even = is_even("gz")
    for f in range(fields + 1):
        for p in range(4):
            low, high = pick(4 * f + p)
            beyond[f, p] = jnp.where(row < 4, high, roll(low, 4, 0))
            beyond[f, p + 4] = jnp.where(row < 4, roll(high, 4, 0), low)
    inner = (row == 2) | (row == 3)
    for which, ref in enumerate(sends):
        up = even if which == 0 else jnp.logical_not(even)
        at = [None] + [jnp.where(up, Z - d, d - 1) for d in range(1, 5)]
        k = 0
        for f in range(fields):
            for d in range(1, 5):
                ref[k] = start[f, at[d]]
                k += 1
            far = beyond[f, at[3]]
            ref[k] = jnp.where(
                row == 3, roll(far, 3, 0), jnp.where(row == 4, roll(far, -3, 0), beyond[f, at[1]])
            )
            k += 1
        for f in range(0, fields, 2):
            shared = roll(beyond[min(f + 1, fields - 1), at[2]], 4, 0)
            ref[k] = jnp.where((row >= 2) & (row < 6), shared, beyond[f, at[2]])
            k += 1
        for d in range(1, 4):
            ref[k] = diagonal[at[d]]
            k += 1
        ref[k] = jnp.where(inner, roll(beyond[fields, at[2]], 3, 0), beyond[fields, at[1]])


def z_tiles(fields):
    return 5 * fields + (fields + 1) // 2 + 4


def known(fields, f):
    depth = 4 if f < fields else 3
    for at in range(-depth, Z + depth):
        distance = max(-at, at - Z + 1, 0)
        for part in range(2 if distance < depth else 1):
            yield at % SLOTS, part


def end_columns(fields, up, tile_of, halo):
    _, lane = iotas()
    tiles = [jnp.zeros((Y, X), F32)] * x_tiles(fields)
    for f in range(fields + 1):
        for z, part in known(fields, f):
            if (z >= Z) != halo:
                continue
            index, column = divmod(2 * f + part, 4)
            base = 16 * (z % 8) + 4 * column
            moved = turn(tile_of(f, z, part), up, base + 4, base)
            k = 2 * index + z // 8
            tiles[k] = jnp.where((lane >= base) & (lane < base + 4), moved, tiles[k])
    return tiles


def pack_x_own(fields, start, diagonal, beyond, *sends):
    def tile_of(f, z, part):
        if part:
            return beyond[f, z]
        return start[f, z] if f < fields else diagonal[z]

    even = is_even("gx")
    for which, ref in enumerate(sends):
        tiles = end_columns(fields, even if which == 0 else jnp.logical_not(even), tile_of, False)
        for k, tile in enumerate(tiles):
            ref[k] = tile


def pack_x(fields, count, ways, x_ways, *refs):
    owns, refs = refs[:x_ways], refs[x_ways + 1 :]
    received, (wide, *sends) = refs[:ways], refs[ways:]
    row, _ = iotas()
    pick = facing("gz", count, received)
    even = is_even("gx")
    found = {}
    k = 0
    for f in range(fields + 1):
        depth = 4 if f < fields else 3
        for d in range(1, depth + 1):
            found[f, SLOTS - d, 0], found[f, Z - 1 + d, 0] = pick(k)
            k += 1
        if f < fields:
            for z, far_z, tile in zip((SLOTS - 1, Z), (SLOTS - 3, Z + 2), pick(k)):
                found[f, z, 1] = tile
                found[f, far_z, 1] = jnp.where(row < 4, roll(tile, -3, 0), roll(tile, 3, 0))
            k += 1
            if f == fields - 1:
                for g in range(fields):
                    shared = pick(k + g // 2)
                    found[g, SLOTS - 2, 1], found[g, Z + 1, 1] = (roll(t, 4 * (g % 2), 0) for t in shared)
                k += (fields + 1) // 2
        else:
            low, high = pick(k)
            k += 1
            found[f, SLOTS - 1, 1], found[f, Z, 1] = low, high
            found[f, SLOTS - 2, 1], found[f, Z + 1, 1] = roll(low, -3, 0), roll(high, -3, 0)
    for (f, z, part), tile in found.items():
        wide[f, z - Z, part] = tile
    for which, ref in enumerate(sends):
        up = even if which == 0 else jnp.logical_not(even)
        tiles = end_columns(fields, up, lambda f, z, part: found[f, z, part], True)
        for k, tile in enumerate(tiles):
            ref[k] = tile + owns[which][k]


def x_tiles(fields):
    return 2 * ((2 * (fields + 1) + 3) // 4)


def coefficients(d):
    inside = d > 0.0
    return jnp.where(inside, (d - 1.0) * (1.0 / 7.0), 0.0), jnp.where(inside, 1.0 / 7.0, 0.0)


def beside_y(mine, other):
    row, _ = iotas()
    above, above_other = roll(mine, -1, 0), roll(other, -1, 0)
    below, below_other = roll(mine, 1, 0), roll(other, 1, 0)
    last, first = row == Y - 1, row == 0
    return (
        jnp.where(last, above_other, above) + jnp.where(first, below_other, below),
        jnp.where(last, above, above_other) + jnp.where(first, below, below_other),
    )


def powers(fields, count, start, diagonal, beyond, wide, history_split, center, own, sums, *refs):
    halo, coef_a, coef_b, split = refs
    columns = fields * (STEPS + 1)
    _, lane = iotas()
    inside = set(range(Z))
    ends = ends_of(count)

    def given(f, z, part):
        if z >= Z:
            return wide[f, z - Z, part]
        if part:
            return beyond[f, z]
        return start[f, z] if f < fields else diagonal[z]

    for z, part in known(fields, fields):
        if part == 0 and z in inside:
            coef_a[z, 0] = (diagonal[z] - 1.0) * (1.0 / 7.0)
        else:
            coef_a[z, part], coef_b[z, part] = coefficients(given(fields, z, part))

    def read(level, f, z, part):
        if level == 0:
            return given(f, z, part)
        if part == 0 and z in inside:
            return center[pl.ds((fields * level + f) * CELLS + z * Y, Y), :]
        return halo[level - 1, f, z, part]

    for f in range(fields):
        for z in range(Z):
            center[pl.ds(f * CELLS + z * Y, Y), :] = start[f, z]
    for level in range(1, STEPS + 1):
        reach = STEPS - level
        for f in range(fields):
            for at in range(-reach, Z + reach):
                z, before, after = at % SLOTS, (at - 1) % SLOTS, (at + 1) % SLOTS
                distance = max(-at, at - Z + 1, 0)
                tiles = [read(level - 1, f, z, p) for p in range(2)]
                along_y = beside_y(*tiles)
                for part in range(2 if distance < reach else 1):
                    tile = tiles[part]
                    total = jnp.where(lane == 0, 0.0, roll(tile, 1, 1))
                    total = total + jnp.where(lane == X - 1, 0.0, roll(tile, -1, 1))
                    total = total + along_y[part]
                    total = total + read(level - 1, f, before, part)
                    total = total + read(level - 1, f, after, part)
                    own_cells = part == 0 and z in inside
                    b = 1.0 / 7.0 if own_cells else coef_b[z, part]
                    value = coef_a[z, part] * tile - b * total
                    if level > 1:
                        value = value + value - read(level - 2, f, z, part)
                    if own_cells:
                        center[pl.ds((fields * level + f) * CELLS + z * Y, Y), :] = value
                    else:
                        halo[level - 1, f, z, part] = value
    center[pl.ds(columns * CELLS, (BROWS - columns) * CELLS), :] = jnp.zeros(
        ((BROWS - columns) * CELLS, X), F32
    )

    lanes = lax.broadcasted_iota(jnp.int32, (BROWS, X), 1)
    taken = [(lanes >= first) & (lanes < first + 4) for first in (choose(r, X - 4, 0) for r in ends)]
    for cell in range(CELLS):
        rows = center[pl.ds(cell, BROWS, stride=CELLS), :]
        for mask in taken:
            rows = jnp.where(mask, 0.0, rows)
        high, low = split_rows(rows, BPAD)
        split[0:BPAD, cell * X : (cell + 1) * X] = high
        split[BPAD : 2 * BPAD, cell * X : (cell + 1) * X] = low
    sums[...] = inner_products(split[...], history_split[...])

    for e, right in enumerate(ends):
        for f in range(fields + 1):
            tiles = [[jnp.zeros((Y, X), F32)] * 2 for _ in range(2)]
            for z, part in known(fields, f):
                base = 16 * (z % 8)
                first = choose(right, base, base + 4)
                moved = turn(given(f, z, part), right, base + 8, base + 4)
                tiles[part][z // 8] = jnp.where(
                    (lane >= first) & (lane < first + 8), moved, tiles[part][z // 8]
                )
            for part in range(2):
                for t in range(2):
                    own[e, f, part, t] = tiles[part][t]


def inner_products(split, history_split):
    basis = join_lanes(join(product(split, split), BPAD), BPAD)
    cross = join_lanes(join(product(split, history_split), BPAD), HPAD)
    both = jnp.concatenate([cross, basis, jnp.zeros((BPAD, X - HPAD - BPAD), F32)], axis=1)
    return both[:BROWS]


def powers_at_ends(fields, count, ways, own, history_ends, before, history_gram, *refs):
    received, (sums, patch, work, split) = refs[:ways], refs[ways:]
    columns = fields * (STEPS + 1)
    _, lane = iotas()
    column = lane & 15
    pick = facing("gx", count, received) if count > 2 else None
    ends = ends_of(count)
    taken = (column >= 4) & (column < 8)

    for e, right in enumerate(ends):

        def halo_of(k):
            return received[0][k] if count == 2 else pick(k)[e]

        first = choose(right, 8, 0)
        from_halo = (column >= first) & (column < first + 4)
        coefs = {}
        for f in range(fields + 1):
            for part in range(2):
                index, c = divmod(2 * f + part, 4)
                for t in range(2):
                    moved = turn(halo_of(2 * index + t), right, 8 - 4 * c, -4 * c)
                    tile = jnp.where(from_halo, moved, own[e, f, part, t])
                    if f < fields:
                        work[0, f, part, t] = tile
                    else:
                        coefs[part, t] = coefficients(tile)
        for level in range(1, STEPS + 1):
            for f in range(fields):
                tiles = [[work[level - 1, f, p, t] for t in range(2)] for p in range(2)]
                along_y = [beside_y(tiles[0][t], tiles[1][t]) for t in range(2)]
                for part, t in ((0, 0), (0, 1), (1, 0), (1, 1)):
                    if (level == STEPS and (part or t)) or (level == STEPS - 1 and part and t):
                        continue
                    tile = tiles[part][t]
                    nexts = [roll(tiles[part][i], -16, 1) for i in (t, 1 - t)]
                    lasts = [roll(tiles[part][i], 16, 1) for i in (t, 1 - t)]
                    total = roll(tile, 1, 1) + roll(tile, -1, 1) + along_y[t][part]
                    total = total + jnp.where(lane >= X - 16, nexts[1], nexts[0])
                    total = total + jnp.where(lane < 16, lasts[1], lasts[0])
                    a, b = coefs[part, t]
                    value = a * tile - b * total
                    if level > 1:
                        value = value + value - work[level - 2, f, part, t]
                    work[level, f, part, t] = value
        for level in range(STEPS + 1):
            for f in range(fields):
                k = fields * level + f
                patch[e, k * Y : (k + 1) * Y, :] = jnp.where(taken, work[level, f, 0, 0], 0.0)
        patch[e, columns * Y :, :] = jnp.zeros(((BROWS - columns) * Y, X), F32)
        for y in range(Y):
            high, low = split_rows(patch[e, pl.ds(y, BROWS, stride=Y), :], BPAD)
            at = (e * Y + y) * X
            split[0:BPAD, at : at + X] = high
            split[BPAD : 2 * BPAD, at : at + X] = low
    both = before[...] + inner_products(split[...], history_ends[...])
    first, second, third = (both[k : k + Y] for k in range(0, BROWS, Y))
    sums[0:8] = history_gram[0:8]
    sums[8:16] = jnp.where(lane < 96, history_gram[8:16], roll(first, 32, 1))
    sums[16:24] = jnp.where(lane < ROWS, first, roll(second, ROWS, 1))
    sums[24:32] = jnp.where(
        lane < ROWS, third, jnp.where(lane < 80, roll(second, -8, 1), roll(third, 16, 1))
    )


PACKED = ((0, 0), (0, 56), (1, 0), (1, 40), (0, 104), (1, 72), (1, 88))


def pack_gram(gram):
    _, lane = iotas()
    gram = jnp.concatenate([gram, jnp.zeros((HPAD, X - HPAD), F32)], axis=1)
    tiles = [jnp.zeros((Y, X), F32)] * 2
    for i, (t, first) in enumerate(PACKED):
        inside = (lane >= first) & (lane < first + ROWS - 8 * i)
        tiles[t] = jnp.where(inside, roll(gram[8 * i : 8 * i + 8], first - 8 * i, 1), tiles[t])
    return jnp.concatenate(tiles, axis=0)


def unpack_sums(total):
    _, lane = iotas()
    tiles = [total[8 * k : 8 * k + 8] for k in range(4)]
    rows = []
    for i, (t, first) in enumerate(PACKED):
        row = jnp.where((lane >= 8 * i) & (lane < ROWS), roll(tiles[t], 8 * i - first, 1), 0.0)
        rows.append(jnp.where(lane < 8 * i + 8, 0.5 * row, row))
    rows.append(jnp.zeros((Y, X), F32))
    upper = jnp.concatenate(rows, axis=0)[:, :HPAD]
    coef = [tiles[2], roll(tiles[2], -ROWS, 1), tiles[3]]
    coef = jnp.concatenate([jnp.where(lane < ROWS, c, 0.0) for c in coef], axis=0)[:, :HPAD]
    basis = [roll(tiles[1], -96, 1), roll(tiles[3], -ROWS, 1), roll(tiles[3], -80, 1)]
    basis = jnp.concatenate([jnp.where(lane < BROWS, b, 0.0) for b in basis], axis=0)[:, :BPAD]
    return upper, coef, basis


def patch_and_split(fields, count, center, patch, split, whole):
    _, lane = iotas()
    for k in range(BROWS):
        for z in range(Z):
            tile = center[pl.ds(k * CELLS + z * Y, Y), :]
            if fields <= k < fields * (STEPS + 1):
                for e, right in enumerate(ends_of(count)):
                    base = 16 * z + 4
                    moved = turn(patch[e, k * Y : (k + 1) * Y, :], right, X - 4 - base, -base)
                    first = choose(right, X - 4, 0)
                    tile = jnp.where((lane >= first) & (lane < first + 4), moved, tile)
            whole[pl.ds(k * CELLS + z * Y, Y), :] = tile
    for cell in range(CELLS):
        high, low = split_rows(whole[pl.ds(cell, BROWS, stride=CELLS), :], BPAD)
        split[0:BPAD, cell * X : (cell + 1) * X] = high
        split[BPAD : 2 * BPAD, cell * X : (cell + 1) * X] = low


def split_rows(rows, padded):
    rows = jnp.concatenate([rows, jnp.zeros((padded - rows.shape[0], rows.shape[1]), F32)], axis=0)
    high = rows.astype(BF16)
    return high, (rows - high.astype(F32)).astype(BF16)


def product(left, right):
    return lax.dot_general(left, right, (((1,), (1,)), ((), ())), preferred_element_type=F32)


def join(both, padded):
    return both[:padded] + both[padded:]


def join_lanes(both, padded):
    return both[:, :padded] + both[:, padded:]


def load_history(history, here, done):
    copy = pltpu.make_async_copy(history, here, done)
    copy.start()
    copy.wait()


def pack_history(count, ends_count, history, split, packed):
    _, lane = iotas()
    for e, right in enumerate(ends_of(ends_count)):
        for h in range(count):
            tile = jnp.zeros((Y, X), F32)
            for z in range(Z):
                base = 16 * z + 4
                moved = turn(history[pl.ds(h * CELLS + z * Y, Y), :], right, base + 4, base)
                tile = jnp.where((lane >= base) & (lane < base + 4), moved, tile)
            packed[pl.ds(h * Y, Y), :] = tile
        for y in range(Y):
            high, low = split_rows(packed[pl.ds(y, count, stride=Y), :], HPAD)
            at = (e * Y + y) * X
            split[0:HPAD, at : at + X] = high
            split[HPAD : 2 * HPAD, at : at + X] = low


def history_kernel(count, history, split, gram):
    for cell in range(CELLS):
        high, low = split_rows(history[pl.ds(cell, count, stride=CELLS), :], HPAD)
        split[0:HPAD, cell * X : (cell + 1) * X] = high
        split[HPAD : 2 * HPAD, cell * X : (cell + 1) * X] = low
    gram[...] = pack_gram(join_lanes(join(product(split[...], split[...]), HPAD), HPAD))


def split_matrix(matrix):
    high = matrix.astype(BF16)
    return high, (matrix - high.astype(F32)).astype(BF16)


def reciprocal(value):
    guess = pl.reciprocal(value, approx=True)
    guess = guess * (2.0 - value * guess)
    return guess * (2.0 - value * guess)


def finish(columns, cells, history_split, split, *refs):
    parts, (out, factor, staged, factor_staged, done, projected) = refs[:-6], refs[-6:]
    total = (parts[0][...] + parts[1][...]) * (1.0 / cells)
    upper, coef, basis_gram = unpack_sums(total)
    inner = jnp.dot(coef, upper, precision=HIGHEST, preferred_element_type=F32)
    inner = inner + lax.dot_general(
        coef, upper, (((1,), (1,)), ((), ())), precision=HIGHEST, preferred_element_type=F32
    )
    inner = inner - 2.0 * coef
    inner = jnp.concatenate([inner, jnp.zeros((BPAD - BROWS, HPAD), F32)], axis=0)
    gram = basis_gram + lax.dot_general(
        coef, inner, (((1,), (1,)), ((), ())), precision=HIGHEST, preferred_element_type=F32
    )
    coef_high, coef_low = split_matrix(-jnp.concatenate([coef, jnp.zeros((BPAD - BROWS, HPAD), F32)], axis=0))
    one = jnp.where(
        lax.broadcasted_iota(jnp.int32, (BPAD, BPAD), 0) == lax.broadcasted_iota(jnp.int32, (BPAD, BPAD), 1), 1.0, 0.0
    ).astype(BF16)
    basis_minus = jnp.concatenate(
        [
            jnp.concatenate([coef_high, coef_high, one, one], axis=1),
            jnp.concatenate([coef_low, jnp.zeros((BPAD, HPAD + 2 * BPAD), BF16)], axis=1),
        ],
        axis=0,
    )
    width = WIDTH * X
    for c in range(CELLS * X // width):
        at = slice(c * width, (c + 1) * width)
        right = jnp.concatenate([history_split[:, at], split[:, at]], axis=0)
        high, low = split_matrix(join(jnp.dot(basis_minus, right, preferred_element_type=F32), BPAD))
        projected[0:BPAD, at] = high
        projected[BPAD:, at] = low
    row = lax.broadcasted_iota(jnp.int32, (BROWS, X), 0)
    lane = lax.broadcasted_iota(jnp.int32, (BROWS, X), 1)
    work = jnp.concatenate([gram, jnp.zeros((BROWS, X - BPAD), F32)], axis=1)
    work = jnp.where(lane == row + BPAD, 1.0, work)
    panel = columns
    for start in range(0, columns, panel):
        spread = [
            jnp.broadcast_to(work[:, k : k + 1], (BROWS, X)) for k in range(start, start + panel)
        ]
        for j in range(panel):
            k = start + j
            scale = spread[j] * reciprocal(spread[j][k : k + 1, :])
            scale = jnp.where(row > k, scale, 0.0)
            for later in range(j + 1, panel):
                spread[later] = spread[later] - scale * spread[later][k : k + 1, :]
            work = work - scale * work[k : k + 1, :]
    pivots = jnp.sum(jnp.where(lane == row, work, 0.0), axis=1, keepdims=True)
    good = lax.broadcasted_iota(jnp.int32, (BROWS, 1), 0) < columns
    work = work * jnp.where(good, 1.0 / jnp.sqrt(jnp.where(good, pivots, 1.0)), 0.0)
    factor_staged[...] = jnp.where(lane >= row, work, 0.0)[0:columns, 0:columns]
    copies = [pltpu.make_async_copy(factor_staged, factor, done.at[0])]
    copies[0].start()
    work = jnp.concatenate([work, jnp.zeros((BPAD - BROWS, X), F32)], axis=0)
    basis_high, basis_low = split_matrix(work[:, BPAD : 2 * BPAD])
    left = jnp.concatenate([basis_high, basis_high, basis_low], axis=1)
    width = WIDTH * X
    inside = width // X
    blocks = staged.reshape(BROWS, CELLS, X)
    for c in range(CELLS // inside):
        right = projected[:, c * width : (c + 1) * width]
        right = jnp.concatenate([right, right[:BPAD]], axis=0)
        result = jnp.dot(left, right, preferred_element_type=F32)
        for j in range(inside):
            staged[pl.ds(c * inside + j, columns, stride=CELLS), :] = result[
                0:columns, j * X : (j + 1) * X
            ]
        cells_done = (c + 1) * inside
        if cells_done % PIECE == 0:
            piece = pl.ds(cells_done - PIECE, PIECE)
            copies.append(
                pltpu.make_async_copy(
                    blocks.at[pl.ds(0, columns), piece, :], out.at[:, piece, :], done.at[len(copies)]
                )
            )
            copies[-1].start()
    for copy in copies:
        copy.wait()


def call(
    kernel,
    outs,
    flops,
    bytes_accessed,
    scratch=(),
    limit=40 * 1024 * 1024,
    place=jax.ShapeDtypeStruct,
    **specs,
):
    return pl.pallas_call(
        kernel,
        **specs,
        out_shape=[place(shape, dtype) for shape, dtype in outs],
        scratch_shapes=list(scratch),
        compiler_params=pltpu.CompilerParams(vmem_limit_bytes=limit),
        cost_estimate=pl.CostEstimate(flops=flops, bytes_accessed=bytes_accessed, transcendentals=0),
    )


def sum_over_devices(array, sizes):
    devices = range(sizes[0] * sizes[1] * sizes[2])
    bits = []
    for axis, stride in ((2, 1), (0, sizes[1] * sizes[2]), (1, sizes[2])):
        bits += [stride << b for b in range(sizes[axis].bit_length() - 1)]
    others = None
    for bit in bits:
        array = array if others is None else array + others
        others = lax.ppermute(array, AXES, [(i, i ^ (bit | 1)) for i in devices])
    return [array, others]


def on_device(sizes, history, start, diagonal):
    fields, history_count = start.shape[0], history.shape[0]
    columns = fields * (STEPS + 1)
    all_fields = fields + 1
    count = dict(zip(AXES, sizes))
    ways = {axis: 1 if size == 2 else 2 for axis, size in count.items()}
    cells = Z * Y * X * sizes[0] * sizes[1] * sizes[2]
    tile = Y * X * 4

    ends = 1 if count["gx"] == 2 else 2
    there = pl.BlockSpec(memory_space=pltpu.HBM)
    anywhere = pl.BlockSpec(memory_space=pl.ANY)
    here = pl.BlockSpec(memory_space=pltpu.VMEM)

    with jax.named_scope("halo_y"):
        start, diagonal, *sends = call(
            functools.partial(pack_y, fields),
            [(start.shape, F32), (diagonal.shape, F32)]
            + [((4 * all_fields, Y, X), F32)] * ways["gy"],
            1000,
            start.size * 4,
            [pltpu.SemaphoreType.DMA((all_fields,))],
            None,
            pltpu.VMEM,
            in_specs=[there, there],
        )(start, diagonal)
        received = swaps(sends, sizes, "gy")
    with jax.named_scope("load_history"):
        rows = call(
            load_history,
            [(history.shape, F32)],
            1000,
            history.size * 4,
            [pltpu.SemaphoreType.DMA],
            None,
            pltpu.VMEM,
            in_specs=[there],
        )(history)[0].reshape(history_count * CELLS, X)
    with jax.named_scope("history_at_ends"):
        history_ends = call(
            functools.partial(pack_history, history_count, count["gx"]),
            [((2 * HPAD, ends * Y * X), BF16)],
            1000,
            history.size * 2,
            [pltpu.VMEM((history_count * Y, X), F32)],
        )(rows)[0]
    with jax.named_scope("halo_z"):
        beyond, *sends = call(
            functools.partial(pack_z, fields, count["gy"], ways["gy"]),
            [((all_fields, Z, Y, X), F32)] + [((z_tiles(fields), Y, X), F32)] * ways["gz"],
            1000,
            start.size * 4,
            in_specs=[here, here, anywhere] + [here] * ways["gy"],
        )(start, diagonal, history_ends, *received)
        received = swaps(sends, sizes, "gz")
    with jax.named_scope("history_products"):
        history_split, history_gram = call(
            functools.partial(history_kernel, history_count),
            [((2 * HPAD, CELLS * X), BF16), ((2 * Y, X), F32)],
            2 * 128 * 128 * CELLS * X,
            history.size * 4,
        )(rows)
    with jax.named_scope("halo_x"):
        x_shapes = [((x_tiles(fields), Y, X), F32)] * ways["gx"]
        owns = call(functools.partial(pack_x_own, fields), x_shapes, 1000, start.size * 4)(
            start, diagonal, beyond
        )
        wide, *sends = call(
            functools.partial(pack_x, fields, count["gz"], ways["gz"], ways["gx"]),
            [((all_fields, SLOTS - Z, 2, Y, X), F32)] + x_shapes,
            1000,
            start.size * 4,
            in_specs=[here] * ways["gx"] + [anywhere] + [here] * ways["gz"],
        )(*owns, history_gram, *received)
        received = swaps(sends, sizes, "gx")
    with jax.named_scope("matrix_powers"):
        center, own, sums = call(
            functools.partial(powers, fields, count["gx"]),
            [
                ((BROWS * CELLS, X), F32),
                ((ends, all_fields, 2, 2, Y, X), F32),
                ((BROWS, X), F32),
            ],
            2 * 192 * 64 * CELLS * X,
            start.size * 4,
            [
                pltpu.VMEM((STEPS - 1, fields, SLOTS, 2, Y, X), F32),
                pltpu.VMEM((SLOTS, 2, Y, X), F32),
                pltpu.VMEM((SLOTS, 2, Y, X), F32),
                pltpu.VMEM((2 * BPAD, CELLS * X), BF16),
            ],
        )(start, diagonal, beyond, wide, history_split)
    with jax.named_scope("powers_at_ends"):
        sums, patch = call(
            functools.partial(powers_at_ends, fields, count["gx"], ways["gx"]),
            [((4 * Y, X), F32), ((ends, BROWS * Y, X), F32)],
            1000000,
            start.size * 4,
            [
                pltpu.VMEM((STEPS + 1, fields, 2, 2, Y, X), F32),
                pltpu.VMEM((2 * BPAD, ends * Y * X), BF16),
            ],
        )(own, history_ends, sums, history_gram, *received)
    with jax.named_scope("whole_basis"):
        split = call(
            functools.partial(patch_and_split, fields, count["gx"]),
            [((2 * BPAD, CELLS * X), BF16)],
            1000,
            columns * CELLS * X * 4,
            [pltpu.VMEM((BROWS * CELLS, X), F32)],
        )(center, patch)[0]
    with jax.named_scope("sum_over_devices"):
        parts = sum_over_devices(sums, sizes)
    with jax.named_scope("orthonormalize"):
        out, factor = call(
            functools.partial(finish, columns, cells),
            [((columns, CELLS, X), F32), ((columns, columns), F32)],
            2 * 192 * 64 * CELLS * X,
            columns * CELLS * X * 4,
            [
                pltpu.VMEM((BROWS * CELLS, X), F32),
                pltpu.VMEM((columns, columns), F32),
                pltpu.SemaphoreType.DMA((CELLS // PIECE + 1,)),
                pltpu.VMEM((2 * BPAD, CELLS * X), BF16),
            ],
            out_specs=[pl.BlockSpec(memory_space=pltpu.HBM)] * 2,
        )(history_split, split, *parts)
    return out.reshape(columns, Z, Y, X), factor


def solution(mesh):
    sizes = tuple(mesh.shape[axis] for axis in AXES)
    return jax.shard_map(
        functools.partial(on_device, sizes),
        mesh=mesh,
        in_specs=(P(None, "gz", "gy", "gx"), P(None, "gz", "gy", "gx"), P("gz", "gy", "gx")),
        out_specs=(P(None, "gz", "gy", "gx"), P()),
        check_vma=False,
    )
```

```python
import functools
import itertools

import jax
import jax.numpy as jnp
from jax import lax
from jax.experimental import pallas as pl
from jax.experimental.pallas import tpu as pltpu
from jax.sharding import PartitionSpec as P

STEPS = 4
F32 = jnp.float32
BF16 = jnp.bfloat16
AXES = ("gx", "gy", "gz")
HIGHEST = lax.Precision.HIGHEST
Z, Y, X = 8, 8, 128
CELLS = Z * Y
PIECE = 16
WIDTH = 8
SLOTS = 16
BPAD = 32
BROWS = 24
HPAD = 64
ROWS = 56


def roll(tile, shift, axis):
    shift %= tile.shape[axis]
    return pltpu.roll(tile, shift, axis) if shift else tile


def iotas():
    return (
        lax.broadcasted_iota(jnp.int32, (Y, X), 0),
        lax.broadcasted_iota(jnp.int32, (Y, X), 1),
    )


def is_even(axis):
    return lax.rem(lax.axis_index(axis), 2) == 0


def facing(axis, count, received):
    index = lax.axis_index(axis)
    even = lax.rem(index, 2) == 0
    low_there, high_there = index > 0, index < count - 1

    def pick(k):
        first = received[0][k]
        if len(received) == 1:
            return jnp.where(even, 0.0, first), jnp.where(even, first, 0.0)
        second = received[1][k]
        low = jnp.where(low_there, jnp.where(even, second, first), 0.0)
        high = jnp.where(high_there, jnp.where(even, first, second), 0.0)
        return low, high

    return pick


def swaps(arrays, sizes, axis):
    first, second = [], []
    dimension = AXES.index(axis)
    aside = 0 if dimension == 2 else 2
    for place in itertools.product(*map(range, sizes)):
        at = place[dimension]

        def pair(dimension, to):
            other = place[:dimension] + (to,) + place[dimension + 1 :]
            return tuple(
                (p[0] * sizes[1] + p[1]) * sizes[2] + p[2] for p in (place, other)
            )

        first.append(pair(dimension, at ^ 1))
        beyond = at + 1 if at % 2 else at - 1
        if 0 <= beyond < sizes[dimension]:
            second.append(pair(dimension, beyond))
        else:
            second.append(pair(aside, place[aside] ^ 1))
    return [lax.ppermute(a, AXES, pairs) for a, pairs in zip(arrays, (first, second))]


def choose(right, there, here):
    return (there if right else here) if isinstance(right, bool) else jnp.where(right, there, here)


def turn(tile, right, there, here):
    if isinstance(right, bool):
        return roll(tile, there if right else here, 1)
    return pltpu.roll(tile, jnp.where(right, there % X, here % X), 1)


def ends_of(count):
    return [is_even("gx")] if count == 2 else [False, True]


def pack_y(fields, start_there, diagonal_there, start, diagonal, *refs):
    sends, done = refs[:-1], refs[-1]
    copies = [
        pltpu.make_async_copy(start_there.at[f], start.at[f], done.at[f]) for f in range(fields)
    ]
    copies.append(pltpu.make_async_copy(diagonal_there, diagonal, done.at[fields]))
    for copy in copies:
        copy.start()
    row, _ = iotas()
    even = is_even("gy")
    highs, lows = [], []
    for f in range(fields + 1):
        copies[f].wait()
        for p in range(4):
            one, two = (start[f, z] if f < fields else diagonal[z] for z in (p, p + 4))
            highs.append(jnp.where(row < 4, roll(one, 4, 0), two))
            lows.append(jnp.where(row < 4, one, roll(two, 4, 0)))
    last_high, last_low = highs.pop(), lows.pop()
    for p in range(3):
        k = 4 * fields + p
        highs[k] = jnp.where((row & 3) == 0, roll(last_high, -1 - p, 0), highs[k])
        lows[k] = jnp.where((row & 3) == 3, roll(last_low, 3 - p, 0), lows[k])
    for k, (to_high, to_low) in enumerate(zip(highs, lows)):
        sends[0][k] = jnp.where(even, to_high, to_low)
        if len(sends) > 1:
            sends[1][k] = jnp.where(even, to_low, to_high)


def pack_z(fields, count, ways, start, diagonal, _, *refs):
    received, (beyond, *sends) = refs[:ways], refs[ways:]
    row, _ = iotas()
    pick = facing("gy", count, received)
    even = is_even("gz")
    for f in range(fields + 1):
        for p in range(4):
            if f == fields and p == 3:
                low = high = jnp.zeros((Y, X), F32)
                for q, (from_low, from_high) in enumerate(pick(4 * f + i) for i in range(3)):
                    low = jnp.where((row & 3) == q + 1, roll(from_low, q + 1, 0), low)
                    high = jnp.where((row & 3) == q, roll(from_high, q - 3, 0), high)
            else:
                low, high = pick(4 * f + p)
            beyond[f, p] = jnp.where(row < 4, high, roll(low, 4, 0))
            beyond[f, p + 4] = jnp.where(row < 4, roll(high, 4, 0), low)
    inner = (row == 2) | (row == 3)
    for which, ref in enumerate(sends):
        up = even if which == 0 else jnp.logical_not(even)
        at = [None] + [jnp.where(up, Z - d, d - 1) for d in range(1, 5)]
        k = 0
        for f in range(fields):
            for d in range(1, 5):
                ref[k] = start[f, at[d]]
                k += 1
            far = beyond[f, at[3]]
            ref[k] = jnp.where(
                row == 3, roll(far, 3, 0), jnp.where(row == 4, roll(far, -3, 0), beyond[f, at[1]])
            )
            k += 1
        for f in range(0, fields, 2):
            shared = roll(beyond[min(f + 1, fields - 1), at[2]], 4, 0)
            ref[k] = jnp.where((row >= 2) & (row < 6), shared, beyond[f, at[2]])
            k += 1
        for d in range(1, 4):
            ref[k] = diagonal[at[d]]
            k += 1
        ref[k] = jnp.where(inner, roll(beyond[fields, at[2]], 3, 0), beyond[fields, at[1]])


def z_tiles(fields):
    return 5 * fields + (fields + 1) // 2 + 4


def known(fields, f):
    depth = 4 if f < fields else 3
    for at in range(-depth, Z + depth):
        distance = max(-at, at - Z + 1, 0)
        for part in range(2 if distance < depth else 1):
            yield at % SLOTS, part


def end_columns(fields, up, tile_of, halo):
    _, lane = iotas()
    tiles = [jnp.zeros((Y, X), F32)] * x_tiles(fields)
    for f in range(fields + 1):
        for z, part in known(fields, f):
            if (z >= Z) != halo:
                continue
            index, column = divmod(2 * f + part, 4)
            base = 16 * (z % 8) + 4 * column
            moved = turn(tile_of(f, z, part), up, base + 4, base)
            k = 2 * index + z // 8
            tiles[k] = jnp.where((lane >= base) & (lane < base + 4), moved, tiles[k])
    return tiles


def pack_x_own(fields, start, diagonal, beyond, *sends):
    def tile_of(f, z, part):
        if part:
            return beyond[f, z]
        return start[f, z] if f < fields else diagonal[z]

    even = is_even("gx")
    for which, ref in enumerate(sends):
        tiles = end_columns(fields, even if which == 0 else jnp.logical_not(even), tile_of, False)
        for k, tile in enumerate(tiles):
            ref[k] = tile


def pack_x(fields, count, ways, x_ways, *refs):
    owns, refs = refs[:x_ways], refs[x_ways + 1 :]
    received, (wide, *sends) = refs[:ways], refs[ways:]
    row, _ = iotas()
    pick = facing("gz", count, received)
    even = is_even("gx")
    found = {}
    k = 0
    for f in range(fields + 1):
        depth = 4 if f < fields else 3
        for d in range(1, depth + 1):
            found[f, SLOTS - d, 0], found[f, Z - 1 + d, 0] = pick(k)
            k += 1
        if f < fields:
            for z, far_z, tile in zip((SLOTS - 1, Z), (SLOTS - 3, Z + 2), pick(k)):
                found[f, z, 1] = tile
                found[f, far_z, 1] = jnp.where(row < 4, roll(tile, -3, 0), roll(tile, 3, 0))
            k += 1
            if f == fields - 1:
                for g in range(fields):
                    shared = pick(k + g // 2)
                    found[g, SLOTS - 2, 1], found[g, Z + 1, 1] = (roll(t, 4 * (g % 2), 0) for t in shared)
                k += (fields + 1) // 2
        else:
            low, high = pick(k)
            k += 1
            found[f, SLOTS - 1, 1], found[f, Z, 1] = low, high
            found[f, SLOTS - 2, 1], found[f, Z + 1, 1] = roll(low, -3, 0), roll(high, -3, 0)
    for (f, z, part), tile in found.items():
        wide[f, z - Z, part] = tile
    for which, ref in enumerate(sends):
        up = even if which == 0 else jnp.logical_not(even)
        tiles = end_columns(fields, up, lambda f, z, part: found[f, z, part], True)
        for k, tile in enumerate(tiles):
            ref[k] = tile + owns[which][k]


def x_tiles(fields):
    return 2 * ((2 * (fields + 1) + 3) // 4)


def coefficients(d):
    inside = d > 0.0
    return jnp.where(inside, (d - 1.0) * (1.0 / 7.0), 0.0), jnp.where(inside, 1.0 / 7.0, 0.0)


def beside_y(mine, other):
    row, _ = iotas()
    above, above_other = roll(mine, -1, 0), roll(other, -1, 0)
    below, below_other = roll(mine, 1, 0), roll(other, 1, 0)
    last, first = row == Y - 1, row == 0
    return (
        jnp.where(last, above_other, above) + jnp.where(first, below_other, below),
        jnp.where(last, above, above_other) + jnp.where(first, below, below_other),
    )


def powers(fields, count, start, diagonal, beyond, wide, history_split, center, own, sums, *refs):
    halo, coef_a, coef_b, split = refs
    columns = fields * (STEPS + 1)
    _, lane = iotas()
    inside = set(range(Z))
    ends = ends_of(count)

    def given(f, z, part):
        if z >= Z:
            return wide[f, z - Z, part]
        if part:
            return beyond[f, z]
        return start[f, z] if f < fields else diagonal[z]

    for z, part in known(fields, fields):
        if part == 0 and z in inside:
            coef_a[z, 0] = (diagonal[z] - 1.0) * (1.0 / 7.0)
        else:
            coef_a[z, part], coef_b[z, part] = coefficients(given(fields, z, part))

    def read(level, f, z, part):
        if level == 0:
            return given(f, z, part)
        if part == 0 and z in inside:
            return center[pl.ds((fields * level + f) * CELLS + z * Y, Y), :]
        return halo[level - 1, f, z, part]

    for f in range(fields):
        for z in range(Z):
            center[pl.ds(f * CELLS + z * Y, Y), :] = start[f, z]
    for level in range(1, STEPS + 1):
        reach = STEPS - level
        for f in range(fields):
            for at in range(-reach, Z + reach):
                z, before, after = at % SLOTS, (at - 1) % SLOTS, (at + 1) % SLOTS
                distance = max(-at, at - Z + 1, 0)
                tiles = [read(level - 1, f, z, p) for p in range(2)]
                along_y = beside_y(*tiles)
                for part in range(2 if distance < reach else 1):
                    tile = tiles[part]
                    total = jnp.where(lane == 0, 0.0, roll(tile, 1, 1))
                    total = total + jnp.where(lane == X - 1, 0.0, roll(tile, -1, 1))
                    total = total + along_y[part]
                    total = total + read(level - 1, f, before, part)
                    total = total + read(level - 1, f, after, part)
                    own_cells = part == 0 and z in inside
                    b = 1.0 / 7.0 if own_cells else coef_b[z, part]
                    value = coef_a[z, part] * tile - b * total
                    if level > 1:
                        value = value + value - read(level - 2, f, z, part)
                    if own_cells:
                        center[pl.ds((fields * level + f) * CELLS + z * Y, Y), :] = value
                    else:
                        halo[level - 1, f, z, part] = value
    center[pl.ds(columns * CELLS, (BROWS - columns) * CELLS), :] = jnp.zeros(
        ((BROWS - columns) * CELLS, X), F32
    )

    lanes = lax.broadcasted_iota(jnp.int32, (BROWS, X), 1)
    taken = [(lanes >= first) & (lanes < first + 4) for first in (choose(r, X - 4, 0) for r in ends)]
    for cell in range(CELLS):
        rows = center[pl.ds(cell, BROWS, stride=CELLS), :]
        for mask in taken:
            rows = jnp.where(mask, 0.0, rows)
        high, low = split_rows(rows, BPAD)
        split[0:BPAD, cell * X : (cell + 1) * X] = high
        split[BPAD : 2 * BPAD, cell * X : (cell + 1) * X] = low
    sums[...] = inner_products(split[...], history_split[...])

    for e, right in enumerate(ends):
        for f in range(fields + 1):
            tiles = [[jnp.zeros((Y, X), F32)] * 2 for _ in range(2)]
            for z, part in known(fields, f):
                base = 16 * (z % 8)
                first = choose(right, base, base + 4)
                moved = turn(given(f, z, part), right, base + 8, base + 4)
                tiles[part][z // 8] = jnp.where(
                    (lane >= first) & (lane < first + 8), moved, tiles[part][z // 8]
                )
            for part in range(2):
                for t in range(2):
                    own[e, f, part, t] = tiles[part][t]


def inner_products(split, history_split):
    basis = join_lanes(join(product(split, split), BPAD), BPAD)
    cross = join_lanes(join(product(split, history_split), BPAD), HPAD)
    both = jnp.concatenate([cross, basis, jnp.zeros((BPAD, X - HPAD - BPAD), F32)], axis=1)
    return both[:BROWS]


def powers_at_ends(fields, count, ways, own, history_ends, before, history_gram, *refs):
    received, (sums, patch, work, split) = refs[:ways], refs[ways:]
    columns = fields * (STEPS + 1)
    _, lane = iotas()
    column = lane & 15
    pick = facing("gx", count, received) if count > 2 else None
    ends = ends_of(count)
    taken = (column >= 4) & (column < 8)

    for e, right in enumerate(ends):

        def halo_of(k):
            return received[0][k] if count == 2 else pick(k)[e]

        first = choose(right, 8, 0)
        from_halo = (column >= first) & (column < first + 4)
        coefs = {}
        for f in range(fields + 1):
            for part in range(2):
                index, c = divmod(2 * f + part, 4)
                for t in range(2):
                    moved = turn(halo_of(2 * index + t), right, 8 - 4 * c, -4 * c)
                    tile = jnp.where(from_halo, moved, own[e, f, part, t])
                    if f < fields:
                        work[0, f, part, t] = tile
                    else:
                        coefs[part, t] = coefficients(tile)
        for level in range(1, STEPS + 1):
            for f in range(fields):
                tiles = [[work[level - 1, f, p, t] for t in range(2)] for p in range(2)]
                along_y = [beside_y(tiles[0][t], tiles[1][t]) for t in range(2)]
                for part, t in ((0, 0), (0, 1), (1, 0), (1, 1)):
                    if (level == STEPS and (part or t)) or (level == STEPS - 1 and part and t):
                        continue
                    tile = tiles[part][t]
                    nexts = [roll(tiles[part][i], -16, 1) for i in (t, 1 - t)]
                    lasts = [roll(tiles[part][i], 16, 1) for i in (t, 1 - t)]
                    total = roll(tile, 1, 1) + roll(tile, -1, 1) + along_y[t][part]
                    total = total + jnp.where(lane >= X - 16, nexts[1], nexts[0])
                    total = total + jnp.where(lane < 16, lasts[1], lasts[0])
                    a, b = coefs[part, t]
                    value = a * tile - b * total
                    if level > 1:
                        value = value + value - work[level - 2, f, part, t]
                    work[level, f, part, t] = value
        for level in range(STEPS + 1):
            for f in range(fields):
                k = fields * level + f
                patch[e, k * Y : (k + 1) * Y, :] = jnp.where(taken, work[level, f, 0, 0], 0.0)
        patch[e, columns * Y :, :] = jnp.zeros(((BROWS - columns) * Y, X), F32)
        for y in range(Y):
            high, low = split_rows(patch[e, pl.ds(y, BROWS, stride=Y), :], BPAD)
            at = (e * Y + y) * X
            split[0:BPAD, at : at + X] = high
            split[BPAD : 2 * BPAD, at : at + X] = low
    both = before[...] + inner_products(split[...], history_ends[...])
    first, second, third = (both[k : k + Y] for k in range(0, BROWS, Y))
    sums[0:8] = history_gram[0:8]
    sums[8:16] = jnp.where(lane < 96, history_gram[8:16], roll(first, 32, 1))
    sums[16:24] = jnp.where(lane < ROWS, first, roll(second, ROWS, 1))
    sums[24:32] = jnp.where(
        lane < ROWS, third, jnp.where(lane < 80, roll(second, -8, 1), roll(third, 16, 1))
    )


PACKED = ((0, 0), (0, 56), (1, 0), (1, 40), (0, 104), (1, 72), (1, 88))


def pack_gram(gram):
    _, lane = iotas()
    gram = jnp.concatenate([gram, jnp.zeros((HPAD, X - HPAD), F32)], axis=1)
    tiles = [jnp.zeros((Y, X), F32)] * 2
    for i, (t, first) in enumerate(PACKED):
        inside = (lane >= first) & (lane < first + ROWS - 8 * i)
        tiles[t] = jnp.where(inside, roll(gram[8 * i : 8 * i + 8], first - 8 * i, 1), tiles[t])
    return jnp.concatenate(tiles, axis=0)


def unpack_sums(total):
    _, lane = iotas()
    tiles = [total[8 * k : 8 * k + 8] for k in range(4)]
    rows = []
    for i, (t, first) in enumerate(PACKED):
        row = jnp.where((lane >= 8 * i) & (lane < ROWS), roll(tiles[t], 8 * i - first, 1), 0.0)
        rows.append(jnp.where(lane < 8 * i + 8, 0.5 * row, row))
    rows.append(jnp.zeros((Y, X), F32))
    upper = jnp.concatenate(rows, axis=0)[:, :HPAD]
    coef = [tiles[2], roll(tiles[2], -ROWS, 1), tiles[3]]
    coef = jnp.concatenate([jnp.where(lane < ROWS, c, 0.0) for c in coef], axis=0)[:, :HPAD]
    basis = [roll(tiles[1], -96, 1), roll(tiles[3], -ROWS, 1), roll(tiles[3], -80, 1)]
    basis = jnp.concatenate([jnp.where(lane < BROWS, b, 0.0) for b in basis], axis=0)[:, :BPAD]
    return upper, coef, basis


def patch_and_split(fields, count, center, patch, split, whole):
    _, lane = iotas()
    for k in range(BROWS):
        for z in range(Z):
            tile = center[pl.ds(k * CELLS + z * Y, Y), :]
            if fields <= k < fields * (STEPS + 1):
                for e, right in enumerate(ends_of(count)):
                    base = 16 * z + 4
                    moved = turn(patch[e, k * Y : (k + 1) * Y, :], right, X - 4 - base, -base)
                    first = choose(right, X - 4, 0)
                    tile = jnp.where((lane >= first) & (lane < first + 4), moved, tile)
            whole[pl.ds(k * CELLS + z * Y, Y), :] = tile
    for cell in range(CELLS):
        high, low = split_rows(whole[pl.ds(cell, BROWS, stride=CELLS), :], BPAD)
        split[0:BPAD, cell * X : (cell + 1) * X] = high
        split[BPAD : 2 * BPAD, cell * X : (cell + 1) * X] = low


def split_rows(rows, padded):
    rows = jnp.concatenate([rows, jnp.zeros((padded - rows.shape[0], rows.shape[1]), F32)], axis=0)
    high = rows.astype(BF16)
    return high, (rows - high.astype(F32)).astype(BF16)


def product(left, right):
    return lax.dot_general(left, right, (((1,), (1,)), ((), ())), preferred_element_type=F32)


def join(both, padded):
    return both[:padded] + both[padded:]


def join_lanes(both, padded):
    return both[:, :padded] + both[:, padded:]


def load_history(history, here, done):
    copy = pltpu.make_async_copy(history, here, done)
    copy.start()
    copy.wait()


def pack_history(count, ends_count, history, split, packed):
    _, lane = iotas()
    for e, right in enumerate(ends_of(ends_count)):
        for h in range(count):
            tile = jnp.zeros((Y, X), F32)
            for z in range(Z):
                base = 16 * z + 4
                moved = turn(history[pl.ds(h * CELLS + z * Y, Y), :], right, base + 4, base)
                tile = jnp.where((lane >= base) & (lane < base + 4), moved, tile)
            packed[pl.ds(h * Y, Y), :] = tile
        for y in range(Y):
            high, low = split_rows(packed[pl.ds(y, count, stride=Y), :], HPAD)
            at = (e * Y + y) * X
            split[0:HPAD, at : at + X] = high
            split[HPAD : 2 * HPAD, at : at + X] = low


def history_kernel(count, history, split, gram):
    for cell in range(CELLS):
        high, low = split_rows(history[pl.ds(cell, count, stride=CELLS), :], HPAD)
        split[0:HPAD, cell * X : (cell + 1) * X] = high
        split[HPAD : 2 * HPAD, cell * X : (cell + 1) * X] = low
    gram[...] = pack_gram(join_lanes(join(product(split[...], split[...]), HPAD), HPAD))


def split_matrix(matrix):
    high = matrix.astype(BF16)
    return high, (matrix - high.astype(F32)).astype(BF16)


def reciprocal(value):
    guess = pl.reciprocal(value, approx=True)
    guess = guess * (2.0 - value * guess)
    return guess * (2.0 - value * guess)


def finish(columns, cells, history_split, split, *refs):
    parts, (out, factor, staged, factor_staged, done, projected) = refs[:-6], refs[-6:]
    total = (parts[0][...] + parts[1][...]) * (1.0 / cells)
    upper, coef, basis_gram = unpack_sums(total)
    inner = jnp.dot(coef, upper, precision=HIGHEST, preferred_element_type=F32)
    inner = inner + lax.dot_general(
        coef, upper, (((1,), (1,)), ((), ())), precision=HIGHEST, preferred_element_type=F32
    )
    inner = inner - 2.0 * coef
    inner = jnp.concatenate([inner, jnp.zeros((BPAD - BROWS, HPAD), F32)], axis=0)
    gram = basis_gram + lax.dot_general(
        coef, inner, (((1,), (1,)), ((), ())), precision=HIGHEST, preferred_element_type=F32
    )
    coef_high, coef_low = split_matrix(-jnp.concatenate([coef, jnp.zeros((BPAD - BROWS, HPAD), F32)], axis=0))
    one = jnp.where(
        lax.broadcasted_iota(jnp.int32, (BPAD, BPAD), 0) == lax.broadcasted_iota(jnp.int32, (BPAD, BPAD), 1), 1.0, 0.0
    ).astype(BF16)
    basis_minus = jnp.concatenate(
        [
            jnp.concatenate([coef_high, coef_high, one, one], axis=1),
            jnp.concatenate([coef_low, jnp.zeros((BPAD, HPAD + 2 * BPAD), BF16)], axis=1),
        ],
        axis=0,
    )
    width = WIDTH * X
    for c in range(CELLS * X // width):
        at = slice(c * width, (c + 1) * width)
        right = jnp.concatenate([history_split[:, at], split[:, at]], axis=0)
        high, low = split_matrix(join(jnp.dot(basis_minus, right, preferred_element_type=F32), BPAD))
        projected[0:BPAD, at] = high
        projected[BPAD:, at] = low
    row = lax.broadcasted_iota(jnp.int32, (BROWS, X), 0)
    lane = lax.broadcasted_iota(jnp.int32, (BROWS, X), 1)
    work = jnp.concatenate([gram, jnp.zeros((BROWS, X - BPAD), F32)], axis=1)
    work = jnp.where(lane == row + BPAD, 1.0, work)
    panel = columns
    for start in range(0, columns, panel):
        spread = [
            jnp.broadcast_to(work[:, k : k + 1], (BROWS, X)) for k in range(start, start + panel)
        ]
        for j in range(panel):
            k = start + j
            scale = spread[j] * reciprocal(spread[j][k : k + 1, :])
            scale = jnp.where(row > k, scale, 0.0)
            for later in range(j + 1, panel):
                spread[later] = spread[later] - scale * spread[later][k : k + 1, :]
            work = work - scale * work[k : k + 1, :]
    pivots = jnp.sum(jnp.where(lane == row, work, 0.0), axis=1, keepdims=True)
    good = lax.broadcasted_iota(jnp.int32, (BROWS, 1), 0) < columns
    work = work * jnp.where(good, 1.0 / jnp.sqrt(jnp.where(good, pivots, 1.0)), 0.0)
    factor_staged[...] = jnp.where(lane >= row, work, 0.0)[0:columns, 0:columns]
    copies = [pltpu.make_async_copy(factor_staged, factor, done.at[0])]
    copies[0].start()
    work = jnp.concatenate([work, jnp.zeros((BPAD - BROWS, X), F32)], axis=0)
    basis_high, basis_low = split_matrix(work[:, BPAD : 2 * BPAD])
    left = jnp.concatenate([basis_high, basis_high, basis_low], axis=1)
    width = WIDTH * X
    inside = width // X
    blocks = staged.reshape(BROWS, CELLS, X)
    for c in range(CELLS // inside):
        right = projected[:, c * width : (c + 1) * width]
        right = jnp.concatenate([right, right[:BPAD]], axis=0)
        result = jnp.dot(left, right, preferred_element_type=F32)
        for j in range(inside):
            staged[pl.ds(c * inside + j, columns, stride=CELLS), :] = result[
                0:columns, j * X : (j + 1) * X
            ]
        cells_done = (c + 1) * inside
        if cells_done % PIECE == 0:
            piece = pl.ds(cells_done - PIECE, PIECE)
            copies.append(
                pltpu.make_async_copy(
                    blocks.at[pl.ds(0, columns), piece, :], out.at[:, piece, :], done.at[len(copies)]
                )
            )
            copies[-1].start()
    for copy in copies:
        copy.wait()


def call(
    kernel,
    outs,
    flops,
    bytes_accessed,
    scratch=(),
    limit=40 * 1024 * 1024,
    place=jax.ShapeDtypeStruct,
    **specs,
):
    return pl.pallas_call(
        kernel,
        **specs,
        out_shape=[place(shape, dtype) for shape, dtype in outs],
        scratch_shapes=list(scratch),
        compiler_params=pltpu.CompilerParams(vmem_limit_bytes=limit),
        cost_estimate=pl.CostEstimate(flops=flops, bytes_accessed=bytes_accessed, transcendentals=0),
    )


def sum_over_devices(array, sizes):
    devices = range(sizes[0] * sizes[1] * sizes[2])
    bits = []
    for axis, stride in ((2, 1), (0, sizes[1] * sizes[2]), (1, sizes[2])):
        bits += [stride << b for b in range(sizes[axis].bit_length() - 1)]
    others = None
    for bit in bits:
        array = array if others is None else array + others
        others = lax.ppermute(array, AXES, [(i, i ^ (bit | 1)) for i in devices])
    return [array, others]


def on_device(sizes, history, start, diagonal):
    fields, history_count = start.shape[0], history.shape[0]
    columns = fields * (STEPS + 1)
    all_fields = fields + 1
    count = dict(zip(AXES, sizes))
    ways = {axis: 1 if size == 2 else 2 for axis, size in count.items()}
    cells = Z * Y * X * sizes[0] * sizes[1] * sizes[2]
    tile = Y * X * 4

    ends = 1 if count["gx"] == 2 else 2
    there = pl.BlockSpec(memory_space=pltpu.HBM)
    anywhere = pl.BlockSpec(memory_space=pl.ANY)
    here = pl.BlockSpec(memory_space=pltpu.VMEM)

    with jax.named_scope("halo_y"):
        start, diagonal, *sends = call(
            functools.partial(pack_y, fields),
            [(start.shape, F32), (diagonal.shape, F32)]
            + [((4 * all_fields - 1, Y, X), F32)] * ways["gy"],
            1000,
            start.size * 4,
            [pltpu.SemaphoreType.DMA((all_fields,))],
            None,
            pltpu.VMEM,
            in_specs=[there, there],
        )(start, diagonal)
        received = swaps(sends, sizes, "gy")
    with jax.named_scope("load_history"):
        rows = call(
            load_history,
            [(history.shape, F32)],
            1000,
            history.size * 4,
            [pltpu.SemaphoreType.DMA],
            None,
            pltpu.VMEM,
            in_specs=[there],
        )(history)[0].reshape(history_count * CELLS, X)
    with jax.named_scope("history_at_ends"):
        history_ends = call(
            functools.partial(pack_history, history_count, count["gx"]),
            [((2 * HPAD, ends * Y * X), BF16)],
            1000,
            history.size * 2,
            [pltpu.VMEM((history_count * Y, X), F32)],
        )(rows)[0]
    with jax.named_scope("halo_z"):
        beyond, *sends = call(
            functools.partial(pack_z, fields, count["gy"], ways["gy"]),
            [((all_fields, Z, Y, X), F32)] + [((z_tiles(fields), Y, X), F32)] * ways["gz"],
            1000,
            start.size * 4,
            in_specs=[here, here, anywhere] + [here] * ways["gy"],
        )(start, diagonal, history_ends, *received)
        received = swaps(sends, sizes, "gz")
    with jax.named_scope("history_products"):
        history_split, history_gram = call(
            functools.partial(history_kernel, history_count),
            [((2 * HPAD, CELLS * X), BF16), ((2 * Y, X), F32)],
            2 * 128 * 128 * CELLS * X,
            history.size * 4,
        )(rows)
    with jax.named_scope("halo_x"):
        x_shapes = [((x_tiles(fields), Y, X), F32)] * ways["gx"]
        owns = call(functools.partial(pack_x_own, fields), x_shapes, 1000, start.size * 4)(
            start, diagonal, beyond
        )
        wide, *sends = call(
            functools.partial(pack_x, fields, count["gz"], ways["gz"], ways["gx"]),
            [((all_fields, SLOTS - Z, 2, Y, X), F32)] + x_shapes,
            1000,
            start.size * 4,
            in_specs=[here] * ways["gx"] + [anywhere] + [here] * ways["gz"],
        )(*owns, history_gram, *received)
        received = swaps(sends, sizes, "gx")
    with jax.named_scope("matrix_powers"):
        center, own, sums = call(
            functools.partial(powers, fields, count["gx"]),
            [
                ((BROWS * CELLS, X), F32),
                ((ends, all_fields, 2, 2, Y, X), F32),
                ((BROWS, X), F32),
            ],
            2 * 192 * 64 * CELLS * X,
            start.size * 4,
            [
                pltpu.VMEM((STEPS - 1, fields, SLOTS, 2, Y, X), F32),
                pltpu.VMEM((SLOTS, 2, Y, X), F32),
                pltpu.VMEM((SLOTS, 2, Y, X), F32),
                pltpu.VMEM((2 * BPAD, CELLS * X), BF16),
            ],
        )(start, diagonal, beyond, wide, history_split)
    with jax.named_scope("powers_at_ends"):
        sums, patch = call(
            functools.partial(powers_at_ends, fields, count["gx"], ways["gx"]),
            [((4 * Y, X), F32), ((ends, BROWS * Y, X), F32)],
            1000000,
            start.size * 4,
            [
                pltpu.VMEM((STEPS + 1, fields, 2, 2, Y, X), F32),
                pltpu.VMEM((2 * BPAD, ends * Y * X), BF16),
            ],
        )(own, history_ends, sums, history_gram, *received)
    with jax.named_scope("whole_basis"):
        split = call(
            functools.partial(patch_and_split, fields, count["gx"]),
            [((2 * BPAD, CELLS * X), BF16)],
            1000,
            columns * CELLS * X * 4,
            [pltpu.VMEM((BROWS * CELLS, X), F32)],
        )(center, patch)[0]
    with jax.named_scope("sum_over_devices"):
        parts = sum_over_devices(sums, sizes)
    with jax.named_scope("orthonormalize"):
        out, factor = call(
            functools.partial(finish, columns, cells),
            [((columns, CELLS, X), F32), ((columns, columns), F32)],
            2 * 192 * 64 * CELLS * X,
            columns * CELLS * X * 4,
            [
                pltpu.VMEM((BROWS * CELLS, X), F32),
                pltpu.VMEM((columns, columns), F32),
                pltpu.SemaphoreType.DMA((CELLS // PIECE + 1,)),
                pltpu.VMEM((2 * BPAD, CELLS * X), BF16),
            ],
            out_specs=[pl.BlockSpec(memory_space=pltpu.HBM)] * 2,
        )(history_split, split, *parts)
    return out.reshape(columns, Z, Y, X), factor


def solution(mesh):
    sizes = tuple(mesh.shape[axis] for axis in AXES)
    return jax.shard_map(
        functools.partial(on_device, sizes),
        mesh=mesh,
        in_specs=(P(None, "gz", "gy", "gx"), P(None, "gz", "gy", "gx"), P("gz", "gy", "gx")),
        out_specs=(P(None, "gz", "gy", "gx"), P()),
        check_vma=False,
    )
```
